32 devices in a mesh: dp: 2 (over x), label: 16 (over z, y, core).
Axes of the slice: x: 2, y: 2, z: 4, core: 2. Of those that a mesh axis runs over, the one named last changes fastest.
Arguments:
- embed: bfloat16 [2048, 768], P('dp'), may hold values from -6 to 6
- weight: bfloat16 [16384, 768], P('label'), may hold values from -0.21875 to 0.21875
- bias: bfloat16 [16384], P('label'), may hold values from -4 to 4
- beam: int32 [16, 38], P('dp'), may hold values from 0 to 127, as said below
- positives: int32 [2048, 8], P('dp'), may hold values from 0 to 16383, as said below
Outputs:
- row_grads: bfloat16 [2048, 768], P(('dp', 'label'))
- label_grads: bfloat16 [16384, 768], P(('label', 'dp'))
The draws below stay inside these ranges and needn't reach their ends.
Inputs may be any that keep to these rules, and one draw needn't show every extreme that they name: `beam`: the label device of cluster c is c // 8. A block's 38 clusters are distinct. For the 8 blocks of one data shard, one label device holds exactly 8 of every block's clusters, and every other label device holds exactly 2 clusters of every block. `positives`: each is a label of one of the beam clusters of the instance's own block; repeats may occur.
All inputs are finite; a program needn't handle non-finite values.
Results may differ from the reference program's by a relative error of at most 0.015.
Values may be sent and summed in bfloat16 or wider, within the bound.
No kernel may reach another device: no remote copies, remote signals or barrier semaphores. Data moves between devices by JAX's collectives and lax.ppermute only.
A program may use at most 64 MiB of HBM per device.

```python
import jax
import jax.numpy as jnp
from jax import lax

D = 768
INST_BLOCK = 128
CLUSTER = 128
HOT = 8
SIB = 2
BEAM = 38
POS = 8
BLK_DEV = 8
CL_DEV = 8
NBLK = 16
NINST = 2048
CLUSTERS = 128
LABELS = 16384
N_DP = 2
N_LABEL = 16


def beam_table(key):
    busy_key, hot_key, sib_key, shuffle_key = jax.random.split(key, 4)
    busy_dev = jax.random.randint(busy_key, (N_DP,), 0, N_LABEL)
    busy_of = jnp.repeat(busy_dev, BLK_DEV)
    hot_pick = jax.vmap(lambda sub_key: jax.random.permutation(sub_key, CL_DEV))(jax.random.split(hot_key, NBLK))[:, :HOT]
    hot_ids = busy_of[:, None] * CL_DEV + hot_pick
    others = (busy_of[:, None] + jnp.arange(1, N_LABEL, dtype=jnp.int32)[None, :]) % N_LABEL
    sib_pick = jax.vmap(lambda sub_key: jax.random.permutation(sub_key, CL_DEV))(jax.random.split(sib_key, NBLK * (N_LABEL - 1)))[:, :SIB]
    sib_pick = sib_pick.reshape(NBLK, N_LABEL - 1, SIB)
    other_ids = (others[:, :, None] * CL_DEV + sib_pick).reshape(NBLK, (N_LABEL - 1) * SIB)
    beam_ids = jnp.concatenate([hot_ids, other_ids], axis=1).astype(jnp.int32)
    shuffle = jax.vmap(lambda sub_key: jax.random.permutation(sub_key, BEAM))(jax.random.split(shuffle_key, NBLK))
    return jnp.take_along_axis(beam_ids, shuffle, axis=1)


def draw_beam(key, part):
    return beam_table(key)


def draw_positives(key, part):
    beam_ids = beam_table(key)
    key = jax.random.fold_in(key, 5)
    slot_key, label_key = jax.random.split(key)
    slot_no = jax.random.randint(slot_key, (NINST, POS), 0, BEAM)
    within = jax.random.randint(label_key, (NINST, POS), 0, CLUSTER)
    block_of = jnp.arange(NINST, dtype=jnp.int32) // INST_BLOCK
    chosen = beam_ids[block_of[:, None], slot_no]
    return (chosen * CLUSTER + within).astype(jnp.int32)


def level_of(own_key, extent, shards, low, largest):
    loudness = 1.0
    for dim, shards_of in shards:
        draws = jax.random.uniform(jax.random.fold_in(jax.random.fold_in(own_key, 6), dim), (shards_of,), jnp.float32, low / len(shards), largest / len(shards))
        loudness = loudness * jnp.repeat(jnp.exp(draws), extent[dim] // shards_of).reshape((-1,) + (1,) * (len(extent) - 1 - dim))
    return loudness


def gaussian(rng, dims, width, most, cuts=(), held_as=jnp.bfloat16):
    values = width * jax.random.normal(rng, dims, jnp.float32)
    if cuts:
        values = values * level_of(rng, dims, cuts, -0.22, 0.18)
    return jnp.clip(values, -most, most).astype(held_as)


def setup_inputs(seed: int = 0) -> dict:
    key_of = jax.random.split(jax.random.key(seed), 6)
    return {
        "embed": gaussian(key_of[0], (NINST, D), 1.0, 6.0, ((0, 2),)),
        "weight": gaussian(key_of[1], (LABELS, D), D ** -0.5, 0.21875, ((0, 16),)),
        "bias": gaussian(key_of[2], (LABELS,), 1.0, 4.0, ((0, 16),)),
        "beam": draw_beam(jax.random.fold_in(key_of[5], 71), 0),
        "positives": draw_positives(jax.random.fold_in(key_of[5], 71), 0),
    }


grad_scale = 0.125


def block_terms(block_rows, positive_rows, beam_row, slabs, biases):
    chosen = slabs[beam_row]
    flattened = chosen.reshape(BEAM * CLUSTER, D)
    bias_row = biases[beam_row].reshape(BEAM * CLUSTER).astype(jnp.float32)
    scores = jnp.dot(block_rows, flattened.T, preferred_element_type=jnp.float32) + bias_row[None, :]
    labels = (beam_row[:, None] * CLUSTER + jnp.arange(CLUSTER, dtype=jnp.int32)[None, :]).reshape(BEAM * CLUSTER)
    target = jnp.any(positive_rows[:, :, None] == labels[None, None, :], axis=1).astype(jnp.float32)
    slopes = ((jax.nn.sigmoid(scores) - target) * grad_scale).astype(jnp.bfloat16)
    row_term = jnp.dot(slopes, flattened, preferred_element_type=jnp.float32)
    label_term = jnp.dot(slopes.T, block_rows, preferred_element_type=jnp.float32).reshape(BEAM, CLUSTER, D)
    return row_term, label_term


def reference(embed, weight, bias, beam, positives):
    slabs = weight.reshape(CLUSTERS, CLUSTER, D)
    biases = bias.reshape(CLUSTERS, CLUSTER)
    blocks = embed.reshape(NBLK, INST_BLOCK, D)
    wanted = positives.reshape(NBLK, INST_BLOCK, POS)
    row_parts = []
    label_total = jnp.zeros((CLUSTERS, CLUSTER, D), jnp.float32)
    for shard_no in range(N_DP):
        first_block = shard_no * BLK_DEV

        def visit_block(label_acc, local_block):
            block_id = first_block + local_block
            beam_row = beam[block_id]
            row_term, label_term = block_terms(blocks[block_id], wanted[block_id], beam_row, slabs, biases)
            label_acc = label_acc.at[beam_row].add(label_term)
            return label_acc, row_term

        label_acc, row_acc = lax.scan(visit_block, jnp.zeros((CLUSTERS, CLUSTER, D), jnp.float32), jnp.arange(BLK_DEV, dtype=jnp.int32))
        row_parts.append(row_acc)
        rounded = lax.optimization_barrier(label_acc.astype(jnp.bfloat16))
        label_total = label_total + rounded.astype(jnp.float32)
    row_grads = jnp.concatenate(row_parts, axis=0).reshape(NINST, D).astype(jnp.bfloat16)
    label_grads = label_total.reshape(LABELS, D).astype(jnp.bfloat16)
    return row_grads, label_grads
```

```python
import functools

import jax
import jax.numpy as jnp
from jax import lax
from jax.experimental import pallas as pl
from jax.experimental.pallas import tpu as pltpu
from jax.sharding import PartitionSpec as P

INST_BLOCK = 128
CLUSTER = 128
TILE = 256
CHUNK = 256
BLOCKS = 8
SCALE = 0.125
ORDER = ((1, 3, 6, 7), (0, 2, 4, 5))

F32 = jnp.float32
BF16 = jnp.bfloat16
VMEM_LIMIT = 32 * 1024 * 1024


def half_index():
    return lax.axis_index("dp") // (lax.axis_size("dp") // 2)


def place(n_label):
    subs = n_label // 2 // BLOCKS
    pair = lax.axis_index("label") // 2
    return pair // subs, pair % subs, lax.axis_index("label") % 2


def slope_chunks(jobs, scores, w, embed, bias_ref, mask_ref, pos_ref, before, emit):
    half_rows = w.shape[0] // 2
    label_no = lax.broadcasted_iota(jnp.int32, (CLUSTER, TILE), 0).astype(jnp.int16)
    words = {}

    def score(n):
        k, t, h = jobs[n]
        before(k, t, h)
        first = k * half_rows + h * CHUNK
        scores[n % 2] = lax.dot_general(
            w[first : first + CHUNK],
            embed[t * TILE : (t + 1) * TILE],
            (((1,), (1,)), ((), ())),
            preferred_element_type=F32,
        )

    score(0)
    for n, (k, t, h) in enumerate(jobs):
        if n + 1 < len(jobs):
            score(n + 1)
        if (k, t) not in words:
            half = 1 - half_index() if k == 0 else half_index()
            first_label = (lax.axis_index("label") * 2 + half) * half_rows
            local = pos_ref[:, t * TILE : (t + 1) * TILE] - first_label
            inside = (local >= 0) & (local < half_rows)
            bits = jnp.where(inside, jnp.left_shift(1, (local >> 7) & 15), 0).astype(jnp.int16)
            within = (local & (CLUSTER - 1)).astype(jnp.int16)
            word = jnp.zeros((CLUSTER, TILE), jnp.int16)
            for p in range(pos_ref.shape[0]):
                word = word | jnp.where(
                    label_no == jnp.broadcast_to(within[p : p + 1], word.shape),
                    jnp.broadcast_to(bits[p : p + 1], word.shape),
                    jnp.int16(0),
                )
            words[k, t] = word
        for i in range(CHUNK // CLUSTER):
            c = h * (CHUNK // CLUSTER) + i
            hit = (words[k, t] & jnp.int16(1 << c)) != 0
            sign = jnp.where(hit, jnp.bfloat16(-1), jnp.bfloat16(1)).astype(F32)
            groups = []
            for g in range(TILE // INST_BLOCK):
                lanes = slice(g * INST_BLOCK, (g + 1) * INST_BLOCK)
                z = (scores[n % 2, i * CLUSTER : (i + 1) * CLUSTER, lanes] + bias_ref[k, c]) * 0.5
                pair = t // 2 * 2 + g
                groups.append((jnp.tanh(z) + sign[:, lanes]).astype(BF16) * mask_ref[k, c, pair : pair + 1])
            emit(k, t, c, jnp.concatenate(groups, axis=1))


def send_kernel(n_label, embed_hbm, weight_hbm, bias_hbm, beam_hbm, pos_hbm, embed, w, pos, mask, bias_full, slopes_t,
                label_out, own_slopes_t, row_out, bias_raw, beam_raw, pos_raw, beam, scores, slopes, sems):
    half_rows = label_out.shape[0]
    clusters = half_rows // CLUSTER
    tiles = embed.shape[0] // TILE
    half = 1 - half_index()
    over, within, core = place(n_label)
    piece = embed.shape[0] // n_label
    subs = INST_BLOCK // piece // 2
    small = [
        pltpu.make_async_copy(source, target, sems.at[k])
        for k, (source, target) in enumerate(((beam_hbm, beam_raw), (bias_hbm, bias_raw), (pos_hbm, pos_raw)))
    ]
    w_copies = [
        pltpu.make_async_copy(
            weight_hbm.at[pl.ds(pl.multiple_of(which * half_rows, half_rows), half_rows)],
            w.at[pl.ds(k * half_rows, half_rows)],
            sems.at[3 + k],
        )
        for k, which in enumerate((half, 1 - half))
    ]
    e_copies = []
    for t in range(tiles):
        e_copies.append([])
        for r in ORDER[t // 2]:
            for j in range(subs):
                i = t * (TILE // piece) + len(e_copies[t])
                row = (r ^ over) * INST_BLOCK + (2 * (j ^ within if subs > 1 else 0) + (core if t % 2 else 1 - core)) * piece
                e_copies[t].append(
                    pltpu.make_async_copy(
                        embed_hbm.at[pl.ds(pl.multiple_of(row, piece), piece)],
                        embed.at[pl.ds(i * piece, piece)],
                        sems.at[5 + i],
                    )
                )
    for copy in (*small, w_copies[0], *e_copies[0]):
        copy.start()
    for copy in small:
        copy.wait()
    for copy in (*e_copies[1], *e_copies[2], *e_copies[3]):
        copy.start()

    lane = lax.broadcasted_iota(jnp.int32, (BLOCKS, INST_BLOCK), 1)
    low = lane < INST_BLOCK // 2

    def relative_lanes(x):
        code = 2 * within + core
        for k in range((2 * subs).bit_length() - 1):
            shift = piece << k
            turned = jnp.where(
                (lane & shift) != 0, pltpu.roll(x, shift, 1), pltpu.roll(x, INST_BLOCK - shift, 1)
            )
            x = jnp.where((code >> k) % 2 == 1, turned, x)
        if subs > 1:
            x = jnp.concatenate(
                [x[:, (2 * j + c) * piece : (2 * j + c + 1) * piece] for c in range(2) for j in range(subs)], axis=1
            )
        return x

    for n in range(2):
        for g in range(2):
            i = 2 * n + g
            one, two = (
                relative_lanes(pos_raw[:, pl.ds(pl.multiple_of((r ^ over) * INST_BLOCK, INST_BLOCK), INST_BLOCK)])
                for r in ORDER[n][2 * g : 2 * g + 2]
            )
            other = jnp.where(low, pltpu.roll(one, INST_BLOCK // 2, 1), two)
            this = jnp.where(low, one, pltpu.roll(two, INST_BLOCK // 2, 1))
            first = 4 * n * INST_BLOCK + g * INST_BLOCK
            pos[:, first : first + INST_BLOCK] = other
            pos[:, first + TILE : first + TILE + INST_BLOCK] = this
            for h in range(2):
                beam[4 * h + i : 4 * h + i + 1] = beam_raw[pl.ds(ORDER[n][2 * g + h] ^ over, 1)]

    def set_up(k, which):
        first_cluster = (lax.axis_index("label") * 2 + which) * clusters
        biases = bias_raw[...].astype(F32)
        for c in range(clusters):
            chosen = jnp.where(which == 0, biases[c : c + 1], biases[clusters + c : clusters + c + 1])
            bias_full[k, c] = jnp.broadcast_to(chosen, (CLUSTER, CLUSTER)).T
            held = jnp.where(beam[...] == first_cluster + c, 0.5 * SCALE, 0.0)
            held = jnp.broadcast_to(jnp.max(held, axis=1, keepdims=True), (BLOCKS, INST_BLOCK))
            mask[k, c] = jnp.where(low[:4], held[:4], held[4:]).astype(BF16)

    set_up(0, half)
    w_copies[0].wait()

    def before(k, t, h):
        if k == 0 and h == 0:
            for copy in e_copies[t]:
                copy.wait()
            if t == 1:
                w_copies[1].start()
        elif k == 1 and h == 0:
            w_copies[1].wait()

    def emit(k, t, c, part):
        if k == 0:
            slopes_t[c * CLUSTER : (c + 1) * CLUSTER, t * TILE : (t + 1) * TILE] = part
            if t == 0:
                slopes[:, c * CLUSTER : (c + 1) * CLUSTER] = part.T
            if (t, c) == (tiles - 1, 0):
                set_up(1, 1 - half)
        else:
            own_slopes_t[c * CLUSTER : (c + 1) * CLUSTER] = part
            slopes[:, half_rows + c * CLUSTER : half_rows + (c + 1) * CLUSTER] = part.T
        if (k, t) == (0, tiles - 1) and (c + 1) % (CHUNK // CLUSTER) == 0:
            rows = slice((c + 1) * CLUSTER - CHUNK, (c + 1) * CLUSTER)
            label_out[rows] = jnp.dot(slopes_t[rows], embed[...], preferred_element_type=F32).astype(BF16)

    chunks = range(half_rows // CHUNK)
    jobs = [(0, t, h) for t in range(tiles) for h in chunks] + [(1, 0, h) for h in chunks]
    slope_chunks(jobs, scores, w, embed, bias_full, mask, pos, before, emit)
    store_rows([row_out], slopes, w)


def store_rows(outs, slopes, w):
    sums = jnp.dot(slopes[...], w[...], preferred_element_type=F32).astype(BF16)
    count = TILE // len(outs)
    for i, out in enumerate(outs):
        out[...] = sums[i * count : (i + 1) * count].reshape(out.shape)


def row_tile(t, outs, embed, w, pos, mask, bias_full, first_slopes_t, own_slopes_t, scores, slopes):
    half_rows = w.shape[0] // 2

    def emit(k, t, c, part):
        if c == 0:
            slopes[:, :half_rows] = first_slopes_t[:, t * TILE : (t + 1) * TILE].T
        own_slopes_t[c * CLUSTER : (c + 1) * CLUSTER] = part
        slopes[:, half_rows + c * CLUSTER : half_rows + (c + 1) * CLUSTER] = part.T

    jobs = [(1, t, h) for h in range(half_rows // CHUNK)]
    slope_chunks(jobs, scores, w, embed, bias_full, mask, pos, lambda *job: None, emit)
    store_rows(outs, slopes, w)


def keep_rows_kernel(embed, w, pos, mask, bias_full, first_slopes_t, own_slopes_t, row_out, scores, slopes):
    row_tile(1, [row_out], embed, w, pos, mask, bias_full, first_slopes_t, own_slopes_t, scores, slopes)


def last_rows_kernel(embed, w, pos, mask, bias_full, first_slopes_t, one_slopes_t, two_slopes_t, *rest):
    *sends, row_out, label_out, three_slopes_t, four_slopes_t, scores, slopes = rest
    shared = (embed, w, pos, mask, bias_full, first_slopes_t)
    row_tile(2, sends, *shared, three_slopes_t, scores.at[0], slopes.at[0])
    row_tile(3, [row_out], *shared, four_slopes_t, scores.at[1], slopes.at[1])
    total = 0.0
    for t, part in enumerate((one_slopes_t, two_slopes_t, three_slopes_t, four_slopes_t)):
        total = total + jnp.dot(part[...], embed[t * TILE : (t + 1) * TILE], preferred_element_type=F32)
    label_out[...] = total.astype(BF16)


def swapped(value, axis, size, bit):
    return lax.ppermute(value, axis, [(i, i ^ bit) for i in range(size)])


def add(*terms):
    total = terms[0].astype(F32)
    for term in terms[1:]:
        total = total + term.astype(F32)
    return total.astype(BF16)


def on_device(n_dp, n_label, embed, weight, bias, beam, positives):
    rows, features = embed.shape
    labels = weight.shape[0]
    half_rows = labels // 2
    clusters = half_rows // CLUSTER
    piece = rows // n_label
    subs = n_label // 2 // BLOCKS
    pos_count = positives.shape[1]
    bias_rows = bias.reshape(labels // CLUSTER, CLUSTER)
    pos_rows = positives.T
    vmem = pl.BlockSpec(memory_space=pltpu.VMEM)
    hbm = pl.BlockSpec(memory_space=pltpu.HBM)
    params = pltpu.CompilerParams(vmem_limit_bytes=VMEM_LIMIT)
    shape = jax.ShapeDtypeStruct
    tile_shape = shape((half_rows, TILE), BF16)
    row_shape = shape((BLOCKS // 2, subs, piece, features), BF16)
    score_scratch = pltpu.VMEM((2, CHUNK, TILE), F32)
    slope_scratch = pltpu.VMEM((TILE, labels), BF16)

    def cost(halves):
        return pl.CostEstimate(flops=halves * 2 * rows * half_rows * features, bytes_accessed=0, transcendentals=0)

    *shared, label_send, one_slopes_t, first_send = pl.pallas_call(
        functools.partial(send_kernel, n_label),
        out_shape=[
            shape((rows, features), BF16),
            shape((labels, features), BF16),
            shape((pos_count, rows), jnp.int32),
            shape((2, clusters, 4, INST_BLOCK), BF16),
            shape((2, clusters, CLUSTER, INST_BLOCK), F32),
            shape((half_rows, rows), BF16),
            shape((half_rows, features), BF16),
            tile_shape,
            row_shape,
        ],
        in_specs=[hbm] * 5,
        out_specs=[vmem] * 9,
        scratch_shapes=[
            pltpu.VMEM(bias_rows.shape, BF16),
            pltpu.VMEM(beam.shape, jnp.int32),
            pltpu.VMEM(pos_rows.shape, jnp.int32),
            pltpu.VMEM(beam.shape, jnp.int32),
            score_scratch,
            slope_scratch,
            pltpu.SemaphoreType.DMA((5 + n_label,)),
        ],
        compiler_params=params,
        cost_estimate=cost(3),
        name="send_half",
    )(*(pltpu.with_memory_space_constraint(x, pltpu.HBM) for x in (embed, weight, bias_rows, beam, pos_rows)))

    first_got = swapped(first_send, "label", n_label, 1)
    label_got = swapped(label_send, "dp", n_dp, n_dp // 2)
    first_got, *shared = lax.optimization_barrier((first_got, *shared))

    two_slopes_t, first_keep = pl.pallas_call(
        keep_rows_kernel,
        out_shape=[tile_shape, row_shape],
        in_specs=[vmem] * 6,
        out_specs=[vmem] * 2,
        scratch_shapes=[score_scratch, slope_scratch],
        compiler_params=params,
        cost_estimate=cost(0),
        name="keep_rows",
    )(*shared)

    axes = [2 * subs, 4 * subs, 8 * subs]
    one_got = swapped(add(first_keep[:2], first_got[:2]), "label", n_label, axes[0])
    two_got = swapped(add(first_keep[2:], first_got[2:]), "label", n_label, axes[1])

    part_shape = shape((subs, piece, features), BF16)
    *last_send, last_keep, label_keep = pl.pallas_call(
        last_rows_kernel,
        out_shape=[part_shape] * 4 + [row_shape, shape((half_rows, features), BF16)],
        in_specs=[vmem] * 8,
        out_specs=[vmem] * 6,
        scratch_shapes=[
            pltpu.VMEM((half_rows, TILE), BF16),
            pltpu.VMEM((half_rows, TILE), BF16),
            pltpu.VMEM((2, 2, CHUNK, TILE), F32),
            pltpu.VMEM((2, TILE, labels), BF16),
        ],
        compiler_params=params,
        cost_estimate=cost(0),
        name="last_rows",
    )(*shared, one_slopes_t, two_slopes_t)

    last_got = [swapped(part, "label", n_label, 1) for part in last_send]

    two_next = add(last_keep[1], last_got[1], one_got[1])
    five_next = add(last_keep[3], last_got[3], two_got[1])
    two_next_got = swapped(two_next, "label", n_label, axes[1])
    five_next_got = swapped(five_next, "label", n_label, axes[0])
    four = add(last_keep[2], last_got[2], two_got[0], five_next_got)
    four_got = swapped(four, "label", n_label, axes[2])
    row_sum = add(last_keep[0], last_got[0], one_got[0], two_next_got)
    row_got = four_got
    bit = subs
    while bit > 1:
        held = row_sum.shape[0] // 2
        outgoing = add(row_sum[held:], row_got[held:])
        incoming = swapped(outgoing, "label", n_label, bit)
        row_sum = add(row_sum[:held], row_got[:held])
        row_got = incoming
        bit //= 2
    row_out = add(row_sum[0], row_got[0])

    label_sum = add(label_keep, label_got)
    step = n_dp // 4
    at = lax.axis_index("dp")
    while step >= 1:
        held = label_sum.shape[0] // 2
        mine = (at // step) % 2
        outgoing = lax.dynamic_slice_in_dim(label_sum, (1 - mine) * held, held, 0)
        kept = lax.dynamic_slice_in_dim(label_sum, mine * held, held, 0)
        label_sum = add(kept, swapped(outgoing, "dp", n_dp, step))
        step //= 2
    return row_out, label_sum


def solution(mesh):
    in_specs = (P("dp", None), P("label", None), P("label"), P("dp", None), P("dp", None))
    out_specs = (P(("dp", "label"), None), P(("label", "dp"), None))
    body = functools.partial(on_device, mesh.shape["dp"], mesh.shape["label"])
    return jax.shard_map(body, mesh=mesh, in_specs=in_specs, out_specs=out_specs, check_vma=False)
```

```python
import functools

import jax
import jax.numpy as jnp
from jax import lax
from jax.experimental import pallas as pl
from jax.experimental.pallas import tpu as pltpu
from jax.sharding import PartitionSpec as P

INST_BLOCK = 128
CLUSTER = 128
TILE = 256
CHUNK = 128
BLOCKS = 8
SCALE = 0.125

F32 = jnp.float32
BF16 = jnp.bfloat16
VMEM_LIMIT = 32 * 1024 * 1024


def half_index():
    return lax.axis_index("dp") // (lax.axis_size("dp") // 2)


def place(n_label):
    subs = n_label // 2 // BLOCKS
    pair = lax.axis_index("label") // 2
    return pair // subs, pair % subs, lax.axis_index("label") % 2


def slope_chunks(jobs, scores, w, embed, bias_ref, mask_ref, word_ref, before, emit):
    half_rows = w.shape[0] // 2
    clusters = half_rows // CLUSTER

    def score(n):
        k, t, h = jobs[n]
        before(k, t, h)
        first = k * half_rows + h * CHUNK
        scores[n % 2] = lax.dot_general(
            w[first : first + CHUNK],
            embed[t * TILE : (t + 1) * TILE],
            (((1,), (1,)), ((), ())),
            preferred_element_type=F32,
        )

    score(0)
    for n, (k, t, h) in enumerate(jobs):
        if n + 1 < len(jobs):
            score(n + 1)
        for i in range(CHUNK // CLUSTER):
            c = h * (CHUNK // CLUSTER) + i
            hit = (word_ref[:, t * TILE : (t + 1) * TILE] & jnp.int16(1 << (k * clusters + c))) != 0
            sign = jnp.where(hit, jnp.bfloat16(-1), jnp.bfloat16(1)).astype(F32)
            groups = []
            for g in range(TILE // INST_BLOCK):
                lanes = slice(g * INST_BLOCK, (g + 1) * INST_BLOCK)
                z = scores[n % 2, i * CLUSTER : (i + 1) * CLUSTER, lanes] * 0.5 + bias_ref[k, c]
                group = t * (TILE // INST_BLOCK) + g
                groups.append((jnp.tanh(z) + sign[:, lanes]).astype(BF16) * mask_ref[k, c, group : group + 1])
            emit(k, t, c, jnp.concatenate(groups, axis=1))


def block_in(t, i, over, core):
    first, second, third = 1 - t // 2, i // 2, i % 2
    owner = core if t % 2 else 1 - core
    return (first + 2 * second + 4 * third + owner * (first - second)) ^ over


def send_kernel(n_label, embed_hbm, weight_hbm, bias_hbm, beam_hbm, pos_hbm, embed, w, word, mask, bias_full, slopes_t,
                label_out, own_slopes_t, row_out, bias_raw, beam_raw, pos_raw, beam, scores, slopes, sems):
    half_rows = label_out.shape[0]
    clusters = half_rows // CLUSTER
    tiles = embed.shape[0] // TILE
    half = 1 - half_index()
    over, within, core = place(n_label)
    piece = embed.shape[0] // n_label
    subs = INST_BLOCK // piece // 2
    small = [
        pltpu.make_async_copy(source, target, sems.at[k])
        for k, (source, target) in enumerate(((beam_hbm, beam_raw), (bias_hbm, bias_raw), (pos_hbm, pos_raw)))
    ]
    w_copies = [
        pltpu.make_async_copy(
            weight_hbm.at[pl.ds(pl.multiple_of(which * half_rows, half_rows), half_rows)],
            w.at[pl.ds(k * half_rows, half_rows)],
            sems.at[3 + k],
        )
        for k, which in enumerate((half, 1 - half))
    ]
    e_copies = []
    for t in range(tiles):
        e_copies.append([])
        for i in range(4):
            for j in range(subs):
                at = t * (TILE // piece) + len(e_copies[t])
                row = block_in(t, i, over, core) * INST_BLOCK
                row = row + (2 * (j ^ within if subs > 1 else 0) + (core if t % 2 else 1 - core)) * piece
                e_copies[t].append(
                    pltpu.make_async_copy(
                        embed_hbm.at[pl.ds(pl.multiple_of(row, piece), piece)],
                        embed.at[pl.ds(at * piece, piece)],
                        sems.at[5 + at],
                    )
                )
    for copy in (*small, *e_copies[0], w_copies[0], *e_copies[1]):
        copy.start()
    for copy in small:
        copy.wait()
    for copy in (*e_copies[2], *e_copies[3]):
        copy.start()

    lane = lax.broadcasted_iota(jnp.int32, (BLOCKS, INST_BLOCK), 1)
    low = lane < INST_BLOCK // 2

    def relative_lanes(x):
        code = 2 * within + core
        for k in range((2 * subs).bit_length() - 1):
            shift = piece << k
            turned = jnp.where(
                (lane & shift) != 0, pltpu.roll(x, shift, 1), pltpu.roll(x, INST_BLOCK - shift, 1)
            )
            x = jnp.where((code >> k) % 2 == 1, turned, x)
        if subs > 1:
            x = jnp.concatenate(
                [x[:, (2 * j + c) * piece : (2 * j + c + 1) * piece] for c in range(2) for j in range(subs)], axis=1
            )
        return x

    first_label = lax.axis_index("label") * 2 * half_rows
    label_no = lax.broadcasted_iota(jnp.int32, (CLUSTER, INST_BLOCK), 0).astype(jnp.int16)
    for t in range(tiles):
        for g in range(TILE // INST_BLOCK):
            blocks = [block_in(t, 2 * g + h, over, core) for h in range(2)]
            one, two = (
                relative_lanes(pos_raw[:, pl.ds(pl.multiple_of(b * INST_BLOCK, INST_BLOCK), INST_BLOCK)]) for b in blocks
            )
            if t % 2:
                pos = jnp.where(low, one, pltpu.roll(two, INST_BLOCK // 2, 1))
            else:
                pos = jnp.where(low, pltpu.roll(one, INST_BLOCK // 2, 1), two)
            local = pos - first_label
            inside = (local >= 0) & (local < 2 * half_rows)
            bits = jnp.where(inside, jnp.left_shift(1, ((local >> 7) ^ (half * clusters)) & 15), 0).astype(jnp.int16)
            at = (local & (CLUSTER - 1)).astype(jnp.int16)
            found = jnp.zeros((CLUSTER, INST_BLOCK), jnp.int16)
            for p in range(pos.shape[0]):
                found = found | jnp.where(
                    label_no == jnp.broadcast_to(at[p : p + 1], found.shape),
                    jnp.broadcast_to(bits[p : p + 1], found.shape),
                    jnp.int16(0),
                )
            group = t * (TILE // INST_BLOCK) + g
            word[:, group * INST_BLOCK : (group + 1) * INST_BLOCK] = found
            for h in range(2):
                beam[8 * h + group : 8 * h + group + 1] = beam_raw[pl.ds(blocks[h], 1)]

    row = lax.broadcasted_iota(jnp.int32, (2 * clusters, 2 * clusters * INST_BLOCK), 0)
    column = lax.broadcasted_iota(jnp.int32, (2 * clusters, 2 * clusters * INST_BLOCK), 1)
    spread = jnp.where(row == (column // INST_BLOCK) ^ (half * clusters), 0.5, 0.0).astype(BF16)
    biases = lax.dot_general(bias_raw[...], spread, (((0,), (0,)), ((), ())), preferred_element_type=F32)
    first_cluster = lax.axis_index("label") * 2 * clusters
    for k in range(2):
        for c in range(clusters):
            i = k * clusters + c
            bias_full[k, c] = biases[:, i * INST_BLOCK : (i + 1) * INST_BLOCK]
            held = jnp.where(beam[...] == first_cluster + (i ^ (half * clusters)), 0.5 * SCALE, 0.0)
            held = jnp.broadcast_to(jnp.max(held, axis=1, keepdims=True), (2 * BLOCKS, INST_BLOCK))
            mask[k, c] = jnp.where(low, held[:BLOCKS], held[BLOCKS:]).astype(BF16)
    w_copies[0].wait()

    def before(k, t, h):
        if k == 0 and h == 0:
            for copy in e_copies[t]:
                copy.wait()
            if t == 1:
                w_copies[1].start()
        elif k == 1 and h == 0:
            w_copies[1].wait()

    def emit(k, t, c, part):
        if k == 0:
            slopes_t[c * CLUSTER : (c + 1) * CLUSTER, t * TILE : (t + 1) * TILE] = part
            if t == 0:
                slopes[:, c * CLUSTER : (c + 1) * CLUSTER] = part.T
        else:
            own_slopes_t[c * CLUSTER : (c + 1) * CLUSTER] = part
            slopes[:, half_rows + c * CLUSTER : half_rows + (c + 1) * CLUSTER] = part.T
        if (k, t) == (0, tiles - 1) and (c + 1) % (CHUNK // CLUSTER) == 0:
            rows = slice((c + 1) * CLUSTER - CHUNK, (c + 1) * CLUSTER)
            label_out[rows] = jnp.dot(slopes_t[rows], embed[...], preferred_element_type=F32).astype(BF16)

    chunks = range(half_rows // CHUNK)
    jobs = [(0, t, h) for t in range(tiles) for h in chunks] + [(1, 0, h) for h in chunks]
    slope_chunks(jobs, scores, w, embed, bias_full, mask, word, before, emit)
    store_rows([row_out], slopes, w)


def store_rows(outs, slopes, w):
    sums = jnp.dot(slopes[...], w[...], preferred_element_type=F32).astype(BF16)
    count = TILE // len(outs)
    for i, out in enumerate(outs):
        out[...] = sums[i * count : (i + 1) * count].reshape(out.shape)


def row_tile(t, outs, embed, w, word, mask, bias_full, first_slopes_t, own_slopes_t, scores, slopes):
    half_rows = w.shape[0] // 2

    def emit(k, t, c, part):
        if c == 0:
            slopes[:, :half_rows] = first_slopes_t[:, t * TILE : (t + 1) * TILE].T
        own_slopes_t[c * CLUSTER : (c + 1) * CLUSTER] = part
        slopes[:, half_rows + c * CLUSTER : half_rows + (c + 1) * CLUSTER] = part.T

    jobs = [(1, t, h) for h in range(half_rows // CHUNK)]
    slope_chunks(jobs, scores, w, embed, bias_full, mask, word, lambda *job: None, emit)
    store_rows(outs, slopes, w)


def keep_rows_kernel(embed, w, word, mask, bias_full, first_slopes_t, own_slopes_t, row_out, scores, slopes):
    row_tile(1, [row_out], embed, w, word, mask, bias_full, first_slopes_t, own_slopes_t, scores, slopes)


def last_rows_kernel(embed, w, word, mask, bias_full, first_slopes_t, one_slopes_t, two_slopes_t, *rest):
    *sends, row_out, label_out, three_slopes_t, four_slopes_t, scores, slopes = rest
    shared = (embed, w, word, mask, bias_full, first_slopes_t)
    row_tile(2, sends, *shared, three_slopes_t, scores.at[0], slopes.at[0])
    row_tile(3, [row_out], *shared, four_slopes_t, scores.at[1], slopes.at[1])
    total = 0.0
    for t, part in enumerate((one_slopes_t, two_slopes_t, three_slopes_t, four_slopes_t)):
        total = total + jnp.dot(part[...], embed[t * TILE : (t + 1) * TILE], preferred_element_type=F32)
    label_out[...] = total.astype(BF16)


def sum_kernel(places, *refs):
    *terms, out = refs
    out[...] = add(*(term[at] for term, at in zip(terms, places)))


def half_sum_kernel(kept, got, out):
    out[...] = add(kept[: out.shape[0]], got[: out.shape[0]])


def finish_kernel(kept, got, summed, *refs):
    *row_terms, row_out, label_out, row, rest, sems = refs
    first = summed.shape[0]
    copies = [
        pltpu.make_async_copy(row, row_out, sems.at[0]),
        pltpu.make_async_copy(summed, label_out.at[pl.ds(0, first)], sems.at[1]),
        pltpu.make_async_copy(rest, label_out.at[pl.ds(first, rest.shape[0])], sems.at[2]),
    ]
    copies[1].start()
    row[...] = add(*(term[(0,) * (len(term.shape) - 2)] for term in row_terms))
    copies[0].start()
    rest[...] = add(kept[first:], got[first:])
    copies[2].start()
    for copy in copies:
        copy.wait()


def swapped(value, axis, size, bit):
    return lax.ppermute(value, axis, [(i, i ^ bit) for i in range(size)])


def add(*terms):
    total = terms[0].astype(F32)
    for term in terms[1:]:
        total = total + term.astype(F32)
    return total.astype(BF16)


def on_device(n_dp, n_label, embed, weight, bias, beam, positives):
    rows, features = embed.shape
    labels = weight.shape[0]
    half_rows = labels // 2
    clusters = half_rows // CLUSTER
    piece = rows // n_label
    subs = n_label // 2 // BLOCKS
    bias_rows = bias.reshape(labels // CLUSTER, CLUSTER)
    pos_rows = positives.T
    vmem = pl.BlockSpec(memory_space=pltpu.VMEM)
    hbm = pl.BlockSpec(memory_space=pltpu.HBM)
    params = pltpu.CompilerParams(vmem_limit_bytes=VMEM_LIMIT)
    shape = jax.ShapeDtypeStruct
    tile_shape = shape((half_rows, TILE), BF16)
    row_shape = shape((BLOCKS // 2, subs, piece, features), BF16)
    score_scratch = pltpu.VMEM((2, CHUNK, TILE), F32)
    slope_scratch = pltpu.VMEM((TILE, labels), BF16)

    def cost(halves):
        return pl.CostEstimate(flops=halves * 2 * rows * half_rows * features, bytes_accessed=0, transcendentals=0)

    *shared, label_send, one_slopes_t, first_send = pl.pallas_call(
        functools.partial(send_kernel, n_label),
        out_shape=[
            shape((rows, features), BF16),
            shape((labels, features), BF16),
            shape((CLUSTER, rows), jnp.int16),
            shape((2, clusters, BLOCKS, INST_BLOCK), BF16),
            shape((2, clusters, CLUSTER, INST_BLOCK), F32),
            shape((half_rows, rows), BF16),
            shape((half_rows, features), BF16),
            tile_shape,
            row_shape,
        ],
        in_specs=[hbm] * 5,
        out_specs=[vmem] * 9,
        scratch_shapes=[
            pltpu.VMEM(bias_rows.shape, BF16),
            pltpu.VMEM(beam.shape, jnp.int32),
            pltpu.VMEM(pos_rows.shape, jnp.int32),
            pltpu.VMEM((2 * BLOCKS, beam.shape[1]), jnp.int32),
            score_scratch,
            slope_scratch,
            pltpu.SemaphoreType.DMA((5 + n_label,)),
        ],
        compiler_params=params,
        cost_estimate=cost(3),
        name="send_half",
    )(*(pltpu.with_memory_space_constraint(x, pltpu.HBM) for x in (embed, weight, bias_rows, beam, pos_rows)))

    first_got = swapped(first_send, "label", n_label, 1)
    label_got = swapped(label_send, "dp", n_dp, n_dp // 2)
    first_got, *shared = lax.optimization_barrier((first_got, *shared))

    two_slopes_t, first_keep = pl.pallas_call(
        keep_rows_kernel,
        out_shape=[tile_shape, row_shape],
        in_specs=[vmem] * 6,
        out_specs=[vmem] * 2,
        scratch_shapes=[score_scratch, slope_scratch],
        compiler_params=params,
        cost_estimate=cost(0),
        name="keep_rows",
    )(*shared)

    axes = [2 * subs, 4 * subs, 8 * subs]

    def summed_at(*terms):
        arrays, places = zip(*terms)
        size = places[0].stop - places[0].start
        return pl.pallas_call(
            functools.partial(sum_kernel, places),
            out_shape=shape((size, subs, piece, features), BF16),
            in_specs=[vmem] * len(arrays),
            out_specs=vmem,
            compiler_params=params,
            cost_estimate=cost(0),
            name="row_sum",
        )(*arrays)

    def passed_on(value, stage):
        bits = (axes[stage], axes[stage if stage == 2 else 1 - stage])
        return lax.ppermute(value, "label", [(i, i ^ bits[i % 2]) for i in range(n_label)])

    far_got = passed_on(summed_at((first_keep, slice(1, 4)), (first_got, slice(1, 4))), 0)
    near_got = passed_on(summed_at((first_keep, slice(0, 1)), (first_got, slice(0, 1))), 0)

    part_shape = shape((2, subs, piece, features), BF16)
    *last_send, last_keep, label_keep = pl.pallas_call(
        last_rows_kernel,
        out_shape=[part_shape] * 2 + [row_shape, shape((half_rows, features), BF16)],
        in_specs=[vmem] * 8,
        out_specs=[vmem] * 4,
        scratch_shapes=[
            pltpu.VMEM((half_rows, TILE), BF16),
            pltpu.VMEM((half_rows, TILE), BF16),
            pltpu.VMEM((2, 2, CHUNK, TILE), F32),
            pltpu.VMEM((2, TILE, labels), BF16),
        ],
        compiler_params=params,
        cost_estimate=cost(0),
        name="last_rows",
    )(*shared, one_slopes_t, two_slopes_t)

    last_got = [swapped(part, "label", n_label, 1) for part in last_send]
    three_got = passed_on(summed_at((last_keep, slice(3, 4)), (last_got[1], slice(1, 2)), (far_got, slice(2, 3))), 1)
    two_got = passed_on(summed_at((last_keep, slice(2, 3)), (last_got[1], slice(0, 1)), (far_got, slice(1, 2))), 1)
    row_got = passed_on(summed_at((last_keep, slice(1, 2)), (last_got[0], slice(1, 2)), (far_got, slice(0, 1)), (three_got, slice(0, 1))), 2)
    row_terms = [last_keep, last_got[0], near_got, two_got, row_got]
    bit = subs
    while bit > 1:
        row_sum = add(*(term.reshape(-1, subs, piece, features)[0] for term in row_terms[:-1]))
        held = row_sum.shape[0] // 2
        came = row_terms[-1].reshape(subs, piece, features)
        incoming = swapped(add(row_sum[held:], came[held:]), "label", n_label, bit)
        row_terms = [add(row_sum[:held], came[:held]), incoming]
        subs = held
        bit //= 2

    kept, got = label_keep, label_got
    step = n_dp // 4
    at = lax.axis_index("dp")
    while step >= 1:
        label_sum = add(kept, got)
        size = label_sum.shape[0] // 2
        mine = (at // step) % 2
        outgoing = lax.dynamic_slice_in_dim(label_sum, (1 - mine) * size, size, 0)
        kept = lax.dynamic_slice_in_dim(label_sum, mine * size, size, 0)
        got = swapped(outgoing, "dp", n_dp, step)
        step //= 2

    size = kept.shape[0]
    summed = pl.pallas_call(
        half_sum_kernel,
        out_shape=shape((size // 2, features), BF16),
        in_specs=[vmem] * 2,
        out_specs=vmem,
        compiler_params=params,
        cost_estimate=cost(2),
        name="half_sum",
    )(kept, got)
    return pl.pallas_call(
        finish_kernel,
        out_shape=[shape((piece, features), BF16), shape((size, features), BF16)],
        in_specs=[vmem] * (3 + len(row_terms)),
        out_specs=[hbm] * 2,
        scratch_shapes=[
            pltpu.VMEM((piece, features), BF16),
            pltpu.VMEM((size // 2, features), BF16),
            pltpu.SemaphoreType.DMA((3,)),
        ],
        compiler_params=params,
        cost_estimate=cost(0),
        name="finish",
    )(kept, got, summed, *row_terms)


def solution(mesh):
    in_specs = (P("dp", None), P("label", None), P("label"), P("dp", None), P("dp", None))
    out_specs = (P(("dp", "label"), None), P(("label", "dp"), None))
    body = functools.partial(on_device, mesh.shape["dp"], mesh.shape["label"])
    return jax.shard_map(body, mesh=mesh, in_specs=in_specs, out_specs=out_specs, check_vma=False)
```

```python
import functools

import jax
import jax.numpy as jnp
from jax import lax
from jax.experimental import pallas as pl
from jax.experimental.pallas import tpu as pltpu
from jax.sharding import PartitionSpec as P

INST_BLOCK = 128
CLUSTER = 128
TILE = 256
CHUNK = 256
CLUSTERS = 8
BLOCKS = 8
SCALE = 0.125

F32 = jnp.float32
BF16 = jnp.bfloat16
VMEM_LIMIT = 32 * 1024 * 1024


def half_index():
    return lax.axis_index("dp") // (lax.axis_size("dp") // 2)


def place(n_label):
    subs = n_label // 2 // BLOCKS
    pair = lax.axis_index("label") // 2
    return pair // subs, pair % subs, lax.axis_index("label") % 2


def slope_chunks(jobs, scores, w, embed, bias_ref, mask_ref, word_ref, before, emit):
    half_rows = w.shape[0] // 2
    clusters = half_rows // CLUSTER

    def score(n):
        k, t, h = jobs[n]
        before(k, t, h)
        first = k * half_rows + h * CHUNK
        scores[n % 2] = lax.dot_general(
            w[first : first + CHUNK],
            embed[t * TILE : (t + 1) * TILE],
            (((1,), (1,)), ((), ())),
            preferred_element_type=F32,
        )

    score(0)
    for n, (k, t, h) in enumerate(jobs):
        if n + 1 < len(jobs):
            score(n + 1)
        for i in range(CHUNK // CLUSTER):
            c = h * (CHUNK // CLUSTER) + i
            hit = (word_ref[:, t * TILE : (t + 1) * TILE] & jnp.int16(1 << (k * clusters + c))) != 0
            sign = jnp.where(hit, jnp.bfloat16(-1), jnp.bfloat16(1)).astype(F32)
            groups = []
            for g in range(TILE // INST_BLOCK):
                lanes = slice(g * INST_BLOCK, (g + 1) * INST_BLOCK)
                z = scores[n % 2, i * CLUSTER : (i + 1) * CLUSTER, lanes] * 0.5 + bias_ref[k, c]
                group = t * (TILE // INST_BLOCK) + g
                groups.append((jnp.tanh(z) + sign[:, lanes]).astype(BF16) * mask_ref[k, c, group : group + 1])
            emit(k, t, c, jnp.concatenate(groups, axis=1))


def block_in(t, i, over, core):
    first, second, third = 1 - t // 2, i // 2, i % 2
    owner = core if t % 2 else 1 - core
    return (first + 2 * second + 4 * third + owner * (first - second)) ^ over


def set_words(tiles, pos_ref, word):
    half_rows = CLUSTER * CLUSTERS // 2
    first_label = lax.axis_index("label") * 2 * half_rows
    send_half = 1 - half_index()
    label_no = lax.broadcasted_iota(jnp.int32, (CLUSTER, TILE), 0).astype(jnp.int16)
    for t in tiles:
        lanes = slice(t * TILE, (t + 1) * TILE)
        local = pos_ref[:, lanes] - first_label
        inside = (local >= 0) & (local < 2 * half_rows)
        bits = jnp.where(inside, jnp.left_shift(1, ((local >> 7) ^ (send_half * (CLUSTERS // 2))) & 15), 0).astype(jnp.int16)
        at = (local & (CLUSTER - 1)).astype(jnp.int16)
        found = jnp.zeros((CLUSTER, TILE), jnp.int16)
        for p in range(pos_ref.shape[0]):
            found = found | jnp.where(
                label_no == jnp.broadcast_to(at[p : p + 1], found.shape),
                jnp.broadcast_to(bits[p : p + 1], found.shape),
                jnp.int16(0),
            )
        word[:, lanes] = found


def first_kernel(n_label, embed_hbm, weight_hbm, bias_hbm, beam_hbm, pos_hbm, embed, w, pos, mask, bias_full,
                 first_slopes_t, own_slopes_t, row_out, bias_raw, beam_raw, pos_raw, beam, word, scores, slopes, sems):
    half_rows = own_slopes_t.shape[0]
    clusters = half_rows // CLUSTER
    tiles = embed.shape[0] // TILE
    half = 1 - half_index()
    over, within, core = place(n_label)
    piece = embed.shape[0] // n_label
    subs = INST_BLOCK // piece // 2
    small = [
        pltpu.make_async_copy(source, target, sems.at[k])
        for k, (source, target) in enumerate(((beam_hbm, beam_raw), (bias_hbm, bias_raw), (pos_hbm, pos_raw)))
    ]
    w_copies = [
        pltpu.make_async_copy(
            weight_hbm.at[pl.ds(pl.multiple_of(which * half_rows, half_rows), half_rows)],
            w.at[pl.ds(k * half_rows, half_rows)],
            sems.at[3 + k],
        )
        for k, which in enumerate((half, 1 - half))
    ]
    e_copies = []
    for t in range(tiles):
        e_copies.append([])
        for i in range(4):
            for j in range(subs):
                at = t * (TILE // piece) + len(e_copies[t])
                row = block_in(t, i, over, core) * INST_BLOCK
                row = row + (2 * (j ^ within if subs > 1 else 0) + (core if t % 2 else 1 - core)) * piece
                e_copies[t].append(
                    pltpu.make_async_copy(
                        embed_hbm.at[pl.ds(pl.multiple_of(row, piece), piece)],
                        embed.at[pl.ds(at * piece, piece)],
                        sems.at[5 + at],
                    )
                )
    for copy in (*small, *e_copies[0], *w_copies):
        copy.start()
    for copy in small:
        copy.wait()
    for copy in (*e_copies[1], *e_copies[2], *e_copies[3]):
        copy.start()

    lane = lax.broadcasted_iota(jnp.int32, (BLOCKS, INST_BLOCK), 1)
    low = lane < INST_BLOCK // 2

    def relative_lanes(x):
        code = 2 * within + core
        for k in range((2 * subs).bit_length() - 1):
            shift = piece << k
            turned = jnp.where(
                (lane & shift) != 0, pltpu.roll(x, shift, 1), pltpu.roll(x, INST_BLOCK - shift, 1)
            )
            x = jnp.where((code >> k) % 2 == 1, turned, x)
        if subs > 1:
            x = jnp.concatenate(
                [x[:, (2 * j + c) * piece : (2 * j + c + 1) * piece] for c in range(2) for j in range(subs)], axis=1
            )
        return x

    for t in range(tiles):
        for g in range(TILE // INST_BLOCK):
            blocks = [block_in(t, 2 * g + h, over, core) for h in range(2)]
            one, two = (
                relative_lanes(pos_raw[:, pl.ds(pl.multiple_of(b * INST_BLOCK, INST_BLOCK), INST_BLOCK)]) for b in blocks
            )
            group = t * (TILE // INST_BLOCK) + g
            pos[:, group * INST_BLOCK : (group + 1) * INST_BLOCK] = (
                jnp.where(low, one, pltpu.roll(two, INST_BLOCK // 2, 1))
                if t % 2
                else jnp.where(low, pltpu.roll(one, INST_BLOCK // 2, 1), two)
            )
            for h in range(2):
                beam[8 * h + group : 8 * h + group + 1] = beam_raw[pl.ds(blocks[h], 1)]
    set_words([0], pos, word)

    row = lax.broadcasted_iota(jnp.int32, (2 * clusters, 2 * clusters * INST_BLOCK), 0)
    column = lax.broadcasted_iota(jnp.int32, (2 * clusters, 2 * clusters * INST_BLOCK), 1)
    spread = jnp.where(row == (column // INST_BLOCK) ^ (half * clusters), 0.5, 0.0).astype(BF16)
    biases = lax.dot_general(bias_raw[...], spread, (((0,), (0,)), ((), ())), preferred_element_type=F32)
    first_cluster = lax.axis_index("label") * 2 * clusters
    for k in range(2):
        for c in range(clusters):
            i = k * clusters + c
            bias_full[k, c] = biases[:, i * INST_BLOCK : (i + 1) * INST_BLOCK]
            held = jnp.where(beam[...] == first_cluster + (i ^ (half * clusters)), 0.5 * SCALE, 0.0)
            held = jnp.broadcast_to(jnp.max(held, axis=1, keepdims=True), (2 * BLOCKS, INST_BLOCK))
            mask[k, c] = jnp.where(low, held[:BLOCKS], held[BLOCKS:]).astype(BF16)
    for copy in (w_copies[0], *e_copies[0]):
        copy.wait()

    def before(k, t, h):
        if (k, h) == (1, 0):
            w_copies[1].wait()

    def emit(k, t, c, part):
        out = own_slopes_t if k else first_slopes_t
        out[c * CLUSTER : (c + 1) * CLUSTER] = part
        slopes[:, (k * clusters + c) * CLUSTER : (k * clusters + c + 1) * CLUSTER] = part.T

    jobs = [(k, 0, h) for k in range(2) for h in range(half_rows // CHUNK)]
    slope_chunks(jobs, scores, w, embed, bias_full, mask, word, before, emit)
    store_rows([row_out], slopes, w)
    for copy in (*e_copies[1], *e_copies[2], *e_copies[3]):
        copy.wait()


def label_kernel(embed, w, pos, mask, bias_full, one_slopes_t, word, slopes_t, label_out, scores):
    half_rows = label_out.shape[0]
    tiles = embed.shape[0] // TILE
    set_words(range(1, tiles), pos, word)

    def emit(k, t, c, part):
        slopes_t[c * CLUSTER : (c + 1) * CLUSTER, (t - 1) * TILE : t * TILE] = part
        if t == tiles - 1 and (c + 1) % (CHUNK // CLUSTER) == 0:
            rows = slice((c + 1) * CLUSTER - CHUNK, (c + 1) * CLUSTER)
            label_out[rows] = (
                jnp.dot(one_slopes_t[rows], embed[:TILE], preferred_element_type=F32)
                + jnp.dot(slopes_t[rows], embed[TILE:], preferred_element_type=F32)
            ).astype(BF16)

    jobs = [(0, t, h) for t in range(1, tiles) for h in range(half_rows // CHUNK)]
    slope_chunks(jobs, scores, w, embed, bias_full, mask, word, lambda *job: None, emit)


def store_rows(outs, slopes, w):
    sums = jnp.dot(slopes[...], w[...], preferred_element_type=F32).astype(BF16)
    count = TILE // len(outs)
    for i, out in enumerate(outs):
        out[...] = sums[i * count : (i + 1) * count].reshape(out.shape)


def row_tile(t, outs, embed, w, word, mask, bias_full, first_slopes_t, own_slopes_t, scores, slopes):
    half_rows = w.shape[0] // 2

    def emit(k, t, c, part):
        if c == 0:
            slopes[:, :half_rows] = first_slopes_t[:, (t - 1) * TILE : t * TILE].T
        own_slopes_t[c * CLUSTER : (c + 1) * CLUSTER] = part
        slopes[:, half_rows + c * CLUSTER : half_rows + (c + 1) * CLUSTER] = part.T

    jobs = [(1, t, h) for h in range(half_rows // CHUNK)]
    slope_chunks(jobs, scores, w, embed, bias_full, mask, word, lambda *job: None, emit)
    store_rows(outs, slopes, w)


def keep_rows_kernel(embed, w, word, mask, bias_full, first_slopes_t, own_slopes_t, row_out, scores, slopes):
    row_tile(1, [row_out], embed, w, word, mask, bias_full, first_slopes_t, own_slopes_t, scores, slopes)


def last_rows_kernel(embed, w, word, mask, bias_full, first_slopes_t, one_slopes_t, two_slopes_t, *rest):
    *sends, row_out, label_out, three_slopes_t, four_slopes_t, scores, slopes = rest
    shared = (embed, w, word, mask, bias_full, first_slopes_t)
    row_tile(2, sends, *shared, three_slopes_t, scores.at[0], slopes.at[0])
    row_tile(3, [row_out], *shared, four_slopes_t, scores.at[1], slopes.at[1])
    total = 0.0
    for t, part in enumerate((one_slopes_t, two_slopes_t, three_slopes_t, four_slopes_t)):
        total = total + jnp.dot(part[...], embed[t * TILE : (t + 1) * TILE], preferred_element_type=F32)
    label_out[...] = total.astype(BF16)


def sum_kernel(places, *refs):
    *terms, out = refs
    out[...] = add(*(term[at] for term, at in zip(terms, places)))


def half_sum_kernel(kept, got, out):
    out[...] = add(kept[: out.shape[0]], got[: out.shape[0]])


def finish_kernel(kept, got, summed, *refs):
    *row_terms, row_out, label_out, row, rest, sems = refs
    first = summed.shape[0]
    copies = [
        pltpu.make_async_copy(row, row_out, sems.at[0]),
        pltpu.make_async_copy(summed, label_out.at[pl.ds(0, first)], sems.at[1]),
        pltpu.make_async_copy(rest, label_out.at[pl.ds(first, rest.shape[0])], sems.at[2]),
    ]
    copies[1].start()
    row[...] = add(*(term[(0,) * (len(term.shape) - 2)] for term in row_terms))
    copies[0].start()
    rest[...] = add(kept[first:], got[first:])
    copies[2].start()
    for copy in copies:
        copy.wait()


def swapped(value, axis, size, bit):
    return lax.ppermute(value, axis, [(i, i ^ bit) for i in range(size)])


def add(*terms):
    total = terms[0].astype(F32)
    for term in terms[1:]:
        total = total + term.astype(F32)
    return total.astype(BF16)


def on_device(n_dp, n_label, embed, weight, bias, beam, positives):
    rows, features = embed.shape
    labels = weight.shape[0]
    half_rows = labels // 2
    clusters = half_rows // CLUSTER
    piece = rows // n_label
    subs = n_label // 2 // BLOCKS
    bias_rows = bias.reshape(labels // CLUSTER, CLUSTER)
    pos_rows = positives.T
    vmem = pl.BlockSpec(memory_space=pltpu.VMEM)
    hbm = pl.BlockSpec(memory_space=pltpu.HBM)
    params = pltpu.CompilerParams(vmem_limit_bytes=VMEM_LIMIT)
    shape = jax.ShapeDtypeStruct
    tile_shape = shape((half_rows, TILE), BF16)
    row_shape = shape((BLOCKS // 2, subs, piece, features), BF16)
    score_scratch = pltpu.VMEM((2, CHUNK, TILE), F32)
    slope_scratch = pltpu.VMEM((TILE, labels), BF16)

    def cost(halves):
        return pl.CostEstimate(flops=halves * 2 * rows * half_rows * features, bytes_accessed=0, transcendentals=0)

    *common, head_slopes_t, one_slopes_t, first_send = pl.pallas_call(
        functools.partial(first_kernel, n_label),
        out_shape=[
            shape((rows, features), BF16),
            shape((labels, features), BF16),
            shape(pos_rows.shape, jnp.int32),
            shape((2, clusters, BLOCKS, INST_BLOCK), BF16),
            shape((2, clusters, CLUSTER, INST_BLOCK), F32),
            tile_shape,
            tile_shape,
            row_shape,
        ],
        in_specs=[hbm] * 5,
        out_specs=[vmem] * 8,
        scratch_shapes=[
            pltpu.VMEM(bias_rows.shape, BF16),
            pltpu.VMEM(beam.shape, jnp.int32),
            pltpu.VMEM(pos_rows.shape, jnp.int32),
            pltpu.VMEM((2 * BLOCKS, beam.shape[1]), jnp.int32),
            pltpu.VMEM((CLUSTER, TILE), jnp.int16),
            score_scratch,
            slope_scratch,
            pltpu.SemaphoreType.DMA((5 + n_label,)),
        ],
        compiler_params=params,
        cost_estimate=cost(2),
        name="first_rows",
    )(*(pltpu.with_memory_space_constraint(x, pltpu.HBM) for x in (embed, weight, bias_rows, beam, pos_rows)))

    first_got = swapped(first_send, "label", n_label, 1)

    word, first_slopes_t, label_send = pl.pallas_call(
        label_kernel,
        out_shape=[
            shape((CLUSTER, rows), jnp.int16),
            shape((half_rows, rows - TILE), BF16),
            shape((half_rows, features), BF16),
        ],
        in_specs=[vmem] * 6,
        out_specs=[vmem] * 3,
        scratch_shapes=[score_scratch],
        compiler_params=params,
        cost_estimate=cost(0),
        name="send_half",
    )(*common, head_slopes_t)
    embed_own, w, _, mask, bias_full = common
    shared = (embed_own, w, word, mask, bias_full, first_slopes_t)

    label_got = swapped(label_send, "dp", n_dp, n_dp // 2)
    first_got, *shared = lax.optimization_barrier((first_got, *shared))

    two_slopes_t, first_keep = pl.pallas_call(
        keep_rows_kernel,
        out_shape=[tile_shape, row_shape],
        in_specs=[vmem] * 6,
        out_specs=[vmem] * 2,
        scratch_shapes=[score_scratch, slope_scratch],
        compiler_params=params,
        cost_estimate=cost(0),
        name="keep_rows",
    )(*shared)

    axes = [2 * subs, 4 * subs, 8 * subs]

    def summed_at(*terms):
        arrays, places = zip(*terms)
        size = places[0].stop - places[0].start
        return pl.pallas_call(
            functools.partial(sum_kernel, places),
            out_shape=shape((size, subs, piece, features), BF16),
            in_specs=[vmem] * len(arrays),
            out_specs=vmem,
            compiler_params=params,
            cost_estimate=cost(0),
            name="row_sum",
        )(*arrays)

    def passed_on(value, stage):
        bits = (axes[stage], axes[stage if stage == 2 else 1 - stage])
        return lax.ppermute(value, "label", [(i, i ^ bits[i % 2]) for i in range(n_label)])

    far_got = passed_on(summed_at((first_keep, slice(1, 4)), (first_got, slice(1, 4))), 0)
    near_got = passed_on(summed_at((first_keep, slice(0, 1)), (first_got, slice(0, 1))), 0)

    part_shape = shape((2, subs, piece, features), BF16)
    *last_send, last_keep, label_keep = pl.pallas_call(
        last_rows_kernel,
        out_shape=[part_shape] * 2 + [row_shape, shape((half_rows, features), BF16)],
        in_specs=[vmem] * 8,
        out_specs=[vmem] * 4,
        scratch_shapes=[
            pltpu.VMEM((half_rows, TILE), BF16),
            pltpu.VMEM((half_rows, TILE), BF16),
            pltpu.VMEM((2, 2, CHUNK, TILE), F32),
            pltpu.VMEM((2, TILE, labels), BF16),
        ],
        compiler_params=params,
        cost_estimate=cost(0),
        name="last_rows",
    )(*shared, one_slopes_t, two_slopes_t)

    last_got = [swapped(part, "label", n_label, 1) for part in last_send]
    three_got = passed_on(summed_at((last_keep, slice(3, 4)), (last_got[1], slice(1, 2)), (far_got, slice(2, 3))), 1)
    two_got = passed_on(summed_at((last_keep, slice(2, 3)), (last_got[1], slice(0, 1)), (far_got, slice(1, 2))), 1)
    row_got = passed_on(summed_at((last_keep, slice(1, 2)), (last_got[0], slice(1, 2)), (far_got, slice(0, 1)), (three_got, slice(0, 1))), 2)
    row_terms = [last_keep, last_got[0], near_got, two_got, row_got]
    bit = subs
    while bit > 1:
        row_sum = add(*(term.reshape(-1, subs, piece, features)[0] for term in row_terms[:-1]))
        held = row_sum.shape[0] // 2
        came = row_terms[-1].reshape(subs, piece, features)
        incoming = swapped(add(row_sum[held:], came[held:]), "label", n_label, bit)
        row_terms = [add(row_sum[:held], came[:held]), incoming]
        subs = held
        bit //= 2

    kept, got = label_keep, label_got
    step = n_dp // 4
    at = lax.axis_index("dp")
    while step >= 1:
        label_sum = add(kept, got)
        size = label_sum.shape[0] // 2
        mine = (at // step) % 2
        outgoing = lax.dynamic_slice_in_dim(label_sum, (1 - mine) * size, size, 0)
        kept = lax.dynamic_slice_in_dim(label_sum, mine * size, size, 0)
        got = swapped(outgoing, "dp", n_dp, step)
        step //= 2

    size = kept.shape[0]
    summed = pl.pallas_call(
        half_sum_kernel,
        out_shape=shape((size // 2, features), BF16),
        in_specs=[vmem] * 2,
        out_specs=vmem,
        compiler_params=params,
        cost_estimate=cost(2),
        name="half_sum",
    )(kept, got)
    return pl.pallas_call(
        finish_kernel,
        out_shape=[shape((piece, features), BF16), shape((size, features), BF16)],
        in_specs=[vmem] * (3 + len(row_terms)),
        out_specs=[hbm] * 2,
        scratch_shapes=[
            pltpu.VMEM((piece, features), BF16),
            pltpu.VMEM((size // 2, features), BF16),
            pltpu.SemaphoreType.DMA((3,)),
        ],
        compiler_params=params,
        cost_estimate=cost(0),
        name="finish",
    )(kept, got, summed, *row_terms)


def solution(mesh):
    in_specs = (P("dp", None), P("label", None), P("label"), P("dp", None), P("dp", None))
    out_specs = (P(("dp", "label"), None), P(("label", "dp"), None))
    body = functools.partial(on_device, mesh.shape["dp"], mesh.shape["label"])
    return jax.shard_map(body, mesh=mesh, in_specs=in_specs, out_specs=out_specs, check_vma=False)
```

```python
import functools

import jax
import jax.numpy as jnp
from jax import lax
from jax.experimental import pallas as pl
from jax.experimental.pallas import tpu as pltpu
from jax.sharding import PartitionSpec as P

INST_BLOCK = 128
CLUSTER = 128
TILE = 256
CHUNK = 256
CLUSTERS = 8
BLOCKS = 8
SCALE = 0.125

F32 = jnp.float32
BF16 = jnp.bfloat16
VMEM_LIMIT = 32 * 1024 * 1024


def half_index():
    return lax.axis_index("dp") // (lax.axis_size("dp") // 2)


def place(n_label):
    subs = n_label // 2 // BLOCKS
    pair = lax.axis_index("label") // 2
    return pair // subs, pair % subs, lax.axis_index("label") % 2


def slope_chunks(jobs, scores, w, embed, bias_ref, mask_ref, word_ref, before, emit):
    half_rows = w.shape[0] // 2
    clusters = half_rows // CLUSTER

    def score(n):
        k, t, h = jobs[n]
        before(k, t, h)
        first = k * half_rows + h * CHUNK
        scores[n % 2] = lax.dot_general(
            w[first : first + CHUNK],
            embed[t * TILE : (t + 1) * TILE],
            (((1,), (1,)), ((), ())),
            preferred_element_type=F32,
        )

    score(0)
    for n, (k, t, h) in enumerate(jobs):
        if n + 1 < len(jobs):
            score(n + 1)
        for i in range(CHUNK // CLUSTER):
            c = h * (CHUNK // CLUSTER) + i
            hit = (word_ref[:, t * TILE : (t + 1) * TILE] & jnp.int16(1 << (k * clusters + c))) != 0
            sign = jnp.where(hit, jnp.bfloat16(-1), jnp.bfloat16(1)).astype(F32)
            groups = []
            for g in range(TILE // INST_BLOCK):
                lanes = slice(g * INST_BLOCK, (g + 1) * INST_BLOCK)
                z = scores[n % 2, i * CLUSTER : (i + 1) * CLUSTER, lanes] * 0.5 + bias_ref[k, c]
                group = t * (TILE // INST_BLOCK) + g
                groups.append((jnp.tanh(z) + sign[:, lanes]).astype(BF16) * mask_ref[k, c, group : group + 1])
            emit(k, t, c, jnp.concatenate(groups, axis=1))


def block_in(t, i, over, core):
    first, second, third = 1 - t // 2, i // 2, i % 2
    owner = core if t % 2 else 1 - core
    return (first + 2 * second + 4 * third + owner * (first - second)) ^ over


def set_words(tiles, pos_ref, word):
    half_rows = CLUSTER * CLUSTERS // 2
    first_label = lax.axis_index("label") * 2 * half_rows
    send_half = 1 - half_index()
    label_no = lax.broadcasted_iota(jnp.int32, (CLUSTER, TILE), 0).astype(jnp.int16)
    for t in tiles:
        lanes = slice(t * TILE, (t + 1) * TILE)
        local = pos_ref[:, lanes] - first_label
        inside = (local >= 0) & (local < 2 * half_rows)
        bits = jnp.where(inside, jnp.left_shift(1, ((local >> 7) ^ (send_half * (CLUSTERS // 2))) & 15), 0).astype(jnp.int16)
        at = (local & (CLUSTER - 1)).astype(jnp.int16)
        found = jnp.zeros((CLUSTER, TILE), jnp.int16)
        for p in range(pos_ref.shape[0]):
            found = found | jnp.where(
                label_no == jnp.broadcast_to(at[p : p + 1], found.shape),
                jnp.broadcast_to(bits[p : p + 1], found.shape),
                jnp.int16(0),
            )
        word[:, lanes] = found


def first_kernel(n_label, embed_hbm, weight_hbm, bias_hbm, beam_hbm, pos_hbm, embed, w, pos, mask, bias_full,
                 first_slopes_t, own_slopes_t, row_out, bias_raw, beam_raw, pos_raw, beam, word, scores, slopes, sems):
    half_rows = own_slopes_t.shape[0]
    clusters = half_rows // CLUSTER
    tiles = embed.shape[0] // TILE
    half = 1 - half_index()
    over, within, core = place(n_label)
    piece = embed.shape[0] // n_label
    subs = INST_BLOCK // piece // 2
    small = [
        pltpu.make_async_copy(source, target, sems.at[k])
        for k, (source, target) in enumerate(((beam_hbm, beam_raw), (bias_hbm, bias_raw), (pos_hbm, pos_raw)))
    ]
    w_copies = [
        pltpu.make_async_copy(
            weight_hbm.at[pl.ds(pl.multiple_of(which * half_rows, half_rows), half_rows)],
            w.at[pl.ds(k * half_rows, half_rows)],
            sems.at[3 + k],
        )
        for k, which in enumerate((half, 1 - half))
    ]
    e_copies = []
    for t in range(tiles):
        e_copies.append([])
        for i in range(4):
            for j in range(subs):
                at = t * (TILE // piece) + len(e_copies[t])
                row = block_in(t, i, over, core) * INST_BLOCK
                row = row + (2 * (j ^ within if subs > 1 else 0) + (core if t % 2 else 1 - core)) * piece
                e_copies[t].append(
                    pltpu.make_async_copy(
                        embed_hbm.at[pl.ds(pl.multiple_of(row, piece), piece)],
                        embed.at[pl.ds(at * piece, piece)],
                        sems.at[5 + at],
                    )
                )
    for copy in (*small, *e_copies[0], *w_copies):
        copy.start()
    for copy in small:
        copy.wait()

    lane = lax.broadcasted_iota(jnp.int32, (BLOCKS, INST_BLOCK), 1)
    low = lane < INST_BLOCK // 2

    def relative_lanes(x):
        code = 2 * within + core
        for k in range((2 * subs).bit_length() - 1):
            shift = piece << k
            turned = jnp.where(
                (lane & shift) != 0, pltpu.roll(x, shift, 1), pltpu.roll(x, INST_BLOCK - shift, 1)
            )
            x = jnp.where((code >> k) % 2 == 1, turned, x)
        if subs > 1:
            x = jnp.concatenate(
                [x[:, (2 * j + c) * piece : (2 * j + c + 1) * piece] for c in range(2) for j in range(subs)], axis=1
            )
        return x

    def set_positives(t):
        for g in range(TILE // INST_BLOCK):
            one, two = (
                relative_lanes(
                    pos_raw[:, pl.ds(pl.multiple_of(block_in(t, 2 * g + h, over, core) * INST_BLOCK, INST_BLOCK), INST_BLOCK)]
                )
                for h in range(2)
            )
            group = t * (TILE // INST_BLOCK) + g
            pos[:, group * INST_BLOCK : (group + 1) * INST_BLOCK] = (
                jnp.where(low, one, pltpu.roll(two, INST_BLOCK // 2, 1))
                if t % 2
                else jnp.where(low, pltpu.roll(one, INST_BLOCK // 2, 1), two)
            )

    for t in range(tiles):
        for i in range(4):
            group = 8 * (i % 2) + t * 2 + i // 2
            beam[group : group + 1] = beam_raw[pl.ds(block_in(t, i, over, core), 1)]
    set_positives(0)
    set_words([0], pos, word)

    row = lax.broadcasted_iota(jnp.int32, (2 * clusters, 2 * clusters * INST_BLOCK), 0)
    column = lax.broadcasted_iota(jnp.int32, (2 * clusters, 2 * clusters * INST_BLOCK), 1)
    spread = jnp.where(row == (column // INST_BLOCK) ^ (half * clusters), 0.5, 0.0).astype(BF16)
    biases = lax.dot_general(bias_raw[...], spread, (((0,), (0,)), ((), ())), preferred_element_type=F32)
    first_cluster = lax.axis_index("label") * 2 * clusters
    for k in range(2):
        for c in range(clusters):
            i = k * clusters + c
            bias_full[k, c] = biases[:, i * INST_BLOCK : (i + 1) * INST_BLOCK]
            held = jnp.where(beam[...] == first_cluster + (i ^ (half * clusters)), 0.5 * SCALE, 0.0)
            held = jnp.broadcast_to(jnp.max(held, axis=1, keepdims=True), (2 * BLOCKS, INST_BLOCK))
            mask[k, c] = jnp.where(low, held[:BLOCKS], held[BLOCKS:]).astype(BF16)
    for copy in (w_copies[0], *e_copies[0]):
        copy.wait()

    def before(k, t, h):
        if (k, h) == (1, 0):
            w_copies[1].wait()
            for copy in (*e_copies[1], *e_copies[2], *e_copies[3]):
                copy.start()

    def emit(k, t, c, part):
        out = own_slopes_t if k else first_slopes_t
        out[c * CLUSTER : (c + 1) * CLUSTER] = part
        slopes[:, (k * clusters + c) * CLUSTER : (k * clusters + c + 1) * CLUSTER] = part.T

    jobs = [(k, 0, h) for k in range(2) for h in range(half_rows // CHUNK)]
    slope_chunks(jobs, scores, w, embed, bias_full, mask, word, before, emit)
    for t in range(1, tiles):
        set_positives(t)
    store_rows([row_out], slopes, w)
    for copy in (*e_copies[1], *e_copies[2], *e_copies[3]):
        copy.wait()


def label_kernel(embed, w, pos, mask, bias_full, one_slopes_t, word, slopes_t, label_out, scores):
    half_rows = label_out.shape[0]
    tiles = embed.shape[0] // TILE
    set_words(range(1, tiles), pos, word)

    def emit(k, t, c, part):
        slopes_t[c * CLUSTER : (c + 1) * CLUSTER, (t - 1) * TILE : t * TILE] = part
        if t == tiles - 1 and (c + 1) % (CHUNK // CLUSTER) == 0:
            rows = slice((c + 1) * CLUSTER - CHUNK, (c + 1) * CLUSTER)
            label_out[rows] = (
                jnp.dot(one_slopes_t[rows], embed[:TILE], preferred_element_type=F32)
                + jnp.dot(slopes_t[rows], embed[TILE:], preferred_element_type=F32)
            ).astype(BF16)

    jobs = [(0, t, h) for t in range(1, tiles) for h in range(half_rows // CHUNK)]
    slope_chunks(jobs, scores, w, embed, bias_full, mask, word, lambda *job: None, emit)


def store_rows(outs, slopes, w):
    sums = jnp.dot(slopes[...], w[...], preferred_element_type=F32).astype(BF16)
    count = TILE // len(outs)
    for i, out in enumerate(outs):
        out[...] = sums[i * count : (i + 1) * count].reshape(out.shape)


def row_tile(t, outs, embed, w, word, mask, bias_full, first_slopes_t, own_slopes_t, scores, slopes):
    half_rows = w.shape[0] // 2

    def emit(k, t, c, part):
        if c == 0:
            slopes[:, :half_rows] = first_slopes_t[:, (t - 1) * TILE : t * TILE].T
        own_slopes_t[c * CLUSTER : (c + 1) * CLUSTER] = part
        slopes[:, half_rows + c * CLUSTER : half_rows + (c + 1) * CLUSTER] = part.T

    jobs = [(1, t, h) for h in range(half_rows // CHUNK)]
    slope_chunks(jobs, scores, w, embed, bias_full, mask, word, lambda *job: None, emit)
    store_rows(outs, slopes, w)


def keep_rows_kernel(embed, w, word, mask, bias_full, first_slopes_t, own_slopes_t, row_out, scores, slopes):
    row_tile(1, [row_out], embed, w, word, mask, bias_full, first_slopes_t, own_slopes_t, scores, slopes)


def last_rows_kernel(embed, w, word, mask, bias_full, first_slopes_t, *rest):
    *outs, three_slopes_t, four_slopes_t, scores, slopes = rest
    shared = (embed, w, word, mask, bias_full, first_slopes_t)
    row_tile(2, outs[:-1], *shared, three_slopes_t, scores.at[0], slopes.at[0])
    row_tile(3, outs[-1:], *shared, four_slopes_t, scores.at[1], slopes.at[1])


def keep_kernel(embed, *refs):
    *slopes_t, label_out = refs
    total = 0.0
    for t, part in enumerate(slopes_t):
        total = total + jnp.dot(part[...], embed[t * TILE : (t + 1) * TILE], preferred_element_type=F32)
    label_out[...] = total.astype(BF16)


def sum_kernel(places, *refs):
    *terms, out = refs
    out[...] = add(*(term[at] for term, at in zip(terms, places)))


def half_sum_kernel(kept, got, out):
    out[...] = add(kept[: out.shape[0]], got[: out.shape[0]])


def finish_kernel(kept, got, summed, *refs):
    *row_terms, row_out, label_out, row, rest, sems = refs
    first = summed.shape[0]
    copies = [
        pltpu.make_async_copy(row, row_out, sems.at[0]),
        pltpu.make_async_copy(summed, label_out.at[pl.ds(0, first)], sems.at[1]),
        pltpu.make_async_copy(rest, label_out.at[pl.ds(first, rest.shape[0])], sems.at[2]),
    ]
    copies[1].start()
    row[...] = add(*(term[(0,) * (len(term.shape) - 2)] for term in row_terms))
    copies[0].start()
    rest[...] = add(kept[first:], got[first:])
    copies[2].start()
    for copy in copies:
        copy.wait()


def swapped(value, axis, size, bit):
    return lax.ppermute(value, axis, [(i, i ^ bit) for i in range(size)])


def add(*terms):
    total = terms[0].astype(F32)
    for term in terms[1:]:
        total = total + term.astype(F32)
    return total.astype(BF16)


def on_device(n_dp, n_label, embed, weight, bias, beam, positives):
    rows, features = embed.shape
    labels = weight.shape[0]
    half_rows = labels // 2
    clusters = half_rows // CLUSTER
    piece = rows // n_label
    subs = n_label // 2 // BLOCKS
    bias_rows = bias.reshape(labels // CLUSTER, CLUSTER)
    pos_rows = positives.T
    vmem = pl.BlockSpec(memory_space=pltpu.VMEM)
    hbm = pl.BlockSpec(memory_space=pltpu.HBM)
    params = pltpu.CompilerParams(vmem_limit_bytes=VMEM_LIMIT)
    shape = jax.ShapeDtypeStruct
    tile_shape = shape((half_rows, TILE), BF16)
    row_shape = shape((BLOCKS // 2, subs, piece, features), BF16)
    score_scratch = pltpu.VMEM((2, CHUNK, TILE), F32)
    slope_scratch = pltpu.VMEM((TILE, labels), BF16)

    def cost(halves):
        return pl.CostEstimate(flops=halves * 2 * rows * half_rows * features, bytes_accessed=0, transcendentals=0)

    *common, head_slopes_t, one_slopes_t, first_send = pl.pallas_call(
        functools.partial(first_kernel, n_label),
        out_shape=[
            shape((rows, features), BF16),
            shape((labels, features), BF16),
            shape(pos_rows.shape, jnp.int32),
            shape((2, clusters, BLOCKS, INST_BLOCK), BF16),
            shape((2, clusters, CLUSTER, INST_BLOCK), F32),
            tile_shape,
            tile_shape,
            row_shape,
        ],
        in_specs=[hbm] * 5,
        out_specs=[vmem] * 8,
        scratch_shapes=[
            pltpu.VMEM(bias_rows.shape, BF16),
            pltpu.VMEM(beam.shape, jnp.int32),
            pltpu.VMEM(pos_rows.shape, jnp.int32),
            pltpu.VMEM((2 * BLOCKS, beam.shape[1]), jnp.int32),
            pltpu.VMEM((CLUSTER, TILE), jnp.int16),
            score_scratch,
            slope_scratch,
            pltpu.SemaphoreType.DMA((5 + n_label,)),
        ],
        compiler_params=params,
        cost_estimate=cost(2),
        name="first_rows",
    )(*(pltpu.with_memory_space_constraint(x, pltpu.HBM) for x in (embed, weight, bias_rows, beam, pos_rows)))

    first_got = swapped(first_send, "label", n_label, 1)

    word, first_slopes_t, label_send = pl.pallas_call(
        label_kernel,
        out_shape=[
            shape((CLUSTER, rows), jnp.int16),
            shape((half_rows, rows - TILE), BF16),
            shape((half_rows, features), BF16),
        ],
        in_specs=[vmem] * 6,
        out_specs=[vmem] * 3,
        scratch_shapes=[score_scratch],
        compiler_params=params,
        cost_estimate=cost(0),
        name="send_half",
    )(*common, head_slopes_t)
    embed_own, w, _, mask, bias_full = common
    shared = (embed_own, w, word, mask, bias_full, first_slopes_t)

    label_got = swapped(label_send, "dp", n_dp, n_dp // 2)
    first_got, *shared = lax.optimization_barrier((first_got, *shared))

    two_slopes_t, first_keep = pl.pallas_call(
        keep_rows_kernel,
        out_shape=[tile_shape, row_shape],
        in_specs=[vmem] * 6,
        out_specs=[vmem] * 2,
        scratch_shapes=[score_scratch, slope_scratch],
        compiler_params=params,
        cost_estimate=cost(0),
        name="keep_rows",
    )(*shared)

    axes = [2 * subs, 4 * subs, 8 * subs]

    def summed_at(*terms):
        arrays, places = zip(*terms)
        size = places[0].stop - places[0].start
        return pl.pallas_call(
            functools.partial(sum_kernel, places),
            out_shape=shape((size, subs, piece, features), BF16),
            in_specs=[vmem] * len(arrays),
            out_specs=vmem,
            compiler_params=params,
            cost_estimate=cost(0),
            name="row_sum",
        )(*arrays)

    def passed_on(value, stage):
        bits = (axes[stage], axes[stage if stage == 2 else 1 - stage])
        return lax.ppermute(value, "label", [(i, i ^ bits[i % 2]) for i in range(n_label)])

    far_got = passed_on(summed_at((first_keep, slice(2, 4)), (first_got, slice(2, 4))), 0)
    near_got = passed_on(summed_at((first_keep, slice(0, 2)), (first_got, slice(0, 2))), 0)

    part_shape = shape((2, subs, piece, features), BF16)
    *last_send, last_keep, three_slopes_t, four_slopes_t = pl.pallas_call(
        last_rows_kernel,
        out_shape=[part_shape] * 2 + [row_shape, tile_shape, tile_shape],
        in_specs=[vmem] * 6,
        out_specs=[vmem] * 5,
        scratch_shapes=[
            pltpu.VMEM((2, 2, CHUNK, TILE), F32),
            pltpu.VMEM((2, TILE, labels), BF16),
        ],
        compiler_params=params,
        cost_estimate=cost(2),
        name="last_rows",
    )(*shared)

    last_got = [swapped(part, "label", n_label, 1) for part in last_send]
    three_got = passed_on(summed_at((last_keep, slice(3, 4)), (last_got[1], slice(1, 2)), (far_got, slice(1, 2))), 1)
    two_got = passed_on(summed_at((last_keep, slice(2, 3)), (last_got[1], slice(0, 1)), (far_got, slice(0, 1))), 1)
    row_got = passed_on(summed_at((last_keep, slice(1, 2)), (last_got[0], slice(1, 2)), (near_got, slice(1, 2)), (three_got, slice(0, 1))), 2)
    row_terms = [last_keep, last_got[0], near_got, two_got, row_got]
    bit = subs
    while bit > 1:
        row_sum = add(*(term.reshape(-1, subs, piece, features)[0] for term in row_terms[:-1]))
        held = row_sum.shape[0] // 2
        came = row_terms[-1].reshape(subs, piece, features)
        incoming = swapped(add(row_sum[held:], came[held:]), "label", n_label, bit)
        row_terms = [add(row_sum[:held], came[:held]), incoming]
        subs = held
        bit //= 2

    label_keep = pl.pallas_call(
        keep_kernel,
        out_shape=shape((half_rows, features), BF16),
        in_specs=[vmem] * 5,
        out_specs=vmem,
        compiler_params=params,
        cost_estimate=cost(0),
        name="keep_half",
    )(embed_own, one_slopes_t, two_slopes_t, three_slopes_t, four_slopes_t)

    kept, got = label_keep, label_got
    step = n_dp // 4
    at = lax.axis_index("dp")
    while step >= 1:
        label_sum = add(kept, got)
        size = label_sum.shape[0] // 2
        mine = (at // step) % 2
        outgoing = lax.dynamic_slice_in_dim(label_sum, (1 - mine) * size, size, 0)
        kept = lax.dynamic_slice_in_dim(label_sum, mine * size, size, 0)
        got = swapped(outgoing, "dp", n_dp, step)
        step //= 2

    size = kept.shape[0]
    summed = pl.pallas_call(
        half_sum_kernel,
        out_shape=shape((size // 2, features), BF16),
        in_specs=[vmem] * 2,
        out_specs=vmem,
        compiler_params=params,
        cost_estimate=cost(2),
        name="half_sum",
    )(kept, got)
    return pl.pallas_call(
        finish_kernel,
        out_shape=[shape((piece, features), BF16), shape((size, features), BF16)],
        in_specs=[vmem] * (3 + len(row_terms)),
        out_specs=[hbm] * 2,
        scratch_shapes=[
            pltpu.VMEM((piece, features), BF16),
            pltpu.VMEM((size // 2, features), BF16),
            pltpu.SemaphoreType.DMA((3,)),
        ],
        compiler_params=params,
        cost_estimate=cost(0),
        name="finish",
    )(kept, got, summed, *row_terms)


def solution(mesh):
    in_specs = (P("dp", None), P("label", None), P("label"), P("dp", None), P("dp", None))
    out_specs = (P(("dp", "label"), None), P(("label", "dp"), None))
    body = functools.partial(on_device, mesh.shape["dp"], mesh.shape["label"])
    return jax.shard_map(body, mesh=mesh, in_specs=in_specs, out_specs=out_specs, check_vma=False)
```

```python
import functools

import jax
import jax.numpy as jnp
from jax import lax
from jax.experimental import pallas as pl
from jax.experimental.pallas import tpu as pltpu
from jax.sharding import PartitionSpec as P

INST_BLOCK = 128
CLUSTER = 128
TILE = 256
CHUNK = 256
CLUSTERS = 8
BLOCKS = 8
SCALE = 0.125

F32 = jnp.float32
BF16 = jnp.bfloat16
VMEM_LIMIT = 32 * 1024 * 1024


def half_index():
    return lax.axis_index("dp") // (lax.axis_size("dp") // 2)


def place(n_label):
    subs = n_label // 2 // BLOCKS
    pair = lax.axis_index("label") // 2
    return pair // subs, pair % subs, lax.axis_index("label") % 2


def slope_chunks(jobs, scores, w, embed, bias_ref, mask_ref, word_ref, before, emit):
    half_rows = w.shape[0] // 2
    clusters = half_rows // CLUSTER

    def score(n):
        k, t, h = jobs[n]
        before(k, t, h)
        first = k * half_rows + h * CHUNK
        scores[n % 2] = lax.dot_general(
            w[first : first + CHUNK],
            embed[t * TILE : (t + 1) * TILE],
            (((1,), (1,)), ((), ())),
            preferred_element_type=F32,
        )

    score(0)
    for n, (k, t, h) in enumerate(jobs):
        if n + 1 < len(jobs):
            score(n + 1)
        for i in range(CHUNK // CLUSTER):
            c = h * (CHUNK // CLUSTER) + i
            hit = (word_ref[:, t * TILE : (t + 1) * TILE] & jnp.int16(1 << (k * clusters + c))) != 0
            sign = jnp.where(hit, jnp.bfloat16(-1), jnp.bfloat16(1)).astype(F32)
            groups = []
            for g in range(TILE // INST_BLOCK):
                lanes = slice(g * INST_BLOCK, (g + 1) * INST_BLOCK)
                z = scores[n % 2, i * CLUSTER : (i + 1) * CLUSTER, lanes] * 0.5 + bias_ref[k, c]
                group = t * (TILE // INST_BLOCK) + g
                groups.append((jnp.tanh(z) + sign[:, lanes]).astype(BF16) * mask_ref[k, c, group : group + 1])
            emit(k, t, c, jnp.concatenate(groups, axis=1))


def block_in(t, i, over, core):
    first, second, third = 1 - t // 2, i // 2, i % 2
    owner = core if t % 2 else 1 - core
    return (first + 2 * second + 4 * third + owner * (first + 2 * second - 3 * third)) ^ over


def set_words(tiles, pos_ref, word):
    half_rows = CLUSTER * CLUSTERS // 2
    first_label = lax.axis_index("label") * 2 * half_rows
    send_half = 1 - half_index()
    label_no = lax.broadcasted_iota(jnp.int32, (CLUSTER, TILE), 0).astype(jnp.int16)
    for t in tiles:
        lanes = slice(t * TILE, (t + 1) * TILE)
        local = pos_ref[:, lanes] - first_label
        inside = (local >= 0) & (local < 2 * half_rows)
        bits = jnp.where(inside, jnp.left_shift(1, ((local >> 7) ^ (send_half * (CLUSTERS // 2))) & 15), 0).astype(jnp.int16)
        at = (local & (CLUSTER - 1)).astype(jnp.int16)
        found = jnp.zeros((CLUSTER, TILE), jnp.int16)
        for p in range(pos_ref.shape[0]):
            found = found | jnp.where(
                label_no == jnp.broadcast_to(at[p : p + 1], found.shape),
                jnp.broadcast_to(bits[p : p + 1], found.shape),
                jnp.int16(0),
            )
        word[:, lanes] = found


def first_kernel(n_label, embed_hbm, weight_hbm, bias_hbm, beam_hbm, pos_hbm, embed, w, pos, mask, bias_full,
                 first_slopes_t, own_slopes_t, row_out, bias_raw, beam_raw, pos_raw, beam, word, scores, slopes, sems):
    half_rows = own_slopes_t.shape[0]
    clusters = half_rows // CLUSTER
    tiles = embed.shape[0] // TILE
    half = 1 - half_index()
    over, within, core = place(n_label)
    piece = embed.shape[0] // n_label
    subs = INST_BLOCK // piece // 2
    small = [
        pltpu.make_async_copy(source, target, sems.at[k])
        for k, (source, target) in enumerate(((beam_hbm, beam_raw), (bias_hbm, bias_raw), (pos_hbm, pos_raw)))
    ]
    w_copies = [
        pltpu.make_async_copy(
            weight_hbm.at[pl.ds(pl.multiple_of(which * half_rows, half_rows), half_rows)],
            w.at[pl.ds(k * half_rows, half_rows)],
            sems.at[3 + k],
        )
        for k, which in enumerate((half, 1 - half))
    ]
    e_copies = []
    for t in range(tiles):
        e_copies.append([])
        for i in range(4):
            for j in range(subs):
                at = t * (TILE // piece) + len(e_copies[t])
                row = block_in(t, i, over, core) * INST_BLOCK
                row = row + (2 * (j ^ within if subs > 1 else 0) + (core if t % 2 else 1 - core)) * piece
                e_copies[t].append(
                    pltpu.make_async_copy(
                        embed_hbm.at[pl.ds(pl.multiple_of(row, piece), piece)],
                        embed.at[pl.ds(at * piece, piece)],
                        sems.at[5 + at],
                    )
                )
    for copy in (*small, *e_copies[0], *w_copies):
        copy.start()
    for copy in small:
        copy.wait()
    for copy in (*e_copies[1], *e_copies[2], *e_copies[3]):
        copy.start()

    lane = lax.broadcasted_iota(jnp.int32, (BLOCKS, INST_BLOCK), 1)
    low = lane < INST_BLOCK // 2

    def relative_lanes(x):
        code = 2 * within + core
        for k in range((2 * subs).bit_length() - 1):
            shift = piece << k
            turned = jnp.where(
                (lane & shift) != 0, pltpu.roll(x, shift, 1), pltpu.roll(x, INST_BLOCK - shift, 1)
            )
            x = jnp.where((code >> k) % 2 == 1, turned, x)
        if subs > 1:
            x = jnp.concatenate(
                [x[:, (2 * j + c) * piece : (2 * j + c + 1) * piece] for c in range(2) for j in range(subs)], axis=1
            )
        return x

    def set_positives(t):
        for g in range(TILE // INST_BLOCK):
            one, two = (
                relative_lanes(
                    pos_raw[:, pl.ds(pl.multiple_of(block_in(t, 2 * g + h, over, core) * INST_BLOCK, INST_BLOCK), INST_BLOCK)]
                )
                for h in range(2)
            )
            group = t * (TILE // INST_BLOCK) + g
            pos[:, group * INST_BLOCK : (group + 1) * INST_BLOCK] = (
                jnp.where(low, one, pltpu.roll(two, INST_BLOCK // 2, 1))
                if t % 2
                else jnp.where(low, pltpu.roll(one, INST_BLOCK // 2, 1), two)
            )

    for t in range(tiles):
        for i in range(4):
            group = 8 * (i % 2) + t * 2 + i // 2
            beam[group : group + 1] = beam_raw[pl.ds(block_in(t, i, over, core), 1)]
    for t in range(tiles):
        set_positives(t)
    set_words([0], pos, word)

    row = lax.broadcasted_iota(jnp.int32, (2 * clusters, 2 * clusters * INST_BLOCK), 0)
    column = lax.broadcasted_iota(jnp.int32, (2 * clusters, 2 * clusters * INST_BLOCK), 1)
    spread = jnp.where(row == (column // INST_BLOCK) ^ (half * clusters), 0.5, 0.0).astype(BF16)
    biases = lax.dot_general(bias_raw[...], spread, (((0,), (0,)), ((), ())), preferred_element_type=F32)
    first_cluster = lax.axis_index("label") * 2 * clusters
    for k in range(2):
        for c in range(clusters):
            i = k * clusters + c
            bias_full[k, c] = biases[:, i * INST_BLOCK : (i + 1) * INST_BLOCK]
            held = jnp.where(beam[...] == first_cluster + (i ^ (half * clusters)), 0.5 * SCALE, 0.0)
            held = jnp.broadcast_to(jnp.max(held, axis=1, keepdims=True), (2 * BLOCKS, INST_BLOCK))
            mask[k, c] = jnp.where(low, held[:BLOCKS], held[BLOCKS:]).astype(BF16)
    for copy in (w_copies[0], *e_copies[0]):
        copy.wait()

    def before(k, t, h):
        if (k, h) == (1, 0):
            w_copies[1].wait()

    def emit(k, t, c, part):
        out = own_slopes_t if k else first_slopes_t
        out[c * CLUSTER : (c + 1) * CLUSTER] = part
        slopes[:, (k * clusters + c) * CLUSTER : (k * clusters + c + 1) * CLUSTER] = part.T

    jobs = [(k, 0, h) for k in range(2) for h in range(half_rows // CHUNK)]
    slope_chunks(jobs, scores, w, embed, bias_full, mask, word, before, emit)
    store_rows([row_out], slopes, w)
    for copy in (*e_copies[1], *e_copies[2], *e_copies[3]):
        copy.wait()


def label_kernel(embed, w, pos, mask, bias_full, one_slopes_t, word, slopes_t, label_out, scores):
    half_rows = label_out.shape[0]
    tiles = embed.shape[0] // TILE
    set_words(range(1, tiles), pos, word)

    def emit(k, t, c, part):
        slopes_t[c * CLUSTER : (c + 1) * CLUSTER, (t - 1) * TILE : t * TILE] = part
        if t == tiles - 1 and (c + 1) % (CHUNK // CLUSTER) == 0:
            rows = slice((c + 1) * CLUSTER - CHUNK, (c + 1) * CLUSTER)
            label_out[rows] = (
                jnp.dot(one_slopes_t[rows], embed[:TILE], preferred_element_type=F32)
                + jnp.dot(slopes_t[rows], embed[TILE:], preferred_element_type=F32)
            ).astype(BF16)

    jobs = [(0, t, h) for t in range(1, tiles) for h in range(half_rows // CHUNK)]
    slope_chunks(jobs, scores, w, embed, bias_full, mask, word, lambda *job: None, emit)


def store_rows(outs, slopes, w):
    sums = jnp.dot(slopes[...], w[...], preferred_element_type=F32).astype(BF16)
    count = TILE // len(outs)
    for i, out in enumerate(outs):
        out[...] = sums[i * count : (i + 1) * count].reshape(out.shape)


def row_tile(t, outs, embed, w, word, mask, bias_full, first_slopes_t, own_slopes_t, scores, slopes):
    half_rows = w.shape[0] // 2

    def emit(k, t, c, part):
        if c == 0:
            slopes[:, :half_rows] = first_slopes_t[:, (t - 1) * TILE : t * TILE].T
        own_slopes_t[c * CLUSTER : (c + 1) * CLUSTER] = part
        slopes[:, half_rows + c * CLUSTER : half_rows + (c + 1) * CLUSTER] = part.T

    jobs = [(1, t, h) for h in range(half_rows // CHUNK)]
    slope_chunks(jobs, scores, w, embed, bias_full, mask, word, lambda *job: None, emit)
    store_rows(outs, slopes, w)


def keep_rows_kernel(embed, w, word, mask, bias_full, first_slopes_t, own_slopes_t, row_out, scores, slopes):
    row_tile(1, [row_out], embed, w, word, mask, bias_full, first_slopes_t, own_slopes_t, scores, slopes)


def last_rows_kernel(embed, w, word, mask, bias_full, first_slopes_t, *rest):
    *outs, three_slopes_t, four_slopes_t, scores, slopes = rest
    shared = (embed, w, word, mask, bias_full, first_slopes_t)
    row_tile(2, outs[:-1], *shared, three_slopes_t, scores.at[0], slopes.at[0])
    row_tile(3, outs[-1:], *shared, four_slopes_t, scores.at[1], slopes.at[1])


def keep_kernel(embed, *refs):
    *slopes_t, label_out = refs
    total = 0.0
    for t, part in enumerate(slopes_t):
        total = total + jnp.dot(part[...], embed[t * TILE : (t + 1) * TILE], preferred_element_type=F32)
    label_out[...] = total.astype(BF16)


def sum_kernel(places, *refs):
    *terms, out = refs
    out[...] = add(*(term[at] for term, at in zip(terms, places)))


def half_sum_kernel(kept, got, out):
    out[...] = add(kept[: out.shape[0]], got[: out.shape[0]])


def finish_kernel(kept, got, summed, *refs):
    *row_terms, row_out, label_out, row, rest, sems = refs
    first = summed.shape[0]
    copies = [
        pltpu.make_async_copy(row, row_out, sems.at[0]),
        pltpu.make_async_copy(summed, label_out.at[pl.ds(0, first)], sems.at[1]),
        pltpu.make_async_copy(rest, label_out.at[pl.ds(first, rest.shape[0])], sems.at[2]),
    ]
    copies[1].start()
    row[...] = add(*(term[(0,) * (len(term.shape) - 2)] for term in row_terms))
    copies[0].start()
    rest[...] = add(kept[first:], got[first:])
    copies[2].start()
    for copy in copies:
        copy.wait()


def swapped(value, axis, size, bit):
    return lax.ppermute(value, axis, [(i, i ^ bit) for i in range(size)])


def add(*terms):
    total = terms[0].astype(F32)
    for term in terms[1:]:
        total = total + term.astype(F32)
    return total.astype(BF16)


def on_device(n_dp, n_label, embed, weight, bias, beam, positives):
    rows, features = embed.shape
    labels = weight.shape[0]
    half_rows = labels // 2
    clusters = half_rows // CLUSTER
    piece = rows // n_label
    subs = n_label // 2 // BLOCKS
    bias_rows = bias.reshape(labels // CLUSTER, CLUSTER)
    pos_rows = positives.T
    vmem = pl.BlockSpec(memory_space=pltpu.VMEM)
    hbm = pl.BlockSpec(memory_space=pltpu.HBM)
    params = pltpu.CompilerParams(vmem_limit_bytes=VMEM_LIMIT)
    shape = jax.ShapeDtypeStruct
    tile_shape = shape((half_rows, TILE), BF16)
    row_shape = shape((BLOCKS // 2, subs, piece, features), BF16)
    score_scratch = pltpu.VMEM((2, CHUNK, TILE), F32)
    slope_scratch = pltpu.VMEM((TILE, labels), BF16)

    def cost(halves):
        return pl.CostEstimate(flops=halves * 2 * rows * half_rows * features, bytes_accessed=0, transcendentals=0)

    *common, head_slopes_t, one_slopes_t, first_send = pl.pallas_call(
        functools.partial(first_kernel, n_label),
        out_shape=[
            shape((rows, features), BF16),
            shape((labels, features), BF16),
            shape(pos_rows.shape, jnp.int32),
            shape((2, clusters, BLOCKS, INST_BLOCK), BF16),
            shape((2, clusters, CLUSTER, INST_BLOCK), F32),
            tile_shape,
            tile_shape,
            row_shape,
        ],
        in_specs=[hbm] * 5,
        out_specs=[vmem] * 8,
        scratch_shapes=[
            pltpu.VMEM(bias_rows.shape, BF16),
            pltpu.VMEM(beam.shape, jnp.int32),
            pltpu.VMEM(pos_rows.shape, jnp.int32),
            pltpu.VMEM((2 * BLOCKS, beam.shape[1]), jnp.int32),
            pltpu.VMEM((CLUSTER, TILE), jnp.int16),
            score_scratch,
            slope_scratch,
            pltpu.SemaphoreType.DMA((5 + n_label,)),
        ],
        compiler_params=params,
        cost_estimate=cost(2),
        name="first_rows",
    )(*(pltpu.with_memory_space_constraint(x, pltpu.HBM) for x in (embed, weight, bias_rows, beam, pos_rows)))

    first_got = swapped(first_send, "label", n_label, 1)

    word, first_slopes_t, label_send = pl.pallas_call(
        label_kernel,
        out_shape=[
            shape((CLUSTER, rows), jnp.int16),
            shape((half_rows, rows - TILE), BF16),
            shape((half_rows, features), BF16),
        ],
        in_specs=[vmem] * 6,
        out_specs=[vmem] * 3,
        scratch_shapes=[score_scratch],
        compiler_params=params,
        cost_estimate=cost(0),
        name="send_half",
    )(*common, head_slopes_t)
    embed_own, w, _, mask, bias_full = common
    shared = (embed_own, w, word, mask, bias_full, first_slopes_t)

    label_got = swapped(label_send, "dp", n_dp, n_dp // 2)
    first_got, *shared = lax.optimization_barrier((first_got, *shared))

    two_slopes_t, first_keep = pl.pallas_call(
        keep_rows_kernel,
        out_shape=[tile_shape, row_shape],
        in_specs=[vmem] * 6,
        out_specs=[vmem] * 2,
        scratch_shapes=[score_scratch, slope_scratch],
        compiler_params=params,
        cost_estimate=cost(0),
        name="keep_rows",
    )(*shared)

    axes = [2 * subs, 4 * subs, 8 * subs]

    def summed_at(*terms):
        arrays, places = zip(*terms)
        size = places[0].stop - places[0].start
        return pl.pallas_call(
            functools.partial(sum_kernel, places),
            out_shape=shape((size, subs, piece, features), BF16),
            in_specs=[vmem] * len(arrays),
            out_specs=vmem,
            compiler_params=params,
            cost_estimate=cost(0),
            name="row_sum",
        )(*arrays)

    def passed_on(value, stage):
        bits = (axes[stage], axes[(stage + 1) % 3])
        return lax.ppermute(value, "label", [(i, i ^ bits[i % 2]) for i in range(n_label)])

    far_got = passed_on(summed_at((first_keep, slice(2, 4)), (first_got, slice(2, 4))), 0)
    near_got = passed_on(summed_at((first_keep, slice(0, 2)), (first_got, slice(0, 2))), 0)

    part_shape = shape((2, subs, piece, features), BF16)
    *last_send, last_keep, three_slopes_t, four_slopes_t = pl.pallas_call(
        last_rows_kernel,
        out_shape=[part_shape] * 2 + [row_shape, tile_shape, tile_shape],
        in_specs=[vmem] * 6,
        out_specs=[vmem] * 5,
        scratch_shapes=[
            pltpu.VMEM((2, 2, CHUNK, TILE), F32),
            pltpu.VMEM((2, TILE, labels), BF16),
        ],
        compiler_params=params,
        cost_estimate=cost(2),
        name="last_rows",
    )(*shared)

    last_got = [swapped(part, "label", n_label, 1) for part in last_send]
    three_got = passed_on(summed_at((last_keep, slice(3, 4)), (last_got[1], slice(1, 2)), (far_got, slice(1, 2))), 1)
    two_got = passed_on(summed_at((last_keep, slice(2, 3)), (last_got[1], slice(0, 1)), (far_got, slice(0, 1))), 1)
    row_got = passed_on(summed_at((last_keep, slice(1, 2)), (last_got[0], slice(1, 2)), (near_got, slice(1, 2)), (three_got, slice(0, 1))), 2)
    row_terms = [last_keep, last_got[0], near_got, two_got, row_got]
    bit = subs
    while bit > 1:
        row_sum = add(*(term.reshape(-1, subs, piece, features)[0] for term in row_terms[:-1]))
        held = row_sum.shape[0] // 2
        came = row_terms[-1].reshape(subs, piece, features)
        incoming = swapped(add(row_sum[held:], came[held:]), "label", n_label, bit)
        row_terms = [add(row_sum[:held], came[:held]), incoming]
        subs = held
        bit //= 2

    label_keep = pl.pallas_call(
        keep_kernel,
        out_shape=shape((half_rows, features), BF16),
        in_specs=[vmem] * 5,
        out_specs=vmem,
        compiler_params=params,
        cost_estimate=cost(0),
        name="keep_half",
    )(embed_own, one_slopes_t, two_slopes_t, three_slopes_t, four_slopes_t)

    kept, got = label_keep, label_got
    step = n_dp // 4
    at = lax.axis_index("dp")
    while step >= 1:
        label_sum = add(kept, got)
        size = label_sum.shape[0] // 2
        mine = (at // step) % 2
        outgoing = lax.dynamic_slice_in_dim(label_sum, (1 - mine) * size, size, 0)
        kept = lax.dynamic_slice_in_dim(label_sum, mine * size, size, 0)
        got = swapped(outgoing, "dp", n_dp, step)
        step //= 2

    size = kept.shape[0]
    summed = pl.pallas_call(
        half_sum_kernel,
        out_shape=shape((size // 2, features), BF16),
        in_specs=[vmem] * 2,
        out_specs=vmem,
        compiler_params=params,
        cost_estimate=cost(2),
        name="half_sum",
    )(kept, got)
    return pl.pallas_call(
        finish_kernel,
        out_shape=[shape((piece, features), BF16), shape((size, features), BF16)],
        in_specs=[vmem] * (3 + len(row_terms)),
        out_specs=[hbm] * 2,
        scratch_shapes=[
            pltpu.VMEM((piece, features), BF16),
            pltpu.VMEM((size // 2, features), BF16),
            pltpu.SemaphoreType.DMA((3,)),
        ],
        compiler_params=params,
        cost_estimate=cost(0),
        name="finish",
    )(kept, got, summed, *row_terms)


def solution(mesh):
    in_specs = (P("dp", None), P("label", None), P("label"), P("dp", None), P("dp", None))
    out_specs = (P(("dp", "label"), None), P(("label", "dp"), None))
    body = functools.partial(on_device, mesh.shape["dp"], mesh.shape["label"])
    return jax.shard_map(body, mesh=mesh, in_specs=in_specs, out_specs=out_specs, check_vma=False)
```

```python
import functools

import jax
import jax.numpy as jnp
from jax import lax
from jax.experimental import pallas as pl
from jax.experimental.pallas import tpu as pltpu
from jax.sharding import PartitionSpec as P

INST_BLOCK = 128
CLUSTER = 128
TILE = 256
CHUNK = 256
CLUSTERS = 8
BLOCKS = 8
SCALE = 0.125

F32 = jnp.float32
BF16 = jnp.bfloat16
VMEM_LIMIT = 32 * 1024 * 1024


def half_index():
    return lax.axis_index("dp") // (lax.axis_size("dp") // 2)


def place(n_label):
    subs = n_label // 2 // BLOCKS
    pair = lax.axis_index("label") // 2
    return pair // subs, pair % subs, lax.axis_index("label") % 2


def slope_chunks(jobs, scores, w, embed, bias_ref, mask_ref, word_ref, before, emit):
    half_rows = w.shape[0] // 2
    clusters = half_rows // CLUSTER

    def score(n):
        k, t, h = jobs[n]
        before(k, t, h)
        first = k * half_rows + h * CHUNK
        scores[n % 2] = lax.dot_general(
            w[first : first + CHUNK],
            embed[t * TILE : (t + 1) * TILE],
            (((1,), (1,)), ((), ())),
            preferred_element_type=F32,
        )

    score(0)
    for n, (k, t, h) in enumerate(jobs):
        if n + 1 < len(jobs):
            score(n + 1)
        for i in range(CHUNK // CLUSTER):
            c = h * (CHUNK // CLUSTER) + i
            hit = (word_ref[:, t * TILE : (t + 1) * TILE] & jnp.int16(1 << (k * clusters + c))) != 0
            sign = jnp.where(hit, jnp.bfloat16(-1), jnp.bfloat16(1)).astype(F32)
            groups = []
            for g in range(TILE // INST_BLOCK):
                lanes = slice(g * INST_BLOCK, (g + 1) * INST_BLOCK)
                z = scores[n % 2, i * CLUSTER : (i + 1) * CLUSTER, lanes] * 0.5 + bias_ref[k, c]
                group = t * (TILE // INST_BLOCK) + g
                groups.append((jnp.tanh(z) + sign[:, lanes]).astype(BF16) * mask_ref[k, c, group : group + 1])
            emit(k, t, c, jnp.concatenate(groups, axis=1))


def block_in(t, i, over, core):
    first, second, third = 1 - t // 2, i // 2, i % 2
    owner = core if t % 2 else 1 - core
    return (first + 2 * second + 4 * third + owner * (first + 2 * second - 3 * third)) ^ over


def set_words(tiles, pos_ref, word):
    half_rows = CLUSTER * CLUSTERS // 2
    first_label = lax.axis_index("label") * 2 * half_rows
    send_half = 1 - half_index()
    label_no = lax.broadcasted_iota(jnp.int32, (CLUSTER, TILE), 0).astype(jnp.int16)
    for t in tiles:
        lanes = slice(t * TILE, (t + 1) * TILE)
        local = pos_ref[:, lanes] - first_label
        inside = (local >= 0) & (local < 2 * half_rows)
        bits = jnp.where(inside, jnp.left_shift(1, ((local >> 7) ^ (send_half * (CLUSTERS // 2))) & 15), 0).astype(jnp.int16)
        at = (local & (CLUSTER - 1)).astype(jnp.int16)
        found = jnp.zeros((CLUSTER, TILE), jnp.int16)
        for p in range(pos_ref.shape[0]):
            found = found | jnp.where(
                label_no == jnp.broadcast_to(at[p : p + 1], found.shape),
                jnp.broadcast_to(bits[p : p + 1], found.shape),
                jnp.int16(0),
            )
        word[:, lanes] = found


def send_kernel(n_label, embed_hbm, weight_hbm, bias_hbm, beam_hbm, pos_hbm, embed, w, word, mask, bias_full, slopes_t,
                label_out, bias_raw, beam_raw, pos_raw, beam, pos, scores, sems):
    half_rows = label_out.shape[0]
    clusters = half_rows // CLUSTER
    tiles = embed.shape[0] // TILE
    half = 1 - half_index()
    over, within, core = place(n_label)
    piece = embed.shape[0] // n_label
    subs = INST_BLOCK // piece // 2
    small = [
        pltpu.make_async_copy(source, target, sems.at[k])
        for k, (source, target) in enumerate(((beam_hbm, beam_raw), (bias_hbm, bias_raw), (pos_hbm, pos_raw)))
    ]
    w_copies = [
        pltpu.make_async_copy(
            weight_hbm.at[pl.ds(pl.multiple_of(which * half_rows, half_rows), half_rows)],
            w.at[pl.ds(k * half_rows, half_rows)],
            sems.at[3 + k],
        )
        for k, which in enumerate((half, 1 - half))
    ]
    e_copies = []
    for t in range(tiles):
        e_copies.append([])
        for i in range(4):
            for j in range(subs):
                at = t * (TILE // piece) + len(e_copies[t])
                row = block_in(t, i, over, core) * INST_BLOCK
                row = row + (2 * (j ^ within if subs > 1 else 0) + (core if t % 2 else 1 - core)) * piece
                e_copies[t].append(
                    pltpu.make_async_copy(
                        embed_hbm.at[pl.ds(pl.multiple_of(row, piece), piece)],
                        embed.at[pl.ds(at * piece, piece)],
                        sems.at[5 + at],
                    )
                )
    for copy in (*small, *e_copies[0], w_copies[0]):
        copy.start()
    for copy in small:
        copy.wait()
    for copy in (*e_copies[1], *e_copies[2], *e_copies[3]):
        copy.start()

    lane = lax.broadcasted_iota(jnp.int32, (BLOCKS, INST_BLOCK), 1)
    low = lane < INST_BLOCK // 2

    def relative_lanes(x):
        code = 2 * within + core
        for k in range((2 * subs).bit_length() - 1):
            shift = piece << k
            turned = jnp.where(
                (lane & shift) != 0, pltpu.roll(x, shift, 1), pltpu.roll(x, INST_BLOCK - shift, 1)
            )
            x = jnp.where((code >> k) % 2 == 1, turned, x)
        if subs > 1:
            x = jnp.concatenate(
                [x[:, (2 * j + c) * piece : (2 * j + c + 1) * piece] for c in range(2) for j in range(subs)], axis=1
            )
        return x

    def set_positives(t):
        for g in range(TILE // INST_BLOCK):
            one, two = (
                relative_lanes(
                    pos_raw[:, pl.ds(pl.multiple_of(block_in(t, 2 * g + h, over, core) * INST_BLOCK, INST_BLOCK), INST_BLOCK)]
                )
                for h in range(2)
            )
            group = t * (TILE // INST_BLOCK) + g
            pos[:, group * INST_BLOCK : (group + 1) * INST_BLOCK] = (
                jnp.where(low, one, pltpu.roll(two, INST_BLOCK // 2, 1))
                if t % 2
                else jnp.where(low, pltpu.roll(one, INST_BLOCK // 2, 1), two)
            )

    for t in range(tiles):
        for i in range(4):
            group = 8 * (i % 2) + t * 2 + i // 2
            beam[group : group + 1] = beam_raw[pl.ds(block_in(t, i, over, core), 1)]
    for t in range(tiles):
        set_positives(t)
    set_words(range(tiles), pos, word)

    row = lax.broadcasted_iota(jnp.int32, (2 * clusters, 2 * clusters * INST_BLOCK), 0)
    column = lax.broadcasted_iota(jnp.int32, (2 * clusters, 2 * clusters * INST_BLOCK), 1)
    spread = jnp.where(row == (column // INST_BLOCK) ^ (half * clusters), 0.5, 0.0).astype(BF16)
    biases = lax.dot_general(bias_raw[...], spread, (((0,), (0,)), ((), ())), preferred_element_type=F32)
    first_cluster = lax.axis_index("label") * 2 * clusters
    for k in range(2):
        for c in range(clusters):
            i = k * clusters + c
            bias_full[k, c] = biases[:, i * INST_BLOCK : (i + 1) * INST_BLOCK]
            held = jnp.where(beam[...] == first_cluster + (i ^ (half * clusters)), 0.5 * SCALE, 0.0)
            held = jnp.broadcast_to(jnp.max(held, axis=1, keepdims=True), (2 * BLOCKS, INST_BLOCK))
            mask[k, c] = jnp.where(low, held[:BLOCKS], held[BLOCKS:]).astype(BF16)
    w_copies[0].wait()

    def before(k, t, h):
        if h == 0:
            for copy in e_copies[t]:
                copy.wait()
            if t == 1:
                w_copies[1].start()

    def emit(k, t, c, part):
        slopes_t[c * CLUSTER : (c + 1) * CLUSTER, t * TILE : (t + 1) * TILE] = part
        if t == tiles - 1 and (c + 1) % (CHUNK // CLUSTER) == 0:
            rows = slice((c + 1) * CLUSTER - CHUNK, (c + 1) * CLUSTER)
            label_out[rows] = jnp.dot(slopes_t[rows], embed[...], preferred_element_type=F32).astype(BF16)

    jobs = [(0, t, h) for t in range(tiles) for h in range(half_rows // CHUNK)]
    slope_chunks(jobs, scores, w, embed, bias_full, mask, word, before, emit)
    w_copies[1].wait()


def store_rows(outs, slopes, w):
    sums = jnp.dot(slopes[...], w[...], preferred_element_type=F32).astype(BF16)
    count = TILE // len(outs)
    for i, out in enumerate(outs):
        out[...] = sums[i * count : (i + 1) * count].reshape(out.shape)


def row_tile(t, outs, embed, w, word, mask, bias_full, first_slopes_t, own_slopes_t, scores, slopes):
    half_rows = w.shape[0] // 2

    def emit(k, t, c, part):
        if c == 0:
            slopes[:, :half_rows] = first_slopes_t[:, t * TILE : (t + 1) * TILE].T
        own_slopes_t[c * CLUSTER : (c + 1) * CLUSTER] = part
        slopes[:, half_rows + c * CLUSTER : half_rows + (c + 1) * CLUSTER] = part.T

    jobs = [(1, t, h) for h in range(half_rows // CHUNK)]
    slope_chunks(jobs, scores, w, embed, bias_full, mask, word, lambda *job: None, emit)
    store_rows(outs, slopes, w)


def rows_kernel(t, embed, w, word, mask, bias_full, first_slopes_t, own_slopes_t, row_out, scores, slopes):
    row_tile(t, [row_out], embed, w, word, mask, bias_full, first_slopes_t, own_slopes_t, scores, slopes)


def last_rows_kernel(embed, w, word, mask, bias_full, first_slopes_t, *rest):
    *outs, three_slopes_t, four_slopes_t, scores, slopes = rest
    shared = (embed, w, word, mask, bias_full, first_slopes_t)
    row_tile(2, outs[:-1], *shared, three_slopes_t, scores.at[0], slopes.at[0])
    row_tile(3, outs[-1:], *shared, four_slopes_t, scores.at[1], slopes.at[1])


def keep_kernel(embed, *refs):
    *slopes_t, label_out = refs
    total = 0.0
    for t, part in enumerate(slopes_t):
        total = total + jnp.dot(part[...], embed[t * TILE : (t + 1) * TILE], preferred_element_type=F32)
    label_out[...] = total.astype(BF16)


def sum_kernel(places, *refs):
    *terms, out = refs
    out[...] = add(*(term[at] for term, at in zip(terms, places)))


def half_sum_kernel(kept, got, out):
    out[...] = add(kept[: out.shape[0]], got[: out.shape[0]])


def finish_kernel(kept, got, summed, *refs):
    *row_terms, row_out, label_out, row, rest, sems = refs
    first = summed.shape[0]
    copies = [
        pltpu.make_async_copy(row, row_out, sems.at[0]),
        pltpu.make_async_copy(summed, label_out.at[pl.ds(0, first)], sems.at[1]),
        pltpu.make_async_copy(rest, label_out.at[pl.ds(first, rest.shape[0])], sems.at[2]),
    ]
    copies[1].start()
    row[...] = add(*(term[(0,) * (len(term.shape) - 2)] for term in row_terms))
    copies[0].start()
    rest[...] = add(kept[first:], got[first:])
    copies[2].start()
    for copy in copies:
        copy.wait()


def swapped(value, axis, size, bit):
    return lax.ppermute(value, axis, [(i, i ^ bit) for i in range(size)])


def add(*terms):
    total = terms[0].astype(F32)
    for term in terms[1:]:
        total = total + term.astype(F32)
    return total.astype(BF16)


def on_device(n_dp, n_label, embed, weight, bias, beam, positives):
    rows, features = embed.shape
    labels = weight.shape[0]
    half_rows = labels // 2
    clusters = half_rows // CLUSTER
    piece = rows // n_label
    subs = n_label // 2 // BLOCKS
    bias_rows = bias.reshape(labels // CLUSTER, CLUSTER)
    pos_rows = positives.T
    vmem = pl.BlockSpec(memory_space=pltpu.VMEM)
    hbm = pl.BlockSpec(memory_space=pltpu.HBM)
    params = pltpu.CompilerParams(vmem_limit_bytes=VMEM_LIMIT)
    shape = jax.ShapeDtypeStruct
    tile_shape = shape((half_rows, TILE), BF16)
    row_shape = shape((BLOCKS // 2, subs, piece, features), BF16)
    score_scratch = pltpu.VMEM((2, CHUNK, TILE), F32)
    slope_scratch = pltpu.VMEM((TILE, labels), BF16)

    def cost(halves):
        return pl.CostEstimate(flops=halves * 2 * rows * half_rows * features, bytes_accessed=0, transcendentals=0)

    *shared, label_send = pl.pallas_call(
        functools.partial(send_kernel, n_label),
        out_shape=[
            shape((rows, features), BF16),
            shape((labels, features), BF16),
            shape((CLUSTER, rows), jnp.int16),
            shape((2, clusters, BLOCKS, INST_BLOCK), BF16),
            shape((2, clusters, CLUSTER, INST_BLOCK), F32),
            shape((half_rows, rows), BF16),
            shape((half_rows, features), BF16),
        ],
        in_specs=[hbm] * 5,
        out_specs=[vmem] * 7,
        scratch_shapes=[
            pltpu.VMEM(bias_rows.shape, BF16),
            pltpu.VMEM(beam.shape, jnp.int32),
            pltpu.VMEM(pos_rows.shape, jnp.int32),
            pltpu.VMEM((2 * BLOCKS, beam.shape[1]), jnp.int32),
            pltpu.VMEM(pos_rows.shape, jnp.int32),
            score_scratch,
            pltpu.SemaphoreType.DMA((5 + n_label,)),
        ],
        compiler_params=params,
        cost_estimate=cost(2),
        name="send_half",
    )(*(pltpu.with_memory_space_constraint(x, pltpu.HBM) for x in (embed, weight, bias_rows, beam, pos_rows)))
    embed_own = shared[0]

    label_got = swapped(label_send, "dp", n_dp, n_dp // 2)

    def tile_rows(t, name, inputs):
        return pl.pallas_call(
            functools.partial(rows_kernel, t),
            out_shape=[tile_shape, row_shape],
            in_specs=[vmem] * 6,
            out_specs=[vmem] * 2,
            scratch_shapes=[score_scratch, slope_scratch],
            compiler_params=params,
            cost_estimate=cost(0),
            name=name,
        )(*inputs)

    one_slopes_t, first_send = tile_rows(0, "first_rows", shared)
    first_got = swapped(first_send, "label", n_label, 1)
    two_slopes_t, first_keep = tile_rows(1, "keep_rows", shared)
    first_got, *shared = lax.optimization_barrier((first_got, *shared))

    axes = [2 * subs, 4 * subs, 8 * subs]

    def summed_at(*terms):
        arrays, places = zip(*terms)
        size = places[0].stop - places[0].start
        return pl.pallas_call(
            functools.partial(sum_kernel, places),
            out_shape=shape((size, subs, piece, features), BF16),
            in_specs=[vmem] * len(arrays),
            out_specs=vmem,
            compiler_params=params,
            cost_estimate=cost(0),
            name="row_sum",
        )(*arrays)

    def passed_on(value, stage):
        bits = (axes[stage], axes[(stage + 1) % 3])
        return lax.ppermute(value, "label", [(i, i ^ bits[i % 2]) for i in range(n_label)])

    far_got = passed_on(summed_at((first_keep, slice(2, 4)), (first_got, slice(2, 4))), 0)
    near_got = passed_on(summed_at((first_keep, slice(0, 2)), (first_got, slice(0, 2))), 0)

    part_shape = shape((2, subs, piece, features), BF16)
    *last_send, last_keep, three_slopes_t, four_slopes_t = pl.pallas_call(
        last_rows_kernel,
        out_shape=[part_shape] * 2 + [row_shape, tile_shape, tile_shape],
        in_specs=[vmem] * 6,
        out_specs=[vmem] * 5,
        scratch_shapes=[
            pltpu.VMEM((2, 2, CHUNK, TILE), F32),
            pltpu.VMEM((2, TILE, labels), BF16),
        ],
        compiler_params=params,
        cost_estimate=cost(0),
        name="last_rows",
    )(*shared)

    last_got = [swapped(part, "label", n_label, 1) for part in last_send]
    three_got = passed_on(summed_at((last_keep, slice(3, 4)), (last_got[1], slice(1, 2)), (far_got, slice(1, 2))), 1)
    two_got = passed_on(summed_at((last_keep, slice(2, 3)), (last_got[1], slice(0, 1)), (far_got, slice(0, 1))), 1)
    row_got = passed_on(summed_at((last_keep, slice(1, 2)), (last_got[0], slice(1, 2)), (near_got, slice(1, 2)), (three_got, slice(0, 1))), 2)
    row_terms = [last_keep, last_got[0], near_got, two_got, row_got]
    bit = subs
    while bit > 1:
        row_sum = add(*(term.reshape(-1, subs, piece, features)[0] for term in row_terms[:-1]))
        held = row_sum.shape[0] // 2
        came = row_terms[-1].reshape(subs, piece, features)
        incoming = swapped(add(row_sum[held:], came[held:]), "label", n_label, bit)
        row_terms = [add(row_sum[:held], came[:held]), incoming]
        subs = held
        bit //= 2

    label_keep = pl.pallas_call(
        keep_kernel,
        out_shape=shape((half_rows, features), BF16),
        in_specs=[vmem] * 5,
        out_specs=vmem,
        compiler_params=params,
        cost_estimate=cost(0),
        name="keep_half",
    )(embed_own, one_slopes_t, two_slopes_t, three_slopes_t, four_slopes_t)

    kept, got = label_keep, label_got
    step = n_dp // 4
    at = lax.axis_index("dp")
    while step >= 1:
        label_sum = add(kept, got)
        size = label_sum.shape[0] // 2
        mine = (at // step) % 2
        outgoing = lax.dynamic_slice_in_dim(label_sum, (1 - mine) * size, size, 0)
        kept = lax.dynamic_slice_in_dim(label_sum, mine * size, size, 0)
        got = swapped(outgoing, "dp", n_dp, step)
        step //= 2

    size = kept.shape[0]
    summed = pl.pallas_call(
        half_sum_kernel,
        out_shape=shape((size // 2, features), BF16),
        in_specs=[vmem] * 2,
        out_specs=vmem,
        compiler_params=params,
        cost_estimate=cost(2),
        name="half_sum",
    )(kept, got)
    return pl.pallas_call(
        finish_kernel,
        out_shape=[shape((piece, features), BF16), shape((size, features), BF16)],
        in_specs=[vmem] * (3 + len(row_terms)),
        out_specs=[hbm] * 2,
        scratch_shapes=[
            pltpu.VMEM((piece, features), BF16),
            pltpu.VMEM((size // 2, features), BF16),
            pltpu.SemaphoreType.DMA((3,)),
        ],
        compiler_params=params,
        cost_estimate=cost(0),
        name="finish",
    )(kept, got, summed, *row_terms)


def solution(mesh):
    in_specs = (P("dp", None), P("label", None), P("label"), P("dp", None), P("dp", None))
    out_specs = (P(("dp", "label"), None), P(("label", "dp"), None))
    body = functools.partial(on_device, mesh.shape["dp"], mesh.shape["label"])
    return jax.shard_map(body, mesh=mesh, in_specs=in_specs, out_specs=out_specs, check_vma=False)
```

```python
import functools

import jax
import jax.numpy as jnp
from jax import lax
from jax.experimental import pallas as pl
from jax.experimental.pallas import tpu as pltpu
from jax.sharding import PartitionSpec as P

INST_BLOCK = 128
CLUSTER = 128
TILE = 256
CHUNK = 256
CLUSTERS = 8
BLOCKS = 8
SCALE = 0.125

F32 = jnp.float32
BF16 = jnp.bfloat16
VMEM_LIMIT = 32 * 1024 * 1024


def half_index():
    return lax.axis_index("dp") // (lax.axis_size("dp") // 2)


def place(n_label):
    subs = n_label // 2 // BLOCKS
    pair = lax.axis_index("label") // 2
    return pair // subs, pair % subs, lax.axis_index("label") % 2


def slope_chunks(jobs, scores, w, embed, bias_ref, mask_ref, word_ref, before, emit):
    half_rows = w.shape[0] // 2
    clusters = half_rows // CLUSTER

    def score(n):
        k, t, h = jobs[n]
        before(k, t, h)
        first = k * half_rows + h * CHUNK
        scores[n % 2] = lax.dot_general(
            w[first : first + CHUNK],
            embed[t * TILE : (t + 1) * TILE],
            (((1,), (1,)), ((), ())),
            preferred_element_type=F32,
        )

    score(0)
    for n, (k, t, h) in enumerate(jobs):
        if n + 1 < len(jobs):
            score(n + 1)
        for i in range(CHUNK // CLUSTER):
            c = h * (CHUNK // CLUSTER) + i
            hit = (word_ref[:, t * TILE : (t + 1) * TILE] & jnp.int16(1 << (k * clusters + c))) != 0
            sign = jnp.where(hit, jnp.bfloat16(-1), jnp.bfloat16(1)).astype(F32)
            groups = []
            for g in range(TILE // INST_BLOCK):
                lanes = slice(g * INST_BLOCK, (g + 1) * INST_BLOCK)
                z = scores[n % 2, i * CLUSTER : (i + 1) * CLUSTER, lanes] * 0.5 + bias_ref[k, c]
                group = t * (TILE // INST_BLOCK) + g
                groups.append((jnp.tanh(z) + sign[:, lanes]).astype(BF16) * mask_ref[k, c, group : group + 1])
            emit(k, t, c, jnp.concatenate(groups, axis=1))


def block_in(t, i, over, core):
    first, second, third = 1 - t // 2, i // 2, i % 2
    owner = core if t % 2 else 1 - core
    return (first + 4 * second + 2 * third + owner * (first - 3 * second + 2 * third)) ^ over


def set_words(tiles, pos_ref, word):
    half_rows = CLUSTER * CLUSTERS // 2
    first_label = lax.axis_index("label") * 2 * half_rows
    send_half = 1 - half_index()
    label_no = lax.broadcasted_iota(jnp.int32, (CLUSTER, TILE), 0).astype(jnp.int16)
    for t in tiles:
        lanes = slice(t * TILE, (t + 1) * TILE)
        local = pos_ref[:, lanes] - first_label
        inside = (local >= 0) & (local < 2 * half_rows)
        bits = jnp.where(inside, jnp.left_shift(1, ((local >> 7) ^ (send_half * (CLUSTERS // 2))) & 15), 0).astype(jnp.int16)
        at = (local & (CLUSTER - 1)).astype(jnp.int16)
        found = jnp.zeros((CLUSTER, TILE), jnp.int16)
        for p in range(pos_ref.shape[0]):
            found = found | jnp.where(
                label_no == jnp.broadcast_to(at[p : p + 1], found.shape),
                jnp.broadcast_to(bits[p : p + 1], found.shape),
                jnp.int16(0),
            )
        word[:, lanes] = found


def send_kernel(n_label, embed_hbm, weight_hbm, bias_hbm, beam_hbm, pos_hbm, embed, w, word, mask, bias_full, slopes_t,
                label_out, bias_raw, beam_raw, pos_raw, beam, pos, scores, sems):
    half_rows = label_out.shape[0]
    clusters = half_rows // CLUSTER
    tiles = embed.shape[0] // TILE
    half = 1 - half_index()
    over, within, core = place(n_label)
    piece = embed.shape[0] // n_label
    subs = INST_BLOCK // piece // 2
    small = [
        pltpu.make_async_copy(source, target, sems.at[k])
        for k, (source, target) in enumerate(((beam_hbm, beam_raw), (bias_hbm, bias_raw), (pos_hbm, pos_raw)))
    ]
    w_copies = [
        pltpu.make_async_copy(
            weight_hbm.at[pl.ds(pl.multiple_of(which * half_rows, half_rows), half_rows)],
            w.at[pl.ds(k * half_rows, half_rows)],
            sems.at[3 + k],
        )
        for k, which in enumerate((half, 1 - half))
    ]
    e_copies = []
    for t in range(tiles):
        e_copies.append([])
        for i in range(4):
            for j in range(subs):
                at = t * (TILE // piece) + len(e_copies[t])
                row = block_in(t, i, over, core) * INST_BLOCK
                row = row + (2 * (j ^ within if subs > 1 else 0) + (core if t % 2 else 1 - core)) * piece
                e_copies[t].append(
                    pltpu.make_async_copy(
                        embed_hbm.at[pl.ds(pl.multiple_of(row, piece), piece)],
                        embed.at[pl.ds(at * piece, piece)],
                        sems.at[5 + at],
                    )
                )
    for copy in (*small, *e_copies[0], w_copies[0]):
        copy.start()
    for copy in small:
        copy.wait()
    for copy in (*e_copies[1], *e_copies[2], *e_copies[3]):
        copy.start()

    lane = lax.broadcasted_iota(jnp.int32, (BLOCKS, INST_BLOCK), 1)
    low = lane < INST_BLOCK // 2

    def relative_lanes(x):
        code = 2 * within + core
        for k in range((2 * subs).bit_length() - 1):
            shift = piece << k
            turned = jnp.where(
                (lane & shift) != 0, pltpu.roll(x, shift, 1), pltpu.roll(x, INST_BLOCK - shift, 1)
            )
            x = jnp.where((code >> k) % 2 == 1, turned, x)
        if subs > 1:
            x = jnp.concatenate(
                [x[:, (2 * j + c) * piece : (2 * j + c + 1) * piece] for c in range(2) for j in range(subs)], axis=1
            )
        return x

    def set_positives(t):
        for g in range(TILE // INST_BLOCK):
            one, two = (
                relative_lanes(
                    pos_raw[:, pl.ds(pl.multiple_of(block_in(t, 2 * g + h, over, core) * INST_BLOCK, INST_BLOCK), INST_BLOCK)]
                )
                for h in range(2)
            )
            group = t * (TILE // INST_BLOCK) + g
            pos[:, group * INST_BLOCK : (group + 1) * INST_BLOCK] = (
                jnp.where(low, one, pltpu.roll(two, INST_BLOCK // 2, 1))
                if t % 2
                else jnp.where(low, pltpu.roll(one, INST_BLOCK // 2, 1), two)
            )

    for t in range(tiles):
        for i in range(4):
            group = 8 * (i % 2) + t * 2 + i // 2
            beam[group : group + 1] = beam_raw[pl.ds(block_in(t, i, over, core), 1)]
    for t in range(tiles):
        set_positives(t)
    set_words(range(tiles), pos, word)

    row = lax.broadcasted_iota(jnp.int32, (2 * clusters, 2 * clusters * INST_BLOCK), 0)
    column = lax.broadcasted_iota(jnp.int32, (2 * clusters, 2 * clusters * INST_BLOCK), 1)
    spread = jnp.where(row == (column // INST_BLOCK) ^ (half * clusters), 0.5, 0.0).astype(BF16)
    biases = lax.dot_general(bias_raw[...], spread, (((0,), (0,)), ((), ())), preferred_element_type=F32)
    first_cluster = lax.axis_index("label") * 2 * clusters
    for k in range(2):
        for c in range(clusters):
            i = k * clusters + c
            bias_full[k, c] = biases[:, i * INST_BLOCK : (i + 1) * INST_BLOCK]
            held = jnp.where(beam[...] == first_cluster + (i ^ (half * clusters)), 0.5 * SCALE, 0.0)
            held = jnp.broadcast_to(jnp.max(held, axis=1, keepdims=True), (2 * BLOCKS, INST_BLOCK))
            mask[k, c] = jnp.where(low, held[:BLOCKS], held[BLOCKS:]).astype(BF16)
    w_copies[0].wait()

    def before(k, t, h):
        if h == 0:
            for copy in e_copies[t]:
                copy.wait()
            if t == 1:
                w_copies[1].start()

    def emit(k, t, c, part):
        slopes_t[c * CLUSTER : (c + 1) * CLUSTER, t * TILE : (t + 1) * TILE] = part
        if t == tiles - 1 and (c + 1) % (CHUNK // CLUSTER) == 0:
            rows = slice((c + 1) * CLUSTER - CHUNK, (c + 1) * CLUSTER)
            label_out[rows] = jnp.dot(slopes_t[rows], embed[...], preferred_element_type=F32).astype(BF16)

    jobs = [(0, t, h) for t in range(tiles) for h in range(half_rows // CHUNK)]
    slope_chunks(jobs, scores, w, embed, bias_full, mask, word, before, emit)
    w_copies[1].wait()


def store_rows(outs, slopes, w):
    sums = jnp.dot(slopes[...], w[...], preferred_element_type=F32).astype(BF16)
    count = TILE // len(outs)
    for i, out in enumerate(outs):
        out[...] = sums[i * count : (i + 1) * count].reshape(out.shape)


def row_tile(t, outs, embed, w, word, mask, bias_full, first_slopes_t, own_slopes_t, scores, slopes):
    half_rows = w.shape[0] // 2

    def emit(k, t, c, part):
        if c == 0:
            slopes[:, :half_rows] = first_slopes_t[:, t * TILE : (t + 1) * TILE].T
        own_slopes_t[c * CLUSTER : (c + 1) * CLUSTER] = part
        slopes[:, half_rows + c * CLUSTER : half_rows + (c + 1) * CLUSTER] = part.T

    jobs = [(1, t, h) for h in range(half_rows // CHUNK)]
    slope_chunks(jobs, scores, w, embed, bias_full, mask, word, lambda *job: None, emit)
    store_rows(outs, slopes, w)


def rows_kernel(t, embed, w, word, mask, bias_full, first_slopes_t, own_slopes_t, row_out, scores, slopes):
    row_tile(t, [row_out], embed, w, word, mask, bias_full, first_slopes_t, own_slopes_t, scores, slopes)


def last_rows_kernel(embed, w, word, mask, bias_full, first_slopes_t, *rest):
    *outs, three_slopes_t, four_slopes_t, scores, slopes = rest
    shared = (embed, w, word, mask, bias_full, first_slopes_t)
    row_tile(2, outs[:-1], *shared, three_slopes_t, scores.at[0], slopes.at[0])
    row_tile(3, outs[-1:], *shared, four_slopes_t, scores.at[1], slopes.at[1])


def keep_kernel(embed, *refs):
    *slopes_t, label_out = refs
    total = 0.0
    for t, part in enumerate(slopes_t):
        total = total + jnp.dot(part[...], embed[t * TILE : (t + 1) * TILE], preferred_element_type=F32)
    label_out[...] = total.astype(BF16)


def sum_kernel(places, *refs):
    *terms, out = refs
    out[...] = add(*(term[at] for term, at in zip(terms, places)))


def half_sum_kernel(kept, got, out):
    out[...] = add(kept[: out.shape[0]], got[: out.shape[0]])


def finish_kernel(kept, got, summed, *refs):
    *row_terms, row_out, label_out, row, rest, sems = refs
    first = summed.shape[0]
    copies = [
        pltpu.make_async_copy(row, row_out, sems.at[0]),
        pltpu.make_async_copy(summed, label_out.at[pl.ds(0, first)], sems.at[1]),
        pltpu.make_async_copy(rest, label_out.at[pl.ds(first, rest.shape[0])], sems.at[2]),
    ]
    copies[1].start()
    row[...] = add(*(term[(0,) * (len(term.shape) - 2)] for term in row_terms))
    copies[0].start()
    rest[...] = add(kept[first:], got[first:])
    copies[2].start()
    for copy in copies:
        copy.wait()


def swapped(value, axis, size, bit):
    return lax.ppermute(value, axis, [(i, i ^ bit) for i in range(size)])


def add(*terms):
    total = terms[0].astype(F32)
    for term in terms[1:]:
        total = total + term.astype(F32)
    return total.astype(BF16)


def on_device(n_dp, n_label, embed, weight, bias, beam, positives):
    rows, features = embed.shape
    labels = weight.shape[0]
    half_rows = labels // 2
    clusters = half_rows // CLUSTER
    piece = rows // n_label
    subs = n_label // 2 // BLOCKS
    bias_rows = bias.reshape(labels // CLUSTER, CLUSTER)
    pos_rows = positives.T
    vmem = pl.BlockSpec(memory_space=pltpu.VMEM)
    hbm = pl.BlockSpec(memory_space=pltpu.HBM)
    params = pltpu.CompilerParams(vmem_limit_bytes=VMEM_LIMIT)
    shape = jax.ShapeDtypeStruct
    tile_shape = shape((half_rows, TILE), BF16)
    row_shape = shape((BLOCKS // 2, subs, piece, features), BF16)
    score_scratch = pltpu.VMEM((2, CHUNK, TILE), F32)
    slope_scratch = pltpu.VMEM((TILE, labels), BF16)

    def cost(halves):
        return pl.CostEstimate(flops=halves * 2 * rows * half_rows * features, bytes_accessed=0, transcendentals=0)

    *shared, label_send = pl.pallas_call(
        functools.partial(send_kernel, n_label),
        out_shape=[
            shape((rows, features), BF16),
            shape((labels, features), BF16),
            shape((CLUSTER, rows), jnp.int16),
            shape((2, clusters, BLOCKS, INST_BLOCK), BF16),
            shape((2, clusters, CLUSTER, INST_BLOCK), F32),
            shape((half_rows, rows), BF16),
            shape((half_rows, features), BF16),
        ],
        in_specs=[hbm] * 5,
        out_specs=[vmem] * 7,
        scratch_shapes=[
            pltpu.VMEM(bias_rows.shape, BF16),
            pltpu.VMEM(beam.shape, jnp.int32),
            pltpu.VMEM(pos_rows.shape, jnp.int32),
            pltpu.VMEM((2 * BLOCKS, beam.shape[1]), jnp.int32),
            pltpu.VMEM(pos_rows.shape, jnp.int32),
            score_scratch,
            pltpu.SemaphoreType.DMA((5 + n_label,)),
        ],
        compiler_params=params,
        cost_estimate=cost(2),
        name="send_half",
    )(*(pltpu.with_memory_space_constraint(x, pltpu.HBM) for x in (embed, weight, bias_rows, beam, pos_rows)))
    embed_own = shared[0]

    label_got = swapped(label_send, "dp", n_dp, n_dp // 2)

    def tile_rows(t, name, inputs):
        return pl.pallas_call(
            functools.partial(rows_kernel, t),
            out_shape=[tile_shape, row_shape],
            in_specs=[vmem] * 6,
            out_specs=[vmem] * 2,
            scratch_shapes=[score_scratch, slope_scratch],
            compiler_params=params,
            cost_estimate=cost(0),
            name=name,
        )(*inputs)

    one_slopes_t, first_send = tile_rows(0, "first_rows", shared)
    first_got = swapped(first_send, "label", n_label, 1)
    two_slopes_t, first_keep = tile_rows(1, "keep_rows", shared)
    first_got, *shared = lax.optimization_barrier((first_got, *shared))

    axes = [2 * subs, 4 * subs, 8 * subs]

    def summed_at(*terms):
        arrays, places = zip(*terms)
        size = places[0].stop - places[0].start
        return pl.pallas_call(
            functools.partial(sum_kernel, places),
            out_shape=shape((size, subs, piece, features), BF16),
            in_specs=[vmem] * len(arrays),
            out_specs=vmem,
            compiler_params=params,
            cost_estimate=cost(0),
            name="row_sum",
        )(*arrays)

    def passed_on(value, stage):
        bits = (axes[(0, 2, 1)[stage]], axes[(1, 0, 2)[stage]])
        return lax.ppermute(value, "label", [(i, i ^ bits[i % 2]) for i in range(n_label)])

    far_got = passed_on(summed_at((first_keep, slice(2, 4)), (first_got, slice(2, 4))), 0)
    near_got = passed_on(summed_at((first_keep, slice(0, 2)), (first_got, slice(0, 2))), 0)

    part_shape = shape((2, subs, piece, features), BF16)
    *last_send, last_keep, three_slopes_t, four_slopes_t = pl.pallas_call(
        last_rows_kernel,
        out_shape=[part_shape] * 2 + [row_shape, tile_shape, tile_shape],
        in_specs=[vmem] * 6,
        out_specs=[vmem] * 5,
        scratch_shapes=[
            pltpu.VMEM((2, 2, CHUNK, TILE), F32),
            pltpu.VMEM((2, TILE, labels), BF16),
        ],
        compiler_params=params,
        cost_estimate=cost(0),
        name="last_rows",
    )(*shared)

    last_got = [swapped(part, "label", n_label, 1) for part in last_send]
    three_got = passed_on(summed_at((last_keep, slice(3, 4)), (last_got[1], slice(1, 2)), (far_got, slice(1, 2))), 1)
    two_got = passed_on(summed_at((last_keep, slice(2, 3)), (last_got[1], slice(0, 1)), (far_got, slice(0, 1))), 1)
    row_got = passed_on(summed_at((last_keep, slice(1, 2)), (last_got[0], slice(1, 2)), (near_got, slice(1, 2)), (three_got, slice(0, 1))), 2)
    row_terms = [last_keep, last_got[0], near_got, two_got, row_got]
    bit = subs
    while bit > 1:
        row_sum = add(*(term.reshape(-1, subs, piece, features)[0] for term in row_terms[:-1]))
        held = row_sum.shape[0] // 2
        came = row_terms[-1].reshape(subs, piece, features)
        incoming = swapped(add(row_sum[held:], came[held:]), "label", n_label, bit)
        row_terms = [add(row_sum[:held], came[:held]), incoming]
        subs = held
        bit //= 2

    label_keep = pl.pallas_call(
        keep_kernel,
        out_shape=shape((half_rows, features), BF16),
        in_specs=[vmem] * 5,
        out_specs=vmem,
        compiler_params=params,
        cost_estimate=cost(0),
        name="keep_half",
    )(embed_own, one_slopes_t, two_slopes_t, three_slopes_t, four_slopes_t)

    kept, got = label_keep, label_got
    step = n_dp // 4
    at = lax.axis_index("dp")
    while step >= 1:
        label_sum = add(kept, got)
        size = label_sum.shape[0] // 2
        mine = (at // step) % 2
        outgoing = lax.dynamic_slice_in_dim(label_sum, (1 - mine) * size, size, 0)
        kept = lax.dynamic_slice_in_dim(label_sum, mine * size, size, 0)
        got = swapped(outgoing, "dp", n_dp, step)
        step //= 2

    size = kept.shape[0]
    summed = pl.pallas_call(
        half_sum_kernel,
        out_shape=shape((size // 2, features), BF16),
        in_specs=[vmem] * 2,
        out_specs=vmem,
        compiler_params=params,
        cost_estimate=cost(2),
        name="half_sum",
    )(kept, got)
    return pl.pallas_call(
        finish_kernel,
        out_shape=[shape((piece, features), BF16), shape((size, features), BF16)],
        in_specs=[vmem] * (3 + len(row_terms)),
        out_specs=[hbm] * 2,
        scratch_shapes=[
            pltpu.VMEM((piece, features), BF16),
            pltpu.VMEM((size // 2, features), BF16),
            pltpu.SemaphoreType.DMA((3,)),
        ],
        compiler_params=params,
        cost_estimate=cost(0),
        name="finish",
    )(kept, got, summed, *row_terms)


def solution(mesh):
    in_specs = (P("dp", None), P("label", None), P("label"), P("dp", None), P("dp", None))
    out_specs = (P(("dp", "label"), None), P(("label", "dp"), None))
    body = functools.partial(on_device, mesh.shape["dp"], mesh.shape["label"])
    return jax.shard_map(body, mesh=mesh, in_specs=in_specs, out_specs=out_specs, check_vma=False)
```

```python
import functools

import jax
import jax.numpy as jnp
from jax import lax
from jax.experimental import pallas as pl
from jax.experimental.pallas import tpu as pltpu
from jax.sharding import PartitionSpec as P

INST_BLOCK = 128
CLUSTER = 128
TILE = 256
CHUNK = 256
CLUSTERS = 8
BLOCKS = 8
SCALE = 0.125

F32 = jnp.float32
BF16 = jnp.bfloat16
VMEM_LIMIT = 32 * 1024 * 1024


def half_index():
    return lax.axis_index("dp") // (lax.axis_size("dp") // 2)


def place(n_label):
    subs = n_label // 2 // BLOCKS
    pair = lax.axis_index("label") // 2
    return pair // subs, pair % subs, lax.axis_index("label") % 2


def slope_chunks(jobs, scores, w, embed, bias_ref, mask_ref, word_ref, before, emit):
    half_rows = w.shape[0] // 2
    clusters = half_rows // CLUSTER

    def score(n):
        k, t, h = jobs[n]
        before(k, t, h)
        first = k * half_rows + h * CHUNK
        scores[n % 2] = lax.dot_general(
            w[first : first + CHUNK],
            embed[t * TILE : (t + 1) * TILE],
            (((1,), (1,)), ((), ())),
            preferred_element_type=F32,
        )

    score(0)
    for n, (k, t, h) in enumerate(jobs):
        if n + 1 < len(jobs):
            score(n + 1)
        for i in range(CHUNK // CLUSTER):
            c = h * (CHUNK // CLUSTER) + i
            hit = (word_ref[:, t * TILE : (t + 1) * TILE] & jnp.int16(1 << (k * clusters + c))) != 0
            sign = jnp.where(hit, jnp.bfloat16(-1), jnp.bfloat16(1)).astype(F32)
            groups = []
            for g in range(TILE // INST_BLOCK):
                lanes = slice(g * INST_BLOCK, (g + 1) * INST_BLOCK)
                z = scores[n % 2, i * CLUSTER : (i + 1) * CLUSTER, lanes] * 0.5 + bias_ref[k, c]
                group = t * (TILE // INST_BLOCK) + g
                groups.append((jnp.tanh(z) + sign[:, lanes]).astype(BF16) * mask_ref[k, c, group : group + 1])
            emit(k, t, c, jnp.concatenate(groups, axis=1))


def block_in(t, i, over, core):
    first, second, third = 1 - t // 2, i // 2, i % 2
    owner = core if t % 2 else 1 - core
    return (first + 2 * second + 4 * third + owner * (first + 2 * second - 3 * third)) ^ over


def set_words(tiles, pos_ref, word):
    half_rows = CLUSTER * CLUSTERS // 2
    first_label = lax.axis_index("label") * 2 * half_rows
    send_half = 1 - half_index()
    label_no = lax.broadcasted_iota(jnp.int32, (CLUSTER, TILE), 0).astype(jnp.int16)
    for t in tiles:
        lanes = slice(t * TILE, (t + 1) * TILE)
        local = pos_ref[:, lanes] - first_label
        inside = (local >= 0) & (local < 2 * half_rows)
        bits = jnp.where(inside, jnp.left_shift(1, ((local >> 7) ^ (send_half * (CLUSTERS // 2))) & 15), 0).astype(jnp.int16)
        at = (local & (CLUSTER - 1)).astype(jnp.int16)
        found = jnp.zeros((CLUSTER, TILE), jnp.int16)
        for p in range(pos_ref.shape[0]):
            found = found | jnp.where(
                label_no == jnp.broadcast_to(at[p : p + 1], found.shape),
                jnp.broadcast_to(bits[p : p + 1], found.shape),
                jnp.int16(0),
            )
        word[:, lanes] = found


def first_kernel(n_label, embed_hbm, weight_hbm, bias_hbm, beam_hbm, pos_hbm, embed, w, pos, mask, bias_full,
                 first_slopes_t, own_slopes_t, row_out, bias_raw, beam_raw, pos_raw, beam, word, scores, slopes, sems):
    half_rows = own_slopes_t.shape[0]
    clusters = half_rows // CLUSTER
    tiles = embed.shape[0] // TILE
    half = 1 - half_index()
    over, within, core = place(n_label)
    piece = embed.shape[0] // n_label
    subs = INST_BLOCK // piece // 2
    small = [
        pltpu.make_async_copy(source, target, sems.at[k])
        for k, (source, target) in enumerate(((beam_hbm, beam_raw), (bias_hbm, bias_raw), (pos_hbm, pos_raw)))
    ]
    w_copies = [
        pltpu.make_async_copy(
            weight_hbm.at[pl.ds(pl.multiple_of(which * half_rows, half_rows), half_rows)],
            w.at[pl.ds(k * half_rows, half_rows)],
            sems.at[3 + k],
        )
        for k, which in enumerate((half, 1 - half))
    ]
    e_copies = []
    for t in range(tiles):
        e_copies.append([])
        for i in range(4):
            for j in range(subs):
                at = t * (TILE // piece) + len(e_copies[t])
                row = block_in(t, i, over, core) * INST_BLOCK
                row = row + (2 * (j ^ within if subs > 1 else 0) + (core if t % 2 else 1 - core)) * piece
                e_copies[t].append(
                    pltpu.make_async_copy(
                        embed_hbm.at[pl.ds(pl.multiple_of(row, piece), piece)],
                        embed.at[pl.ds(at * piece, piece)],
                        sems.at[5 + at],
                    )
                )
    for copy in (*small, *e_copies[0], *w_copies, *e_copies[1], *e_copies[2], *e_copies[3]):
        copy.start()
    for copy in small:
        copy.wait()

    lane = lax.broadcasted_iota(jnp.int32, (BLOCKS, INST_BLOCK), 1)
    low = lane < INST_BLOCK // 2

    def relative_lanes(x):
        code = 2 * within + core
        for k in range((2 * subs).bit_length() - 1):
            shift = piece << k
            turned = jnp.where(
                (lane & shift) != 0, pltpu.roll(x, shift, 1), pltpu.roll(x, INST_BLOCK - shift, 1)
            )
            x = jnp.where((code >> k) % 2 == 1, turned, x)
        if subs > 1:
            x = jnp.concatenate(
                [x[:, (2 * j + c) * piece : (2 * j + c + 1) * piece] for c in range(2) for j in range(subs)], axis=1
            )
        return x

    def set_positives(t):
        for g in range(TILE // INST_BLOCK):
            one, two = (
                relative_lanes(
                    pos_raw[:, pl.ds(pl.multiple_of(block_in(t, 2 * g + h, over, core) * INST_BLOCK, INST_BLOCK), INST_BLOCK)]
                )
                for h in range(2)
            )
            group = t * (TILE // INST_BLOCK) + g
            pos[:, group * INST_BLOCK : (group + 1) * INST_BLOCK] = (
                jnp.where(low, one, pltpu.roll(two, INST_BLOCK // 2, 1))
                if t % 2
                else jnp.where(low, pltpu.roll(one, INST_BLOCK // 2, 1), two)
            )

    for t in range(tiles):
        for i in range(4):
            group = 8 * (i % 2) + t * 2 + i // 2
            beam[group : group + 1] = beam_raw[pl.ds(block_in(t, i, over, core), 1)]
    for t in range(tiles):
        set_positives(t)
    set_words([0], pos, word)

    row = lax.broadcasted_iota(jnp.int32, (2 * clusters, 2 * clusters * INST_BLOCK), 0)
    column = lax.broadcasted_iota(jnp.int32, (2 * clusters, 2 * clusters * INST_BLOCK), 1)
    spread = jnp.where(row == (column // INST_BLOCK) ^ (half * clusters), 0.5, 0.0).astype(BF16)
    biases = lax.dot_general(bias_raw[...], spread, (((0,), (0,)), ((), ())), preferred_element_type=F32)
    first_cluster = lax.axis_index("label") * 2 * clusters
    for k in range(2):
        for c in range(clusters):
            i = k * clusters + c
            bias_full[k, c] = biases[:, i * INST_BLOCK : (i + 1) * INST_BLOCK]
            held = jnp.where(beam[...] == first_cluster + (i ^ (half * clusters)), 0.5 * SCALE, 0.0)
            held = jnp.broadcast_to(jnp.max(held, axis=1, keepdims=True), (2 * BLOCKS, INST_BLOCK))
            mask[k, c] = jnp.where(low, held[:BLOCKS], held[BLOCKS:]).astype(BF16)
    for copy in (w_copies[0], *e_copies[0]):
        copy.wait()

    def before(k, t, h):
        if (k, h) == (1, 0):
            w_copies[1].wait()

    def emit(k, t, c, part):
        out = own_slopes_t if k else first_slopes_t
        out[c * CLUSTER : (c + 1) * CLUSTER] = part
        slopes[:, (k * clusters + c) * CLUSTER : (k * clusters + c + 1) * CLUSTER] = part.T

    jobs = [(k, 0, h) for k in range(2) for h in range(half_rows // CHUNK)]
    slope_chunks(jobs, scores, w, embed, bias_full, mask, word, before, emit)
    store_rows([row_out], slopes, w)
    for copy in (*e_copies[1], *e_copies[2], *e_copies[3]):
        copy.wait()


def label_kernel(embed, w, pos, mask, bias_full, one_slopes_t, word, slopes_t, label_out, scores):
    half_rows = label_out.shape[0]
    tiles = embed.shape[0] // TILE
    set_words(range(1, tiles), pos, word)

    def emit(k, t, c, part):
        slopes_t[c * CLUSTER : (c + 1) * CLUSTER, (t - 1) * TILE : t * TILE] = part
        if t == tiles - 1 and (c + 1) % (CHUNK // CLUSTER) == 0:
            rows = slice((c + 1) * CLUSTER - CHUNK, (c + 1) * CLUSTER)
            label_out[rows] = (
                jnp.dot(one_slopes_t[rows], embed[:TILE], preferred_element_type=F32)
                + jnp.dot(slopes_t[rows], embed[TILE:], preferred_element_type=F32)
            ).astype(BF16)

    jobs = [(0, t, h) for t in range(1, tiles) for h in range(half_rows // CHUNK)]
    slope_chunks(jobs, scores, w, embed, bias_full, mask, word, lambda *job: None, emit)


def store_rows(outs, slopes, w):
    sums = jnp.dot(slopes[...], w[...], preferred_element_type=F32).astype(BF16)
    count = TILE // len(outs)
    for i, out in enumerate(outs):
        out[...] = sums[i * count : (i + 1) * count].reshape(out.shape)


def row_tile(t, outs, embed, w, word, mask, bias_full, first_slopes_t, own_slopes_t, scores, slopes):
    half_rows = w.shape[0] // 2

    def emit(k, t, c, part):
        if c == 0:
            slopes[:, :half_rows] = first_slopes_t[:, (t - 1) * TILE : t * TILE].T
        own_slopes_t[c * CLUSTER : (c + 1) * CLUSTER] = part
        slopes[:, half_rows + c * CLUSTER : half_rows + (c + 1) * CLUSTER] = part.T

    jobs = [(1, t, h) for h in range(half_rows // CHUNK)]
    slope_chunks(jobs, scores, w, embed, bias_full, mask, word, lambda *job: None, emit)
    store_rows(outs, slopes, w)


def keep_rows_kernel(embed, w, word, mask, bias_full, first_slopes_t, own_slopes_t, row_out, scores, slopes):
    row_tile(1, [row_out], embed, w, word, mask, bias_full, first_slopes_t, own_slopes_t, scores, slopes)


def last_rows_kernel(embed, w, word, mask, bias_full, first_slopes_t, *rest):
    *outs, three_slopes_t, four_slopes_t, scores, slopes = rest
    shared = (embed, w, word, mask, bias_full, first_slopes_t)
    row_tile(2, outs[:-1], *shared, three_slopes_t, scores.at[0], slopes.at[0])
    row_tile(3, outs[-1:], *shared, four_slopes_t, scores.at[1], slopes.at[1])


def keep_kernel(embed, *refs):
    *slopes_t, label_out = refs
    total = 0.0
    for t, part in enumerate(slopes_t):
        total = total + jnp.dot(part[...], embed[t * TILE : (t + 1) * TILE], preferred_element_type=F32)
    label_out[...] = total.astype(BF16)


def sum_kernel(places, *refs):
    *terms, out = refs
    out[...] = add(*(term[at] for term, at in zip(terms, places)))


def half_sum_kernel(kept, got, out):
    out[...] = add(kept[: out.shape[0]], got[: out.shape[0]])


def finish_kernel(kept, got, summed, *refs):
    *row_terms, row_out, label_out, row, rest, sems = refs
    first = summed.shape[0]
    copies = [
        pltpu.make_async_copy(row, row_out, sems.at[0]),
        pltpu.make_async_copy(summed, label_out.at[pl.ds(0, first)], sems.at[1]),
        pltpu.make_async_copy(rest, label_out.at[pl.ds(first, rest.shape[0])], sems.at[2]),
    ]
    copies[1].start()
    row[...] = add(*(term[(0,) * (len(term.shape) - 2)] for term in row_terms))
    copies[0].start()
    rest[...] = add(kept[first:], got[first:])
    copies[2].start()
    for copy in copies:
        copy.wait()


def swapped(value, axis, size, bit):
    return lax.ppermute(value, axis, [(i, i ^ bit) for i in range(size)])


def add(*terms):
    total = terms[0].astype(F32)
    for term in terms[1:]:
        total = total + term.astype(F32)
    return total.astype(BF16)


def on_device(n_dp, n_label, embed, weight, bias, beam, positives):
    rows, features = embed.shape
    labels = weight.shape[0]
    half_rows = labels // 2
    clusters = half_rows // CLUSTER
    piece = rows // n_label
    subs = n_label // 2 // BLOCKS
    bias_rows = bias.reshape(labels // CLUSTER, CLUSTER)
    pos_rows = positives.T
    vmem = pl.BlockSpec(memory_space=pltpu.VMEM)
    hbm = pl.BlockSpec(memory_space=pltpu.HBM)
    params = pltpu.CompilerParams(vmem_limit_bytes=VMEM_LIMIT)
    shape = jax.ShapeDtypeStruct
    tile_shape = shape((half_rows, TILE), BF16)
    row_shape = shape((BLOCKS // 2, subs, piece, features), BF16)
    score_scratch = pltpu.VMEM((2, CHUNK, TILE), F32)
    slope_scratch = pltpu.VMEM((TILE, labels), BF16)

    def cost(halves):
        return pl.CostEstimate(flops=halves * 2 * rows * half_rows * features, bytes_accessed=0, transcendentals=0)

    *common, head_slopes_t, one_slopes_t, first_send = pl.pallas_call(
        functools.partial(first_kernel, n_label),
        out_shape=[
            shape((rows, features), BF16),
            shape((labels, features), BF16),
            shape(pos_rows.shape, jnp.int32),
            shape((2, clusters, BLOCKS, INST_BLOCK), BF16),
            shape((2, clusters, CLUSTER, INST_BLOCK), F32),
            tile_shape,
            tile_shape,
            row_shape,
        ],
        in_specs=[hbm] * 5,
        out_specs=[vmem] * 8,
        scratch_shapes=[
            pltpu.VMEM(bias_rows.shape, BF16),
            pltpu.VMEM(beam.shape, jnp.int32),
            pltpu.VMEM(pos_rows.shape, jnp.int32),
            pltpu.VMEM((2 * BLOCKS, beam.shape[1]), jnp.int32),
            pltpu.VMEM((CLUSTER, TILE), jnp.int16),
            score_scratch,
            slope_scratch,
            pltpu.SemaphoreType.DMA((5 + n_label,)),
        ],
        compiler_params=params,
        cost_estimate=cost(2),
        name="first_rows",
    )(*(pltpu.with_memory_space_constraint(x, pltpu.HBM) for x in (embed, weight, bias_rows, beam, pos_rows)))

    first_got = swapped(first_send, "label", n_label, 1)

    word, first_slopes_t, label_send = pl.pallas_call(
        label_kernel,
        out_shape=[
            shape((CLUSTER, rows), jnp.int16),
            shape((half_rows, rows - TILE), BF16),
            shape((half_rows, features), BF16),
        ],
        in_specs=[vmem] * 6,
        out_specs=[vmem] * 3,
        scratch_shapes=[score_scratch],
        compiler_params=params,
        cost_estimate=cost(0),
        name="send_half",
    )(*common, head_slopes_t)
    embed_own, w, _, mask, bias_full = common
    shared = (embed_own, w, word, mask, bias_full, first_slopes_t)

    label_got = swapped(label_send, "dp", n_dp, n_dp // 2)
    first_got, *shared = lax.optimization_barrier((first_got, *shared))

    two_slopes_t, first_keep = pl.pallas_call(
        keep_rows_kernel,
        out_shape=[tile_shape, row_shape],
        in_specs=[vmem] * 6,
        out_specs=[vmem] * 2,
        scratch_shapes=[score_scratch, slope_scratch],
        compiler_params=params,
        cost_estimate=cost(0),
        name="keep_rows",
    )(*shared)

    axes = [2 * subs, 4 * subs, 8 * subs]

    def summed_at(*terms):
        arrays, places = zip(*terms)
        size = places[0].stop - places[0].start
        return pl.pallas_call(
            functools.partial(sum_kernel, places),
            out_shape=shape((size, subs, piece, features), BF16),
            in_specs=[vmem] * len(arrays),
            out_specs=vmem,
            compiler_params=params,
            cost_estimate=cost(0),
            name="row_sum",
        )(*arrays)

    def passed_on(value, stage):
        bits = (axes[stage], axes[(stage + 1) % 3])
        return lax.ppermute(value, "label", [(i, i ^ bits[i % 2]) for i in range(n_label)])

    far_got = passed_on(summed_at((first_keep, slice(2, 4)), (first_got, slice(2, 4))), 0)
    near_got = passed_on(summed_at((first_keep, slice(0, 2)), (first_got, slice(0, 2))), 0)

    part_shape = shape((2, subs, piece, features), BF16)
    *last_send, last_keep, three_slopes_t, four_slopes_t = pl.pallas_call(
        last_rows_kernel,
        out_shape=[part_shape] * 2 + [row_shape, tile_shape, tile_shape],
        in_specs=[vmem] * 6,
        out_specs=[vmem] * 5,
        scratch_shapes=[
            pltpu.VMEM((2, 2, CHUNK, TILE), F32),
            pltpu.VMEM((2, TILE, labels), BF16),
        ],
        compiler_params=params,
        cost_estimate=cost(2),
        name="last_rows",
    )(*shared)

    last_got = [swapped(part, "label", n_label, 1) for part in last_send]
    three_got = passed_on(summed_at((last_keep, slice(3, 4)), (last_got[1], slice(1, 2)), (far_got, slice(1, 2))), 1)
    two_got = passed_on(summed_at((last_keep, slice(2, 3)), (last_got[1], slice(0, 1)), (far_got, slice(0, 1))), 1)
    row_got = passed_on(summed_at((last_keep, slice(1, 2)), (last_got[0], slice(1, 2)), (near_got, slice(1, 2)), (three_got, slice(0, 1))), 2)
    row_terms = [last_keep, last_got[0], near_got, two_got, row_got]
    bit = subs
    while bit > 1:
        row_sum = add(*(term.reshape(-1, subs, piece, features)[0] for term in row_terms[:-1]))
        held = row_sum.shape[0] // 2
        came = row_terms[-1].reshape(subs, piece, features)
        incoming = swapped(add(row_sum[held:], came[held:]), "label", n_label, bit)
        row_terms = [add(row_sum[:held], came[:held]), incoming]
        subs = held
        bit //= 2

    label_keep = pl.pallas_call(
        keep_kernel,
        out_shape=shape((half_rows, features), BF16),
        in_specs=[vmem] * 5,
        out_specs=vmem,
        compiler_params=params,
        cost_estimate=cost(0),
        name="keep_half",
    )(embed_own, one_slopes_t, two_slopes_t, three_slopes_t, four_slopes_t)

    kept, got = label_keep, label_got
    step = n_dp // 4
    at = lax.axis_index("dp")
    while step >= 1:
        label_sum = add(kept, got)
        size = label_sum.shape[0] // 2
        mine = (at // step) % 2
        outgoing = lax.dynamic_slice_in_dim(label_sum, (1 - mine) * size, size, 0)
        kept = lax.dynamic_slice_in_dim(label_sum, mine * size, size, 0)
        got = swapped(outgoing, "dp", n_dp, step)
        step //= 2

    size = kept.shape[0]
    summed = pl.pallas_call(
        half_sum_kernel,
        out_shape=shape((size // 2, features), BF16),
        in_specs=[vmem] * 2,
        out_specs=vmem,
        compiler_params=params,
        cost_estimate=cost(2),
        name="half_sum",
    )(kept, got)
    return pl.pallas_call(
        finish_kernel,
        out_shape=[shape((piece, features), BF16), shape((size, features), BF16)],
        in_specs=[vmem] * (3 + len(row_terms)),
        out_specs=[hbm] * 2,
        scratch_shapes=[
            pltpu.VMEM((piece, features), BF16),
            pltpu.VMEM((size // 2, features), BF16),
            pltpu.SemaphoreType.DMA((3,)),
        ],
        compiler_params=params,
        cost_estimate=cost(0),
        name="finish",
    )(kept, got, summed, *row_terms)


def solution(mesh):
    in_specs = (P("dp", None), P("label", None), P("label"), P("dp", None), P("dp", None))
    out_specs = (P(("dp", "label"), None), P(("label", "dp"), None))
    body = functools.partial(on_device, mesh.shape["dp"], mesh.shape["label"])
    return jax.shard_map(body, mesh=mesh, in_specs=in_specs, out_specs=out_specs, check_vma=False)
```

```python
import functools

import jax
import jax.numpy as jnp
from jax import lax
from jax.experimental import pallas as pl
from jax.experimental.pallas import tpu as pltpu
from jax.sharding import PartitionSpec as P

INST_BLOCK = 128
CLUSTER = 128
TILE = 256
CHUNK = 256
CLUSTERS = 8
BLOCKS = 8
SCALE = 0.125

F32 = jnp.float32
BF16 = jnp.bfloat16
VMEM_LIMIT = 32 * 1024 * 1024


def half_index():
    return lax.axis_index("dp") // (lax.axis_size("dp") // 2)


def place(n_label):
    subs = n_label // 2 // BLOCKS
    pair = lax.axis_index("label") // 2
    return pair // subs, pair % subs, lax.axis_index("label") % 2


def slope_chunks(jobs, scores, w, embed, bias_ref, mask_ref, word_ref, before, emit):
    half_rows = w.shape[0] // 2
    clusters = half_rows // CLUSTER

    def score(n):
        k, t, h = jobs[n]
        before(k, t, h)
        first = k * half_rows + h * CHUNK
        scores[n % 2] = lax.dot_general(
            w[first : first + CHUNK],
            embed[t * TILE : (t + 1) * TILE],
            (((1,), (1,)), ((), ())),
            preferred_element_type=F32,
        )

    score(0)
    for n, (k, t, h) in enumerate(jobs):
        if n + 1 < len(jobs):
            score(n + 1)
        for i in range(CHUNK // CLUSTER):
            c = h * (CHUNK // CLUSTER) + i
            hit = (word_ref[:, t * TILE : (t + 1) * TILE] & jnp.int16(1 << (k * clusters + c))) != 0
            sign = jnp.where(hit, jnp.bfloat16(-1), jnp.bfloat16(1)).astype(F32)
            groups = []
            for g in range(TILE // INST_BLOCK):
                lanes = slice(g * INST_BLOCK, (g + 1) * INST_BLOCK)
                z = scores[n % 2, i * CLUSTER : (i + 1) * CLUSTER, lanes] * 0.5 + bias_ref[k, c]
                group = t * (TILE // INST_BLOCK) + g
                groups.append((jnp.tanh(z) + sign[:, lanes]).astype(BF16) * mask_ref[k, c, group : group + 1])
            emit(k, t, c, jnp.concatenate(groups, axis=1))


def block_in(t, i, over, core):
    first, second, third = 1 - t // 2, i // 2, i % 2
    owner = core if t % 2 else 1 - core
    return (first + 2 * second + 4 * third + owner * (first + 2 * second - 3 * third)) ^ over


def set_words(tiles, pos_ref, word):
    half_rows = CLUSTER * CLUSTERS // 2
    first_label = lax.axis_index("label") * 2 * half_rows
    send_half = 1 - half_index()
    label_no = lax.broadcasted_iota(jnp.int32, (CLUSTER, TILE), 0).astype(jnp.int16)
    for t in tiles:
        lanes = slice(t * TILE, (t + 1) * TILE)
        local = pos_ref[:, lanes] - first_label
        inside = (local >= 0) & (local < 2 * half_rows)
        bits = jnp.where(inside, jnp.left_shift(1, ((local >> 7) ^ (send_half * (CLUSTERS // 2))) & 15), 0).astype(jnp.int16)
        at = (local & (CLUSTER - 1)).astype(jnp.int16)
        found = jnp.zeros((CLUSTER, TILE), jnp.int16)
        for p in range(pos_ref.shape[0]):
            found = found | jnp.where(
                label_no == jnp.broadcast_to(at[p : p + 1], found.shape),
                jnp.broadcast_to(bits[p : p + 1], found.shape),
                jnp.int16(0),
            )
        word[:, lanes] = found


def first_kernel(n_label, embed_hbm, weight_hbm, bias_hbm, beam_hbm, pos_hbm, embed, w, pos, mask, bias_full,
                 first_slopes_t, own_slopes_t, row_out, bias_raw, beam_raw, pos_raw, beam, word, scores, slopes, sems):
    half_rows = own_slopes_t.shape[0]
    clusters = half_rows // CLUSTER
    tiles = embed.shape[0] // TILE
    half = 1 - half_index()
    over, within, core = place(n_label)
    piece = embed.shape[0] // n_label
    subs = INST_BLOCK // piece // 2
    small = [
        pltpu.make_async_copy(source, target, sems.at[k])
        for k, (source, target) in enumerate(((beam_hbm, beam_raw), (bias_hbm, bias_raw), (pos_hbm, pos_raw)))
    ]
    w_copies = [
        pltpu.make_async_copy(
            weight_hbm.at[pl.ds(pl.multiple_of(which * half_rows, half_rows), half_rows)],
            w.at[pl.ds(k * half_rows, half_rows)],
            sems.at[3 + k],
        )
        for k, which in enumerate((half, 1 - half))
    ]
    e_copies = []
    for t in range(tiles):
        e_copies.append([])
        for i in range(4):
            for j in range(subs):
                at = t * (TILE // piece) + len(e_copies[t])
                row = block_in(t, i, over, core) * INST_BLOCK
                row = row + (2 * (j ^ within if subs > 1 else 0) + (core if t % 2 else 1 - core)) * piece
                e_copies[t].append(
                    pltpu.make_async_copy(
                        embed_hbm.at[pl.ds(pl.multiple_of(row, piece), piece)],
                        embed.at[pl.ds(at * piece, piece)],
                        sems.at[5 + at],
                    )
                )
    for copy in (*small, *e_copies[0], *w_copies, *e_copies[1], *e_copies[2], *e_copies[3]):
        copy.start()
    for copy in small:
        copy.wait()

    lane = lax.broadcasted_iota(jnp.int32, (BLOCKS, INST_BLOCK), 1)
    low = lane < INST_BLOCK // 2

    def relative_lanes(x):
        code = 2 * within + core
        for k in range((2 * subs).bit_length() - 1):
            shift = piece << k
            turned = jnp.where(
                (lane & shift) != 0, pltpu.roll(x, shift, 1), pltpu.roll(x, INST_BLOCK - shift, 1)
            )
            x = jnp.where((code >> k) % 2 == 1, turned, x)
        if subs > 1:
            x = jnp.concatenate(
                [x[:, (2 * j + c) * piece : (2 * j + c + 1) * piece] for c in range(2) for j in range(subs)], axis=1
            )
        return x

    def set_positives(t):
        for g in range(TILE // INST_BLOCK):
            one, two = (
                relative_lanes(
                    pos_raw[:, pl.ds(pl.multiple_of(block_in(t, 2 * g + h, over, core) * INST_BLOCK, INST_BLOCK), INST_BLOCK)]
                )
                for h in range(2)
            )
            group = t * (TILE // INST_BLOCK) + g
            pos[:, group * INST_BLOCK : (group + 1) * INST_BLOCK] = (
                jnp.where(low, one, pltpu.roll(two, INST_BLOCK // 2, 1))
                if t % 2
                else jnp.where(low, pltpu.roll(one, INST_BLOCK // 2, 1), two)
            )

    for t in range(tiles):
        for i in range(4):
            group = 8 * (i % 2) + t * 2 + i // 2
            beam[group : group + 1] = beam_raw[pl.ds(block_in(t, i, over, core), 1)]
    for t in range(tiles):
        set_positives(t)
    set_words([0], pos, word)

    row = lax.broadcasted_iota(jnp.int32, (2 * clusters, 2 * clusters * INST_BLOCK), 0)
    column = lax.broadcasted_iota(jnp.int32, (2 * clusters, 2 * clusters * INST_BLOCK), 1)
    spread = jnp.where(row == (column // INST_BLOCK) ^ (half * clusters), 0.5, 0.0).astype(BF16)
    biases = lax.dot_general(bias_raw[...], spread, (((0,), (0,)), ((), ())), preferred_element_type=F32)
    first_cluster = lax.axis_index("label") * 2 * clusters
    for k in range(2):
        for c in range(clusters):
            i = k * clusters + c
            bias_full[k, c] = biases[:, i * INST_BLOCK : (i + 1) * INST_BLOCK]
            held = jnp.where(beam[...] == first_cluster + (i ^ (half * clusters)), 0.5 * SCALE, 0.0)
            held = jnp.broadcast_to(jnp.max(held, axis=1, keepdims=True), (2 * BLOCKS, INST_BLOCK))
            mask[k, c] = jnp.where(low, held[:BLOCKS], held[BLOCKS:]).astype(BF16)
    for copy in (w_copies[0], *e_copies[0]):
        copy.wait()

    def before(k, t, h):
        if (k, h) == (1, 0):
            w_copies[1].wait()

    def emit(k, t, c, part):
        out = own_slopes_t if k else first_slopes_t
        out[c * CLUSTER : (c + 1) * CLUSTER] = part
        slopes[:, (k * clusters + c) * CLUSTER : (k * clusters + c + 1) * CLUSTER] = part.T

    jobs = [(k, 0, h) for k in range(2) for h in range(half_rows // CHUNK)]
    slope_chunks(jobs, scores, w, embed, bias_full, mask, word, before, emit)
    store_rows([row_out], slopes, w)
    for copy in (*e_copies[1], *e_copies[2], *e_copies[3]):
        copy.wait()


def label_kernel(embed, w, pos, mask, bias_full, one_slopes_t, word, slopes_t, label_out, scores):
    half_rows = label_out.shape[0]
    tiles = embed.shape[0] // TILE
    set_words(range(1, tiles), pos, word)

    def emit(k, t, c, part):
        slopes_t[c * CLUSTER : (c + 1) * CLUSTER, (t - 1) * TILE : t * TILE] = part
        if t == tiles - 1 and (c + 1) % (CHUNK // CLUSTER) == 0:
            rows = slice((c + 1) * CLUSTER - CHUNK, (c + 1) * CLUSTER)
            label_out[rows] = (
                jnp.dot(one_slopes_t[rows], embed[:TILE], preferred_element_type=F32)
                + jnp.dot(slopes_t[rows], embed[TILE:], preferred_element_type=F32)
            ).astype(BF16)

    jobs = [(0, t, h) for t in range(1, tiles) for h in range(half_rows // CHUNK)]
    slope_chunks(jobs, scores, w, embed, bias_full, mask, word, lambda *job: None, emit)


def store_rows(outs, slopes, w):
    sums = jnp.dot(slopes[...], w[...], preferred_element_type=F32).astype(BF16)
    count = TILE // len(outs)
    for i, out in enumerate(outs):
        out[...] = sums[i * count : (i + 1) * count].reshape(out.shape)


def row_tile(t, outs, embed, w, word, mask, bias_full, first_slopes_t, own_slopes_t, scores, slopes):
    half_rows = w.shape[0] // 2

    def emit(k, t, c, part):
        if c == 0:
            slopes[:, :half_rows] = first_slopes_t[:, (t - 1) * TILE : t * TILE].T
        own_slopes_t[c * CLUSTER : (c + 1) * CLUSTER] = part
        slopes[:, half_rows + c * CLUSTER : half_rows + (c + 1) * CLUSTER] = part.T

    jobs = [(1, t, h) for h in range(half_rows // CHUNK)]
    slope_chunks(jobs, scores, w, embed, bias_full, mask, word, lambda *job: None, emit)
    store_rows(outs, slopes, w)


def keep_rows_kernel(embed, w, word, mask, bias_full, first_slopes_t, own_slopes_t, row_out, scores, slopes):
    row_tile(1, [row_out], embed, w, word, mask, bias_full, first_slopes_t, own_slopes_t, scores, slopes)


def last_rows_kernel(embed, w, word, mask, bias_full, first_slopes_t, *rest):
    *outs, three_slopes_t, four_slopes_t, scores, slopes = rest
    shared = (embed, w, word, mask, bias_full, first_slopes_t)
    row_tile(2, outs[:-1], *shared, three_slopes_t, scores.at[0], slopes.at[0])
    row_tile(3, outs[-1:], *shared, four_slopes_t, scores.at[1], slopes.at[1])


def keep_kernel(embed, *refs):
    *slopes_t, label_out = refs
    total = 0.0
    for t, part in enumerate(slopes_t):
        total = total + jnp.dot(part[...], embed[t * TILE : (t + 1) * TILE], preferred_element_type=F32)
    label_out[...] = total.astype(BF16)


def sum_kernel(places, *refs):
    *terms, out = refs
    out[...] = add(*(term[at] for term, at in zip(terms, places)))


def half_sum_kernel(kept, got, out):
    out[...] = add(kept[: out.shape[0]], got[: out.shape[0]])


def finish_kernel(kept, got, summed, *refs):
    *row_terms, row_out, label_out, row, rest, sems = refs
    first = summed.shape[0]
    copies = [
        pltpu.make_async_copy(row, row_out, sems.at[0]),
        pltpu.make_async_copy(summed, label_out.at[pl.ds(0, first)], sems.at[1]),
        pltpu.make_async_copy(rest, label_out.at[pl.ds(first, rest.shape[0])], sems.at[2]),
    ]
    copies[1].start()
    row[...] = add(*(term[(0,) * (len(term.shape) - 2)] for term in row_terms))
    copies[0].start()
    rest[...] = add(kept[first:], got[first:])
    copies[2].start()
    for copy in copies:
        copy.wait()


def swapped(value, axis, size, bit):
    return lax.ppermute(value, axis, [(i, i ^ bit) for i in range(size)])


def add(*terms):
    total = terms[0].astype(F32)
    for term in terms[1:]:
        total = total + term.astype(F32)
    return total.astype(BF16)


def on_device(n_dp, n_label, embed, weight, bias, beam, positives):
    rows, features = embed.shape
    labels = weight.shape[0]
    half_rows = labels // 2
    clusters = half_rows // CLUSTER
    piece = rows // n_label
    subs = n_label // 2 // BLOCKS
    bias_rows = bias.reshape(labels // CLUSTER, CLUSTER)
    pos_rows = positives.T
    vmem = pl.BlockSpec(memory_space=pltpu.VMEM)
    hbm = pl.BlockSpec(memory_space=pltpu.HBM)
    params = pltpu.CompilerParams(vmem_limit_bytes=VMEM_LIMIT)
    shape = jax.ShapeDtypeStruct
    tile_shape = shape((half_rows, TILE), BF16)
    row_shape = shape((BLOCKS // 2, subs, piece, features), BF16)
    score_scratch = pltpu.VMEM((2, CHUNK, TILE), F32)
    slope_scratch = pltpu.VMEM((TILE, labels), BF16)

    def cost(halves):
        return pl.CostEstimate(flops=halves * 2 * rows * half_rows * features, bytes_accessed=0, transcendentals=0)

    *common, head_slopes_t, one_slopes_t, first_send = pl.pallas_call(
        functools.partial(first_kernel, n_label),
        out_shape=[
            shape((rows, features), BF16),
            shape((labels, features), BF16),
            shape(pos_rows.shape, jnp.int32),
            shape((2, clusters, BLOCKS, INST_BLOCK), BF16),
            shape((2, clusters, CLUSTER, INST_BLOCK), F32),
            tile_shape,
            tile_shape,
            row_shape,
        ],
        in_specs=[hbm] * 5,
        out_specs=[vmem] * 8,
        scratch_shapes=[
            pltpu.VMEM(bias_rows.shape, BF16),
            pltpu.VMEM(beam.shape, jnp.int32),
            pltpu.VMEM(pos_rows.shape, jnp.int32),
            pltpu.VMEM((2 * BLOCKS, beam.shape[1]), jnp.int32),
            pltpu.VMEM((CLUSTER, TILE), jnp.int16),
            score_scratch,
            slope_scratch,
            pltpu.SemaphoreType.DMA((5 + n_label,)),
        ],
        compiler_params=params,
        cost_estimate=cost(2),
        name="first_rows",
    )(*(pltpu.with_memory_space_constraint(x, pltpu.HBM) for x in (embed, weight, bias_rows, beam, pos_rows)))

    first_got = swapped(first_send, "label", n_label, 1)

    word, first_slopes_t, label_send = pl.pallas_call(
        label_kernel,
        out_shape=[
            shape((CLUSTER, rows), jnp.int16),
            shape((half_rows, rows - TILE), BF16),
            shape((half_rows, features), BF16),
        ],
        in_specs=[vmem] * 6,
        out_specs=[vmem] * 3,
        scratch_shapes=[score_scratch],
        compiler_params=params,
        cost_estimate=cost(0),
        name="send_half",
    )(*common, head_slopes_t)
    embed_own, w, _, mask, bias_full = common
    shared = (embed_own, w, word, mask, bias_full, first_slopes_t)

    label_got = swapped(label_send, "dp", n_dp, n_dp // 2)
    first_got, *shared = lax.optimization_barrier((first_got, *shared))

    two_slopes_t, first_keep = pl.pallas_call(
        keep_rows_kernel,
        out_shape=[tile_shape, row_shape],
        in_specs=[vmem] * 6,
        out_specs=[vmem] * 2,
        scratch_shapes=[score_scratch, slope_scratch],
        compiler_params=params,
        cost_estimate=cost(0),
        name="keep_rows",
    )(*shared)

    axes = [2 * subs, 4 * subs, 8 * subs]

    def summed_at(*terms):
        arrays, places = zip(*terms)
        size = places[0].stop - places[0].start
        return pl.pallas_call(
            functools.partial(sum_kernel, places),
            out_shape=shape((size, subs, piece, features), BF16),
            in_specs=[vmem] * len(arrays),
            out_specs=vmem,
            compiler_params=params,
            cost_estimate=cost(0),
            name="row_sum",
        )(*arrays)

    def passed_on(value, stage):
        bits = (axes[stage], axes[(stage + 1) % 3])
        return lax.ppermute(value, "label", [(i, i ^ bits[i % 2]) for i in range(n_label)])

    first_got = passed_on(summed_at((first_keep, slice(0, 4)), (first_got, slice(0, 4))), 0)

    part_shape = shape((2, subs, piece, features), BF16)
    *last_send, last_keep, three_slopes_t, four_slopes_t = pl.pallas_call(
        last_rows_kernel,
        out_shape=[part_shape] * 2 + [row_shape, tile_shape, tile_shape],
        in_specs=[vmem] * 6,
        out_specs=[vmem] * 5,
        scratch_shapes=[
            pltpu.VMEM((2, 2, CHUNK, TILE), F32),
            pltpu.VMEM((2, TILE, labels), BF16),
        ],
        compiler_params=params,
        cost_estimate=cost(2),
        name="last_rows",
    )(*shared)

    last_got = [swapped(part, "label", n_label, 1) for part in last_send]
    three_got = passed_on(summed_at((last_keep, slice(3, 4)), (last_got[1], slice(1, 2)), (first_got, slice(3, 4))), 1)
    two_got = passed_on(summed_at((last_keep, slice(2, 3)), (last_got[1], slice(0, 1)), (first_got, slice(2, 3))), 1)
    row_got = passed_on(summed_at((last_keep, slice(1, 2)), (last_got[0], slice(1, 2)), (first_got, slice(1, 2)), (three_got, slice(0, 1))), 2)
    row_terms = [last_keep, last_got[0], first_got, two_got, row_got]
    bit = subs
    while bit > 1:
        row_sum = add(*(term.reshape(-1, subs, piece, features)[0] for term in row_terms[:-1]))
        held = row_sum.shape[0] // 2
        came = row_terms[-1].reshape(subs, piece, features)
        incoming = swapped(add(row_sum[held:], came[held:]), "label", n_label, bit)
        row_terms = [add(row_sum[:held], came[:held]), incoming]
        subs = held
        bit //= 2

    label_keep = pl.pallas_call(
        keep_kernel,
        out_shape=shape((half_rows, features), BF16),
        in_specs=[vmem] * 5,
        out_specs=vmem,
        compiler_params=params,
        cost_estimate=cost(0),
        name="keep_half",
    )(embed_own, one_slopes_t, two_slopes_t, three_slopes_t, four_slopes_t)

    kept, got = label_keep, label_got
    step = n_dp // 4
    at = lax.axis_index("dp")
    while step >= 1:
        label_sum = add(kept, got)
        size = label_sum.shape[0] // 2
        mine = (at // step) % 2
        outgoing = lax.dynamic_slice_in_dim(label_sum, (1 - mine) * size, size, 0)
        kept = lax.dynamic_slice_in_dim(label_sum, mine * size, size, 0)
        got = swapped(outgoing, "dp", n_dp, step)
        step //= 2

    size = kept.shape[0]
    summed = pl.pallas_call(
        half_sum_kernel,
        out_shape=shape((size // 2, features), BF16),
        in_specs=[vmem] * 2,
        out_specs=vmem,
        compiler_params=params,
        cost_estimate=cost(2),
        name="half_sum",
    )(kept, got)
    return pl.pallas_call(
        finish_kernel,
        out_shape=[shape((piece, features), BF16), shape((size, features), BF16)],
        in_specs=[vmem] * (3 + len(row_terms)),
        out_specs=[hbm] * 2,
        scratch_shapes=[
            pltpu.VMEM((piece, features), BF16),
            pltpu.VMEM((size // 2, features), BF16),
            pltpu.SemaphoreType.DMA((3,)),
        ],
        compiler_params=params,
        cost_estimate=cost(0),
        name="finish",
    )(kept, got, summed, *row_terms)


def solution(mesh):
    in_specs = (P("dp", None), P("label", None), P("label"), P("dp", None), P("dp", None))
    out_specs = (P(("dp", "label"), None), P(("label", "dp"), None))
    body = functools.partial(on_device, mesh.shape["dp"], mesh.shape["label"])
    return jax.shard_map(body, mesh=mesh, in_specs=in_specs, out_specs=out_specs, check_vma=False)
```

```python
import functools

import jax
import jax.numpy as jnp
from jax import lax
from jax.experimental import pallas as pl
from jax.experimental.pallas import tpu as pltpu
from jax.sharding import PartitionSpec as P

INST_BLOCK = 128
CLUSTER = 128
TILE = 256
CHUNK = 256
CLUSTERS = 8
BLOCKS = 8
SCALE = 0.125

F32 = jnp.float32
BF16 = jnp.bfloat16
VMEM_LIMIT = 32 * 1024 * 1024


def half_index():
    return lax.axis_index("dp") // (lax.axis_size("dp") // 2)


def place(n_label):
    subs = n_label // 2 // BLOCKS
    pair = lax.axis_index("label") // 2
    return pair // subs, pair % subs, lax.axis_index("label") % 2


def slope_chunks(jobs, scores, w, embed, bias_ref, mask_ref, word_ref, before, emit):
    half_rows = w.shape[0] // 2
    clusters = half_rows // CLUSTER

    def score(n):
        k, t, h = jobs[n]
        before(k, t, h)
        first = k * half_rows + h * CHUNK
        scores[n % 2] = lax.dot_general(
            w[first : first + CHUNK],
            embed[t * TILE : (t + 1) * TILE],
            (((1,), (1,)), ((), ())),
            preferred_element_type=F32,
        )

    score(0)
    for n, (k, t, h) in enumerate(jobs):
        if n + 1 < len(jobs):
            score(n + 1)
        for i in range(CHUNK // CLUSTER):
            c = h * (CHUNK // CLUSTER) + i
            hit = (word_ref[:, t * TILE : (t + 1) * TILE] & jnp.int16(1 << (k * clusters + c))) != 0
            sign = jnp.where(hit, jnp.bfloat16(-1), jnp.bfloat16(1)).astype(F32)
            groups = []
            for g in range(TILE // INST_BLOCK):
                lanes = slice(g * INST_BLOCK, (g + 1) * INST_BLOCK)
                z = scores[n % 2, i * CLUSTER : (i + 1) * CLUSTER, lanes] * 0.5 + bias_ref[k, c]
                group = t * (TILE // INST_BLOCK) + g
                groups.append((jnp.tanh(z) + sign[:, lanes]).astype(BF16) * mask_ref[k, c, group : group + 1])
            emit(k, t, c, jnp.concatenate(groups, axis=1))


def block_in(t, i, over, core):
    first, second, third = 1 - t // 2, i // 2, i % 2
    owner = core if t % 2 else 1 - core
    return (first + 2 * second + 4 * third + owner * (first + 2 * second - 3 * third)) ^ over


def set_words(tiles, pos_ref, word):
    half_rows = CLUSTER * CLUSTERS // 2
    first_label = lax.axis_index("label") * 2 * half_rows
    send_half = 1 - half_index()
    label_no = lax.broadcasted_iota(jnp.int32, (CLUSTER, TILE), 0).astype(jnp.int16)
    for t in tiles:
        lanes = slice(t * TILE, (t + 1) * TILE)
        local = pos_ref[:, lanes] - first_label
        inside = (local >= 0) & (local < 2 * half_rows)
        bits = jnp.where(inside, jnp.left_shift(1, ((local >> 7) ^ (send_half * (CLUSTERS // 2))) & 15), 0).astype(jnp.int16)
        at = (local & (CLUSTER - 1)).astype(jnp.int16)
        found = jnp.zeros((CLUSTER, TILE), jnp.int16)
        for p in range(pos_ref.shape[0]):
            found = found | jnp.where(
                label_no == jnp.broadcast_to(at[p : p + 1], found.shape),
                jnp.broadcast_to(bits[p : p + 1], found.shape),
                jnp.int16(0),
            )
        word[:, lanes] = found


def first_kernel(n_label, embed_hbm, weight_hbm, bias_hbm, beam_hbm, pos_hbm, embed, w, pos, mask, bias_full,
                 first_slopes_t, own_slopes_t, row_out, bias_raw, beam_raw, pos_raw, beam, word, scores, slopes, sems):
    half_rows = own_slopes_t.shape[0]
    clusters = half_rows // CLUSTER
    tiles = embed.shape[0] // TILE
    half = 1 - half_index()
    over, within, core = place(n_label)
    piece = embed.shape[0] // n_label
    subs = INST_BLOCK // piece // 2
    small = [
        pltpu.make_async_copy(source, target, sems.at[k])
        for k, (source, target) in enumerate(((beam_hbm, beam_raw), (bias_hbm, bias_raw), (pos_hbm, pos_raw)))
    ]
    w_copies = [
        pltpu.make_async_copy(
            weight_hbm.at[pl.ds(pl.multiple_of(which * half_rows, half_rows), half_rows)],
            w.at[pl.ds(k * half_rows, half_rows)],
            sems.at[3 + k],
        )
        for k, which in enumerate((half, 1 - half))
    ]
    e_copies = []
    for t in range(tiles):
        e_copies.append([])
        for i in range(4):
            for j in range(subs):
                at = t * (TILE // piece) + len(e_copies[t])
                row = block_in(t, i, over, core) * INST_BLOCK
                row = row + (2 * (j ^ within if subs > 1 else 0) + (core if t % 2 else 1 - core)) * piece
                e_copies[t].append(
                    pltpu.make_async_copy(
                        embed_hbm.at[pl.ds(pl.multiple_of(row, piece), piece)],
                        embed.at[pl.ds(at * piece, piece)],
                        sems.at[5 + at],
                    )
                )
    for copy in (*small, *e_copies[0], *w_copies, *e_copies[1], *e_copies[2], *e_copies[3]):
        copy.start()
    for copy in small:
        copy.wait()

    lane = lax.broadcasted_iota(jnp.int32, (BLOCKS, INST_BLOCK), 1)
    low = lane < INST_BLOCK // 2

    def relative_lanes(x):
        code = 2 * within + core
        for k in range((2 * subs).bit_length() - 1):
            shift = piece << k
            turned = jnp.where(
                (lane & shift) != 0, pltpu.roll(x, shift, 1), pltpu.roll(x, INST_BLOCK - shift, 1)
            )
            x = jnp.where((code >> k) % 2 == 1, turned, x)
        if subs > 1:
            x = jnp.concatenate(
                [x[:, (2 * j + c) * piece : (2 * j + c + 1) * piece] for c in range(2) for j in range(subs)], axis=1
            )
        return x

    def set_positives(t):
        for g in range(TILE // INST_BLOCK):
            one, two = (
                relative_lanes(
                    pos_raw[:, pl.ds(pl.multiple_of(block_in(t, 2 * g + h, over, core) * INST_BLOCK, INST_BLOCK), INST_BLOCK)]
                )
                for h in range(2)
            )
            group = t * (TILE // INST_BLOCK) + g
            pos[:, group * INST_BLOCK : (group + 1) * INST_BLOCK] = (
                jnp.where(low, one, pltpu.roll(two, INST_BLOCK // 2, 1))
                if t % 2
                else jnp.where(low, pltpu.roll(one, INST_BLOCK // 2, 1), two)
            )

    for t in range(tiles):
        for i in range(4):
            group = 8 * (i % 2) + t * 2 + i // 2
            beam[group : group + 1] = beam_raw[pl.ds(block_in(t, i, over, core), 1)]
    for t in range(tiles):
        set_positives(t)
    set_words([0], pos, word)

    row = lax.broadcasted_iota(jnp.int32, (2 * clusters, 2 * clusters * INST_BLOCK), 0)
    column = lax.broadcasted_iota(jnp.int32, (2 * clusters, 2 * clusters * INST_BLOCK), 1)
    spread = jnp.where(row == (column // INST_BLOCK) ^ (half * clusters), 0.5, 0.0).astype(BF16)
    biases = lax.dot_general(bias_raw[...], spread, (((0,), (0,)), ((), ())), preferred_element_type=F32)
    first_cluster = lax.axis_index("label") * 2 * clusters
    for k in range(2):
        for c in range(clusters):
            i = k * clusters + c
            bias_full[k, c] = biases[:, i * INST_BLOCK : (i + 1) * INST_BLOCK]
            held = jnp.where(beam[...] == first_cluster + (i ^ (half * clusters)), 0.5 * SCALE, 0.0)
            held = jnp.broadcast_to(jnp.max(held, axis=1, keepdims=True), (2 * BLOCKS, INST_BLOCK))
            mask[k, c] = jnp.where(low, held[:BLOCKS], held[BLOCKS:]).astype(BF16)
    for copy in (w_copies[0], *e_copies[0]):
        copy.wait()

    def before(k, t, h):
        if (k, h) == (1, 0):
            w_copies[1].wait()

    def emit(k, t, c, part):
        out = own_slopes_t if k else first_slopes_t
        out[c * CLUSTER : (c + 1) * CLUSTER] = part
        slopes[:, (k * clusters + c) * CLUSTER : (k * clusters + c + 1) * CLUSTER] = part.T

    jobs = [(k, 0, h) for k in range(2) for h in range(half_rows // CHUNK)]
    slope_chunks(jobs, scores, w, embed, bias_full, mask, word, before, emit)
    store_rows([row_out], slopes, w)
    for copy in (*e_copies[1], *e_copies[2], *e_copies[3]):
        copy.wait()


def label_kernel(embed, w, pos, mask, bias_full, one_slopes_t, word, slopes_t, label_out, scores):
    half_rows = label_out.shape[0]
    tiles = embed.shape[0] // TILE
    set_words(range(1, tiles), pos, word)

    def emit(k, t, c, part):
        slopes_t[c * CLUSTER : (c + 1) * CLUSTER, (t - 1) * TILE : t * TILE] = part

    jobs = [(0, t, h) for t in range(1, tiles) for h in range(half_rows // CHUNK)]
    slope_chunks(jobs, scores, w, embed, bias_full, mask, word, lambda *job: None, emit)
    label_out[...] = (
        jnp.dot(one_slopes_t[...], embed[:TILE], preferred_element_type=F32)
        + jnp.dot(slopes_t[...], embed[TILE:], preferred_element_type=F32)
    ).astype(BF16)


def store_rows(outs, slopes, w):
    sums = jnp.dot(slopes[...], w[...], preferred_element_type=F32).astype(BF16)
    count = TILE // len(outs)
    for i, out in enumerate(outs):
        out[...] = sums[i * count : (i + 1) * count].reshape(out.shape)


def row_tile(t, outs, embed, w, word, mask, bias_full, first_slopes_t, own_slopes_t, scores, slopes):
    half_rows = w.shape[0] // 2

    def emit(k, t, c, part):
        if c == 0:
            slopes[:, :half_rows] = first_slopes_t[:, (t - 1) * TILE : t * TILE].T
        own_slopes_t[c * CLUSTER : (c + 1) * CLUSTER] = part
        slopes[:, half_rows + c * CLUSTER : half_rows + (c + 1) * CLUSTER] = part.T

    jobs = [(1, t, h) for h in range(half_rows // CHUNK)]
    slope_chunks(jobs, scores, w, embed, bias_full, mask, word, lambda *job: None, emit)
    store_rows(outs, slopes, w)


def keep_rows_kernel(embed, w, word, mask, bias_full, first_slopes_t, own_slopes_t, row_out, scores, slopes):
    row_tile(1, [row_out], embed, w, word, mask, bias_full, first_slopes_t, own_slopes_t, scores, slopes)


def last_rows_kernel(embed, w, word, mask, bias_full, first_slopes_t, *rest):
    *outs, three_slopes_t, four_slopes_t, scores, slopes = rest
    shared = (embed, w, word, mask, bias_full, first_slopes_t)
    row_tile(2, outs[:-1], *shared, three_slopes_t, scores.at[0], slopes.at[0])
    row_tile(3, outs[-1:], *shared, four_slopes_t, scores.at[1], slopes.at[1])


def keep_kernel(embed, *refs):
    *slopes_t, label_out = refs
    total = 0.0
    for t, part in enumerate(slopes_t):
        total = total + jnp.dot(part[...], embed[t * TILE : (t + 1) * TILE], preferred_element_type=F32)
    label_out[...] = total.astype(BF16)


def sum_kernel(places, *refs):
    *terms, out = refs
    out[...] = add(*(term[at] for term, at in zip(terms, places)))


def half_sum_kernel(kept, got, out):
    out[...] = add(kept[: out.shape[0]], got[: out.shape[0]])


def finish_kernel(kept, got, summed, *refs):
    *row_terms, row_out, label_out, row, rest, sems = refs
    first = summed.shape[0]
    copies = [
        pltpu.make_async_copy(row, row_out, sems.at[0]),
        pltpu.make_async_copy(summed, label_out.at[pl.ds(0, first)], sems.at[1]),
        pltpu.make_async_copy(rest, label_out.at[pl.ds(first, rest.shape[0])], sems.at[2]),
    ]
    copies[1].start()
    row[...] = add(*(term[(0,) * (len(term.shape) - 2)] for term in row_terms))
    copies[0].start()
    rest[...] = add(kept[first:], got[first:])
    copies[2].start()
    for copy in copies:
        copy.wait()


def swapped(value, axis, size, bit):
    return lax.ppermute(value, axis, [(i, i ^ bit) for i in range(size)])


def add(*terms):
    total = terms[0].astype(F32)
    for term in terms[1:]:
        total = total + term.astype(F32)
    return total.astype(BF16)


def on_device(n_dp, n_label, embed, weight, bias, beam, positives):
    rows, features = embed.shape
    labels = weight.shape[0]
    half_rows = labels // 2
    clusters = half_rows // CLUSTER
    piece = rows // n_label
    subs = n_label // 2 // BLOCKS
    bias_rows = bias.reshape(labels // CLUSTER, CLUSTER)
    pos_rows = positives.T
    vmem = pl.BlockSpec(memory_space=pltpu.VMEM)
    hbm = pl.BlockSpec(memory_space=pltpu.HBM)
    params = pltpu.CompilerParams(vmem_limit_bytes=VMEM_LIMIT)
    shape = jax.ShapeDtypeStruct
    tile_shape = shape((half_rows, TILE), BF16)
    row_shape = shape((BLOCKS // 2, subs, piece, features), BF16)
    score_scratch = pltpu.VMEM((2, CHUNK, TILE), F32)
    slope_scratch = pltpu.VMEM((TILE, labels), BF16)

    def cost(halves):
        return pl.CostEstimate(flops=halves * 2 * rows * half_rows * features, bytes_accessed=0, transcendentals=0)

    *common, head_slopes_t, one_slopes_t, first_send = pl.pallas_call(
        functools.partial(first_kernel, n_label),
        out_shape=[
            shape((rows, features), BF16),
            shape((labels, features), BF16),
            shape(pos_rows.shape, jnp.int32),
            shape((2, clusters, BLOCKS, INST_BLOCK), BF16),
            shape((2, clusters, CLUSTER, INST_BLOCK), F32),
            tile_shape,
            tile_shape,
            row_shape,
        ],
        in_specs=[hbm] * 5,
        out_specs=[vmem] * 8,
        scratch_shapes=[
            pltpu.VMEM(bias_rows.shape, BF16),
            pltpu.VMEM(beam.shape, jnp.int32),
            pltpu.VMEM(pos_rows.shape, jnp.int32),
            pltpu.VMEM((2 * BLOCKS, beam.shape[1]), jnp.int32),
            pltpu.VMEM((CLUSTER, TILE), jnp.int16),
            score_scratch,
            slope_scratch,
            pltpu.SemaphoreType.DMA((5 + n_label,)),
        ],
        compiler_params=params,
        cost_estimate=cost(2),
        name="first_rows",
    )(*(pltpu.with_memory_space_constraint(x, pltpu.HBM) for x in (embed, weight, bias_rows, beam, pos_rows)))

    first_got = swapped(first_send, "label", n_label, 1)

    word, first_slopes_t, label_send = pl.pallas_call(
        label_kernel,
        out_shape=[
            shape((CLUSTER, rows), jnp.int16),
            shape((half_rows, rows - TILE), BF16),
            shape((half_rows, features), BF16),
        ],
        in_specs=[vmem] * 6,
        out_specs=[vmem] * 3,
        scratch_shapes=[score_scratch],
        compiler_params=params,
        cost_estimate=cost(0),
        name="send_half",
    )(*common, head_slopes_t)
    embed_own, w, _, mask, bias_full = common
    shared = (embed_own, w, word, mask, bias_full, first_slopes_t)

    label_got = swapped(label_send, "dp", n_dp, n_dp // 2)
    first_got, *shared = lax.optimization_barrier((first_got, *shared))

    two_slopes_t, first_keep = pl.pallas_call(
        keep_rows_kernel,
        out_shape=[tile_shape, row_shape],
        in_specs=[vmem] * 6,
        out_specs=[vmem] * 2,
        scratch_shapes=[score_scratch, slope_scratch],
        compiler_params=params,
        cost_estimate=cost(0),
        name="keep_rows",
    )(*shared)

    axes = [2 * subs, 4 * subs, 8 * subs]

    def summed_at(*terms):
        arrays, places = zip(*terms)
        size = places[0].stop - places[0].start
        return pl.pallas_call(
            functools.partial(sum_kernel, places),
            out_shape=shape((size, subs, piece, features), BF16),
            in_specs=[vmem] * len(arrays),
            out_specs=vmem,
            compiler_params=params,
            cost_estimate=cost(0),
            name="row_sum",
        )(*arrays)

    def passed_on(value, stage):
        bits = (axes[stage], axes[(stage + 1) % 3])
        return lax.ppermute(value, "label", [(i, i ^ bits[i % 2]) for i in range(n_label)])

    far_got = passed_on(summed_at((first_keep, slice(2, 4)), (first_got, slice(2, 4))), 0)
    near_got = passed_on(summed_at((first_keep, slice(0, 2)), (first_got, slice(0, 2))), 0)

    part_shape = shape((2, subs, piece, features), BF16)
    *last_send, last_keep, three_slopes_t, four_slopes_t = pl.pallas_call(
        last_rows_kernel,
        out_shape=[part_shape] * 2 + [row_shape, tile_shape, tile_shape],
        in_specs=[vmem] * 6,
        out_specs=[vmem] * 5,
        scratch_shapes=[
            pltpu.VMEM((2, 2, CHUNK, TILE), F32),
            pltpu.VMEM((2, TILE, labels), BF16),
        ],
        compiler_params=params,
        cost_estimate=cost(2),
        name="last_rows",
    )(*shared)

    last_got = [swapped(part, "label", n_label, 1) for part in last_send]
    three_got = passed_on(summed_at((last_keep, slice(3, 4)), (last_got[1], slice(1, 2)), (far_got, slice(1, 2))), 1)
    two_got = passed_on(summed_at((last_keep, slice(2, 3)), (last_got[1], slice(0, 1)), (far_got, slice(0, 1))), 1)
    row_got = passed_on(summed_at((last_keep, slice(1, 2)), (last_got[0], slice(1, 2)), (near_got, slice(1, 2)), (three_got, slice(0, 1))), 2)
    row_terms = [last_keep, last_got[0], near_got, two_got, row_got]
    bit = subs
    while bit > 1:
        row_sum = add(*(term.reshape(-1, subs, piece, features)[0] for term in row_terms[:-1]))
        held = row_sum.shape[0] // 2
        came = row_terms[-1].reshape(subs, piece, features)
        incoming = swapped(add(row_sum[held:], came[held:]), "label", n_label, bit)
        row_terms = [add(row_sum[:held], came[:held]), incoming]
        subs = held
        bit //= 2

    label_keep = pl.pallas_call(
        keep_kernel,
        out_shape=shape((half_rows, features), BF16),
        in_specs=[vmem] * 5,
        out_specs=vmem,
        compiler_params=params,
        cost_estimate=cost(0),
        name="keep_half",
    )(embed_own, one_slopes_t, two_slopes_t, three_slopes_t, four_slopes_t)

    kept, got = label_keep, label_got
    step = n_dp // 4
    at = lax.axis_index("dp")
    while step >= 1:
        label_sum = add(kept, got)
        size = label_sum.shape[0] // 2
        mine = (at // step) % 2
        outgoing = lax.dynamic_slice_in_dim(label_sum, (1 - mine) * size, size, 0)
        kept = lax.dynamic_slice_in_dim(label_sum, mine * size, size, 0)
        got = swapped(outgoing, "dp", n_dp, step)
        step //= 2

    size = kept.shape[0]
    summed = pl.pallas_call(
        half_sum_kernel,
        out_shape=shape((size // 2, features), BF16),
        in_specs=[vmem] * 2,
        out_specs=vmem,
        compiler_params=params,
        cost_estimate=cost(2),
        name="half_sum",
    )(kept, got)
    return pl.pallas_call(
        finish_kernel,
        out_shape=[shape((piece, features), BF16), shape((size, features), BF16)],
        in_specs=[vmem] * (3 + len(row_terms)),
        out_specs=[hbm] * 2,
        scratch_shapes=[
            pltpu.VMEM((piece, features), BF16),
            pltpu.VMEM((size // 2, features), BF16),
            pltpu.SemaphoreType.DMA((3,)),
        ],
        compiler_params=params,
        cost_estimate=cost(0),
        name="finish",
    )(kept, got, summed, *row_terms)


def solution(mesh):
    in_specs = (P("dp", None), P("label", None), P("label"), P("dp", None), P("dp", None))
    out_specs = (P(("dp", "label"), None), P(("label", "dp"), None))
    body = functools.partial(on_device, mesh.shape["dp"], mesh.shape["label"])
    return jax.shard_map(body, mesh=mesh, in_specs=in_specs, out_specs=out_specs, check_vma=False)
```

```python
import functools

import jax
import jax.numpy as jnp
from jax import lax
from jax.experimental import pallas as pl
from jax.experimental.pallas import tpu as pltpu
from jax.sharding import PartitionSpec as P

INST_BLOCK = 128
CLUSTER = 128
TILE = 256
CHUNK = 256
CLUSTERS = 8
BLOCKS = 8
SCALE = 0.125

F32 = jnp.float32
BF16 = jnp.bfloat16
VMEM_LIMIT = 32 * 1024 * 1024


def half_index():
    return lax.axis_index("dp") // (lax.axis_size("dp") // 2)


def place(n_label):
    subs = n_label // 2 // BLOCKS
    pair = lax.axis_index("label") // 2
    return pair // subs, pair % subs, lax.axis_index("label") % 2


def slope_chunks(jobs, scores, w, embed, bias_ref, mask_ref, word_ref, before, emit):
    half_rows = w.shape[0] // 2
    clusters = half_rows // CLUSTER

    def score(n):
        k, t, h = jobs[n]
        before(k, t, h)
        first = k * half_rows + h * CHUNK
        scores[n % 2] = lax.dot_general(
            w[first : first + CHUNK],
            embed[t * TILE : (t + 1) * TILE],
            (((1,), (1,)), ((), ())),
            preferred_element_type=F32,
        )

    score(0)
    for n, (k, t, h) in enumerate(jobs):
        if n + 1 < len(jobs):
            score(n + 1)
        for i in range(CHUNK // CLUSTER):
            c = h * (CHUNK // CLUSTER) + i
            hit = (word_ref[:, t * TILE : (t + 1) * TILE] & jnp.int16(1 << (k * clusters + c))) != 0
            sign = jnp.where(hit, jnp.bfloat16(-1), jnp.bfloat16(1)).astype(F32)
            groups = []
            for g in range(TILE // INST_BLOCK):
                lanes = slice(g * INST_BLOCK, (g + 1) * INST_BLOCK)
                z = scores[n % 2, i * CLUSTER : (i + 1) * CLUSTER, lanes] * 0.5 + bias_ref[k, c]
                group = t * (TILE // INST_BLOCK) + g
                groups.append((jnp.tanh(z) + sign[:, lanes]).astype(BF16) * mask_ref[k, c, group : group + 1])
            emit(k, t, c, jnp.concatenate(groups, axis=1))


def block_in(t, i, over, core):
    first, second, third = 1 - t // 2, i // 2, i % 2
    owner = core if t % 2 else 1 - core
    return (first + 2 * second + 4 * third + owner * (first + 2 * second - 3 * third)) ^ over


def set_words(tiles, pos_ref, word):
    half_rows = CLUSTER * CLUSTERS // 2
    first_label = lax.axis_index("label") * 2 * half_rows
    send_half = 1 - half_index()
    label_no = lax.broadcasted_iota(jnp.int32, (CLUSTER, TILE), 0).astype(jnp.int16)
    for t in tiles:
        lanes = slice(t * TILE, (t + 1) * TILE)
        local = pos_ref[:, lanes] - first_label
        inside = (local >= 0) & (local < 2 * half_rows)
        bits = jnp.where(inside, jnp.left_shift(1, ((local >> 7) ^ (send_half * (CLUSTERS // 2))) & 15), 0).astype(jnp.int16)
        at = (local & (CLUSTER - 1)).astype(jnp.int16)
        found = jnp.zeros((CLUSTER, TILE), jnp.int16)
        for p in range(pos_ref.shape[0]):
            found = found | jnp.where(
                label_no == jnp.broadcast_to(at[p : p + 1], found.shape),
                jnp.broadcast_to(bits[p : p + 1], found.shape),
                jnp.int16(0),
            )
        word[:, lanes] = found


def first_kernel(n_label, embed_hbm, weight_hbm, bias_hbm, beam_hbm, pos_hbm, embed, w, pos, mask, bias_full,
                 first_slopes_t, own_slopes_t, row_out, bias_raw, beam_raw, pos_raw, beam, word, scores, slopes, sems):
    half_rows = own_slopes_t.shape[0]
    clusters = half_rows // CLUSTER
    tiles = embed.shape[0] // TILE
    half = 1 - half_index()
    over, within, core = place(n_label)
    piece = embed.shape[0] // n_label
    subs = INST_BLOCK // piece // 2
    small = [
        pltpu.make_async_copy(source, target, sems.at[k])
        for k, (source, target) in enumerate(((beam_hbm, beam_raw), (bias_hbm, bias_raw), (pos_hbm, pos_raw)))
    ]
    w_copies = [
        pltpu.make_async_copy(
            weight_hbm.at[pl.ds(pl.multiple_of(which * half_rows, half_rows), half_rows)],
            w.at[pl.ds(k * half_rows, half_rows)],
            sems.at[3 + k],
        )
        for k, which in enumerate((half, 1 - half))
    ]
    e_copies = []
    for t in range(tiles):
        e_copies.append([])
        for i in range(4):
            for j in range(subs):
                at = t * (TILE // piece) + len(e_copies[t])
                row = block_in(t, i, over, core) * INST_BLOCK
                row = row + (2 * (j ^ within if subs > 1 else 0) + (core if t % 2 else 1 - core)) * piece
                e_copies[t].append(
                    pltpu.make_async_copy(
                        embed_hbm.at[pl.ds(pl.multiple_of(row, piece), piece)],
                        embed.at[pl.ds(at * piece, piece)],
                        sems.at[5 + at],
                    )
                )
    for copy in (*small, *e_copies[0], *w_copies, *e_copies[1], *e_copies[2], *e_copies[3]):
        copy.start()
    for copy in small:
        copy.wait()

    lane = lax.broadcasted_iota(jnp.int32, (BLOCKS, INST_BLOCK), 1)
    low = lane < INST_BLOCK // 2

    def relative_lanes(x):
        code = 2 * within + core
        for k in range((2 * subs).bit_length() - 1):
            shift = piece << k
            turned = jnp.where(
                (lane & shift) != 0, pltpu.roll(x, shift, 1), pltpu.roll(x, INST_BLOCK - shift, 1)
            )
            x = jnp.where((code >> k) % 2 == 1, turned, x)
        if subs > 1:
            x = jnp.concatenate(
                [x[:, (2 * j + c) * piece : (2 * j + c + 1) * piece] for c in range(2) for j in range(subs)], axis=1
            )
        return x

    def set_positives(t):
        for g in range(TILE // INST_BLOCK):
            one, two = (
                relative_lanes(
                    pos_raw[:, pl.ds(pl.multiple_of(block_in(t, 2 * g + h, over, core) * INST_BLOCK, INST_BLOCK), INST_BLOCK)]
                )
                for h in range(2)
            )
            group = t * (TILE // INST_BLOCK) + g
            pos[:, group * INST_BLOCK : (group + 1) * INST_BLOCK] = (
                jnp.where(low, one, pltpu.roll(two, INST_BLOCK // 2, 1))
                if t % 2
                else jnp.where(low, pltpu.roll(one, INST_BLOCK // 2, 1), two)
            )

    for t in range(tiles):
        for i in range(4):
            group = 8 * (i % 2) + t * 2 + i // 2
            beam[group : group + 1] = beam_raw[pl.ds(block_in(t, i, over, core), 1)]
    set_positives(0)
    set_words([0], pos, word)

    row = lax.broadcasted_iota(jnp.int32, (2 * clusters, 2 * clusters * INST_BLOCK), 0)
    column = lax.broadcasted_iota(jnp.int32, (2 * clusters, 2 * clusters * INST_BLOCK), 1)
    spread = jnp.where(row == (column // INST_BLOCK) ^ (half * clusters), 0.5, 0.0).astype(BF16)
    biases = lax.dot_general(bias_raw[...], spread, (((0,), (0,)), ((), ())), preferred_element_type=F32)
    first_cluster = lax.axis_index("label") * 2 * clusters
    for k in range(2):
        for c in range(clusters):
            i = k * clusters + c
            bias_full[k, c] = biases[:, i * INST_BLOCK : (i + 1) * INST_BLOCK]
            held = jnp.where(beam[...] == first_cluster + (i ^ (half * clusters)), 0.5 * SCALE, 0.0)
            held = jnp.broadcast_to(jnp.max(held, axis=1, keepdims=True), (2 * BLOCKS, INST_BLOCK))
            mask[k, c] = jnp.where(low, held[:BLOCKS], held[BLOCKS:]).astype(BF16)
    for copy in (w_copies[0], *e_copies[0]):
        copy.wait()

    def before(k, t, h):
        if (k, h) == (1, 0):
            w_copies[1].wait()

    def emit(k, t, c, part):
        out = own_slopes_t if k else first_slopes_t
        out[c * CLUSTER : (c + 1) * CLUSTER] = part
        slopes[:, (k * clusters + c) * CLUSTER : (k * clusters + c + 1) * CLUSTER] = part.T

    jobs = [(k, 0, h) for k in range(2) for h in range(half_rows // CHUNK)]
    slope_chunks(jobs, scores, w, embed, bias_full, mask, word, before, emit)
    for t in range(1, tiles):
        set_positives(t)
    store_rows([row_out], slopes, w)
    for copy in (*e_copies[1], *e_copies[2], *e_copies[3]):
        copy.wait()


def label_kernel(embed, w, pos, mask, bias_full, one_slopes_t, word, slopes_t, label_out, scores):
    half_rows = label_out.shape[0]
    tiles = embed.shape[0] // TILE
    set_words(range(1, tiles), pos, word)

    def emit(k, t, c, part):
        slopes_t[c * CLUSTER : (c + 1) * CLUSTER, (t - 1) * TILE : t * TILE] = part
        if t == tiles - 1 and (c + 1) % (CHUNK // CLUSTER) == 0:
            rows = slice((c + 1) * CLUSTER - CHUNK, (c + 1) * CLUSTER)
            label_out[rows] = (
                jnp.dot(one_slopes_t[rows], embed[:TILE], preferred_element_type=F32)
                + jnp.dot(slopes_t[rows], embed[TILE:], preferred_element_type=F32)
            ).astype(BF16)

    jobs = [(0, t, h) for t in range(1, tiles) for h in range(half_rows // CHUNK)]
    slope_chunks(jobs, scores, w, embed, bias_full, mask, word, lambda *job: None, emit)


def store_rows(outs, slopes, w):
    sums = jnp.dot(slopes[...], w[...], preferred_element_type=F32).astype(BF16)
    count = TILE // len(outs)
    for i, out in enumerate(outs):
        out[...] = sums[i * count : (i + 1) * count].reshape(out.shape)


def row_tile(t, outs, embed, w, word, mask, bias_full, first_slopes_t, own_slopes_t, scores, slopes):
    half_rows = w.shape[0] // 2

    def emit(k, t, c, part):
        if c == 0:
            slopes[:, :half_rows] = first_slopes_t[:, (t - 1) * TILE : t * TILE].T
        own_slopes_t[c * CLUSTER : (c + 1) * CLUSTER] = part
        slopes[:, half_rows + c * CLUSTER : half_rows + (c + 1) * CLUSTER] = part.T

    jobs = [(1, t, h) for h in range(half_rows // CHUNK)]
    slope_chunks(jobs, scores, w, embed, bias_full, mask, word, lambda *job: None, emit)
    store_rows(outs, slopes, w)


def keep_rows_kernel(embed, w, word, mask, bias_full, first_slopes_t, own_slopes_t, row_out, scores, slopes):
    row_tile(1, [row_out], embed, w, word, mask, bias_full, first_slopes_t, own_slopes_t, scores, slopes)


def last_rows_kernel(embed, w, word, mask, bias_full, first_slopes_t, *rest):
    *outs, three_slopes_t, four_slopes_t, scores, slopes = rest
    shared = (embed, w, word, mask, bias_full, first_slopes_t)
    row_tile(2, outs[:-1], *shared, three_slopes_t, scores.at[0], slopes.at[0])
    row_tile(3, outs[-1:], *shared, four_slopes_t, scores.at[1], slopes.at[1])


def keep_kernel(embed, *refs):
    *slopes_t, label_out = refs
    total = 0.0
    for t, part in enumerate(slopes_t):
        total = total + jnp.dot(part[...], embed[t * TILE : (t + 1) * TILE], preferred_element_type=F32)
    label_out[...] = total.astype(BF16)


def sum_kernel(places, *refs):
    *terms, out = refs
    out[...] = add(*(term[at] for term, at in zip(terms, places)))


def half_sum_kernel(kept, got, out):
    out[...] = add(kept[: out.shape[0]], got[: out.shape[0]])


def finish_kernel(kept, got, summed, *refs):
    *row_terms, row_out, label_out, row, rest, sems = refs
    first = summed.shape[0]
    copies = [
        pltpu.make_async_copy(row, row_out, sems.at[0]),
        pltpu.make_async_copy(summed, label_out.at[pl.ds(0, first)], sems.at[1]),
        pltpu.make_async_copy(rest, label_out.at[pl.ds(first, rest.shape[0])], sems.at[2]),
    ]
    copies[1].start()
    row[...] = add(*(term[(0,) * (len(term.shape) - 2)] for term in row_terms))
    copies[0].start()
    rest[...] = add(kept[first:], got[first:])
    copies[2].start()
    for copy in copies:
        copy.wait()


def swapped(value, axis, size, bit):
    return lax.ppermute(value, axis, [(i, i ^ bit) for i in range(size)])


def add(*terms):
    total = terms[0].astype(F32)
    for term in terms[1:]:
        total = total + term.astype(F32)
    return total.astype(BF16)


def on_device(n_dp, n_label, embed, weight, bias, beam, positives):
    rows, features = embed.shape
    labels = weight.shape[0]
    half_rows = labels // 2
    clusters = half_rows // CLUSTER
    piece = rows // n_label
    subs = n_label // 2 // BLOCKS
    bias_rows = bias.reshape(labels // CLUSTER, CLUSTER)
    pos_rows = positives.T
    vmem = pl.BlockSpec(memory_space=pltpu.VMEM)
    hbm = pl.BlockSpec(memory_space=pltpu.HBM)
    params = pltpu.CompilerParams(vmem_limit_bytes=VMEM_LIMIT)
    shape = jax.ShapeDtypeStruct
    tile_shape = shape((half_rows, TILE), BF16)
    row_shape = shape((BLOCKS // 2, subs, piece, features), BF16)
    score_scratch = pltpu.VMEM((2, CHUNK, TILE), F32)
    slope_scratch = pltpu.VMEM((TILE, labels), BF16)

    def cost(halves):
        return pl.CostEstimate(flops=halves * 2 * rows * half_rows * features, bytes_accessed=0, transcendentals=0)

    *common, head_slopes_t, one_slopes_t, first_send = pl.pallas_call(
        functools.partial(first_kernel, n_label),
        out_shape=[
            shape((rows, features), BF16),
            shape((labels, features), BF16),
            shape(pos_rows.shape, jnp.int32),
            shape((2, clusters, BLOCKS, INST_BLOCK), BF16),
            shape((2, clusters, CLUSTER, INST_BLOCK), F32),
            tile_shape,
            tile_shape,
            row_shape,
        ],
        in_specs=[hbm] * 5,
        out_specs=[vmem] * 8,
        scratch_shapes=[
            pltpu.VMEM(bias_rows.shape, BF16),
            pltpu.VMEM(beam.shape, jnp.int32),
            pltpu.VMEM(pos_rows.shape, jnp.int32),
            pltpu.VMEM((2 * BLOCKS, beam.shape[1]), jnp.int32),
            pltpu.VMEM((CLUSTER, TILE), jnp.int16),
            score_scratch,
            slope_scratch,
            pltpu.SemaphoreType.DMA((5 + n_label,)),
        ],
        compiler_params=params,
        cost_estimate=cost(2),
        name="first_rows",
    )(*(pltpu.with_memory_space_constraint(x, pltpu.HBM) for x in (embed, weight, bias_rows, beam, pos_rows)))

    first_got = swapped(first_send, "label", n_label, 1)

    word, first_slopes_t, label_send = pl.pallas_call(
        label_kernel,
        out_shape=[
            shape((CLUSTER, rows), jnp.int16),
            shape((half_rows, rows - TILE), BF16),
            shape((half_rows, features), BF16),
        ],
        in_specs=[vmem] * 6,
        out_specs=[vmem] * 3,
        scratch_shapes=[score_scratch],
        compiler_params=params,
        cost_estimate=cost(0),
        name="send_half",
    )(*common, head_slopes_t)
    embed_own, w, _, mask, bias_full = common
    shared = (embed_own, w, word, mask, bias_full, first_slopes_t)

    label_got = swapped(label_send, "dp", n_dp, n_dp // 2)
    first_got, *shared = lax.optimization_barrier((first_got, *shared))

    two_slopes_t, first_keep = pl.pallas_call(
        keep_rows_kernel,
        out_shape=[tile_shape, row_shape],
        in_specs=[vmem] * 6,
        out_specs=[vmem] * 2,
        scratch_shapes=[score_scratch, slope_scratch],
        compiler_params=params,
        cost_estimate=cost(0),
        name="keep_rows",
    )(*shared)

    axes = [2 * subs, 4 * subs, 8 * subs]

    def summed_at(*terms):
        arrays, places = zip(*terms)
        size = places[0].stop - places[0].start
        return pl.pallas_call(
            functools.partial(sum_kernel, places),
            out_shape=shape((size, subs, piece, features), BF16),
            in_specs=[vmem] * len(arrays),
            out_specs=vmem,
            compiler_params=params,
            cost_estimate=cost(0),
            name="row_sum",
        )(*arrays)

    def passed_on(value, stage):
        bits = (axes[stage], axes[(stage + 1) % 3])
        return lax.ppermute(value, "label", [(i, i ^ bits[i % 2]) for i in range(n_label)])

    far_got = passed_on(summed_at((first_keep, slice(2, 4)), (first_got, slice(2, 4))), 0)
    near_got = passed_on(summed_at((first_keep, slice(0, 2)), (first_got, slice(0, 2))), 0)

    part_shape = shape((2, subs, piece, features), BF16)
    *last_send, last_keep, three_slopes_t, four_slopes_t = pl.pallas_call(
        last_rows_kernel,
        out_shape=[part_shape] * 2 + [row_shape, tile_shape, tile_shape],
        in_specs=[vmem] * 6,
        out_specs=[vmem] * 5,
        scratch_shapes=[
            pltpu.VMEM((2, 2, CHUNK, TILE), F32),
            pltpu.VMEM((2, TILE, labels), BF16),
        ],
        compiler_params=params,
        cost_estimate=cost(2),
        name="last_rows",
    )(*shared)

    last_got = [swapped(part, "label", n_label, 1) for part in last_send]
    three_got = passed_on(summed_at((last_keep, slice(3, 4)), (last_got[1], slice(1, 2)), (far_got, slice(1, 2))), 1)
    two_got = passed_on(summed_at((last_keep, slice(2, 3)), (last_got[1], slice(0, 1)), (far_got, slice(0, 1))), 1)
    row_got = passed_on(summed_at((last_keep, slice(1, 2)), (last_got[0], slice(1, 2)), (near_got, slice(1, 2)), (three_got, slice(0, 1))), 2)
    row_terms = [last_keep, last_got[0], near_got, two_got, row_got]
    bit = subs
    while bit > 1:
        row_sum = add(*(term.reshape(-1, subs, piece, features)[0] for term in row_terms[:-1]))
        held = row_sum.shape[0] // 2
        came = row_terms[-1].reshape(subs, piece, features)
        incoming = swapped(add(row_sum[held:], came[held:]), "label", n_label, bit)
        row_terms = [add(row_sum[:held], came[:held]), incoming]
        subs = held
        bit //= 2

    label_keep = pl.pallas_call(
        keep_kernel,
        out_shape=shape((half_rows, features), BF16),
        in_specs=[vmem] * 5,
        out_specs=vmem,
        compiler_params=params,
        cost_estimate=cost(0),
        name="keep_half",
    )(embed_own, one_slopes_t, two_slopes_t, three_slopes_t, four_slopes_t)

    kept, got = label_keep, label_got
    step = n_dp // 4
    at = lax.axis_index("dp")
    while step >= 1:
        label_sum = add(kept, got)
        size = label_sum.shape[0] // 2
        mine = (at // step) % 2
        outgoing = lax.dynamic_slice_in_dim(label_sum, (1 - mine) * size, size, 0)
        kept = lax.dynamic_slice_in_dim(label_sum, mine * size, size, 0)
        got = swapped(outgoing, "dp", n_dp, step)
        step //= 2

    size = kept.shape[0]
    summed = pl.pallas_call(
        half_sum_kernel,
        out_shape=shape((size // 2, features), BF16),
        in_specs=[vmem] * 2,
        out_specs=vmem,
        compiler_params=params,
        cost_estimate=cost(2),
        name="half_sum",
    )(kept, got)
    return pl.pallas_call(
        finish_kernel,
        out_shape=[shape((piece, features), BF16), shape((size, features), BF16)],
        in_specs=[vmem] * (3 + len(row_terms)),
        out_specs=[hbm] * 2,
        scratch_shapes=[
            pltpu.VMEM((piece, features), BF16),
            pltpu.VMEM((size // 2, features), BF16),
            pltpu.SemaphoreType.DMA((3,)),
        ],
        compiler_params=params,
        cost_estimate=cost(0),
        name="finish",
    )(kept, got, summed, *row_terms)


def solution(mesh):
    in_specs = (P("dp", None), P("label", None), P("label"), P("dp", None), P("dp", None))
    out_specs = (P(("dp", "label"), None), P(("label", "dp"), None))
    body = functools.partial(on_device, mesh.shape["dp"], mesh.shape["label"])
    return jax.shard_map(body, mesh=mesh, in_specs=in_specs, out_specs=out_specs, check_vma=False)
```
